32 devices in a mesh: dp: 8 (over z, x), tm: 4 (over y, core).
Axes of the slice: x: 2, y: 2, z: 4, core: 2. Of those that a mesh axis runs over, the one named last changes fastest.
Arguments:
- frames: bfloat16 [8, 3072, 1024], P('dp', 'tm'), may hold values from -18 to 18
- lengths: int32 [8], P('dp'), may hold values from 1 to 3072, 14745 in all
- w_in: bfloat16 [1024, 2048], replicated, may hold values from -4 to 4
- w_dw: float32 [31, 1024], replicated, may hold values from -1 to 1
- bn_gain: float32 [1024], replicated, may hold values from 0.25 to 1.75
- bn_bias: float32 [1024], replicated, may hold values from -1 to 1
- w_out: bfloat16 [1024, 1024], replicated, may hold values from -0.1875 to 0.1875
- cotangent: bfloat16 [8, 3072, 1024], P('dp', 'tm'), may hold values from -6 to 6
Outputs:
- output: bfloat16 [8, 3072, 1024], P('dp', 'tm')
- grad_frames: bfloat16 [8, 3072, 1024], P('dp', 'tm')
- grad_w_in: float32 [1024, 2048], P(('dp', 'tm'))
- grad_w_out: float32 [1024, 1024], P(('dp', 'tm'))
- grad_kernel: float32 [31, 1024], replicated
- grad_gain: float32 [1024], replicated
- grad_bias: float32 [1024], replicated
The draws below stay inside these ranges and needn't reach their ends.
Inputs may be any that keep to these rules, and one draw needn't show every extreme that they name: Frame slots at or after a recording's length are padding; the lengths sum to 14745 and the longest is exactly 3072.
All inputs are finite; a program needn't handle non-finite values. No bound on the sum of `lengths` on one device may be relied on, other than what follows from the above.
Results may differ from the reference program's by a relative error of at most 0.015.
Values may be sent and summed in bfloat16 or wider, within the bound.
No kernel may reach another device: no remote copies, remote signals or barrier semaphores. Data moves between devices by JAX's collectives and lax.ppermute only.
A program may use at most 128 MiB of HBM per device.

```python
import math
import jax
import jax.numpy as jnp
import numpy as np
from jax import lax

C = 1024
K = 31
HALO = 15
RECS = 8
LEN = 3072


def draw_frames(key, part):
    base_key, frame_key, record_key = jax.random.split(jax.random.fold_in(key, 17), 3)
    values = jax.random.truncated_normal(base_key, -4.0, 4.0, (RECS, LEN, C), jnp.float32)
    frame_scale = jnp.exp(jax.random.uniform(frame_key, (RECS, LEN, 1), jnp.float32, math.log(0.3), math.log(3.0)))
    record_scale = jnp.exp(jax.random.uniform(record_key, (RECS, 1, 1), jnp.float32, math.log(0.5), math.log(1.5)))
    return (values * frame_scale * record_scale).astype(jnp.bfloat16)


def draw_w_in(key, part):
    base_key, column_key = jax.random.split(jax.random.fold_in(key, 29), 2)
    values = jax.random.truncated_normal(base_key, -4.0, 4.0, (C, 2 * C), jnp.float32)
    column_scale = jnp.exp(jax.random.uniform(column_key, (1, 2 * C), jnp.float32, -1.15, 1.15))
    return (values * column_scale / math.sqrt(C)).astype(jnp.bfloat16)


def levels(own_key, extent, pieces, smallest, largest):
    factor_of = 1.0
    for position, parts in pieces:
        steps = jax.random.uniform(jax.random.fold_in(jax.random.fold_in(own_key, 6), position), (parts,), jnp.float32, smallest / len(pieces), largest / len(pieces))
        factor_of = factor_of * jnp.repeat(jnp.exp(steps), extent[position] // parts).reshape((-1,) + (1,) * (len(extent) - 1 - position))
    return factor_of


def profile(count, total, most, slope):
    loads = [(1 << 20) // math.isqrt(standing ** slope) + 1 for standing in range(2, count + 1)]
    rest, counts = total - most - (count - 1), [1] * (count - 1)
    while rest > 0:
        movable = [i for i in range(count - 1) if counts[i] < most]
        mass, budget = sum([loads[i] for i in movable]), rest
        for i in movable:
            addition = min(most - counts[i], max(1, budget * loads[i] // mass), rest)
            counts[i] = counts[i] + addition
            rest = rest - addition
    return np.array([most] + counts)


def uneven_parts(key, amount, total, most, lean):
    if amount == 2:
        one = jax.random.randint(key, (), max(1, total - most), min(most, total - 1) + 1)
        return jnp.stack([one, total - one])
    sizes = jnp.asarray(profile(amount, total, most, lean), jnp.int32)
    twos = (amount - 1) // 2
    giver, sink = sizes[1:1 + 2 * twos:2], sizes[2:2 + 2 * twos:2]
    slack = jnp.minimum(giver - 1, most - sink)
    moved = jax.random.randint(jax.random.fold_in(key, 1), (twos,), 0, 1 << 20) % (slack + 1)
    sizes = sizes.at[1:1 + 2 * twos:2].set(giver - moved).at[2:2 + 2 * twos:2].set(sink + moved)
    return sizes[jax.random.permutation(jax.random.fold_in(key, 2), amount)]


def normal_values(own_key, extent, scale, reach, cuts=(), kind=jnp.bfloat16):
    loudness = levels(own_key, extent, cuts, -0.22, 0.18) if cuts else 1.0
    values = jax.random.normal(own_key, extent, jnp.float32) * scale * loudness
    return jnp.minimum(jnp.maximum(values, -reach), reach).astype(kind)


def setup_inputs(seed: int = 0) -> dict:
    seeds = jax.random.split(jax.random.key(seed), 9)
    frames = draw_frames(jax.random.fold_in(seeds[8], 71), 0)
    lengths = uneven_parts(seeds[1], RECS, 3 * RECS * LEN // 5, LEN, 1).astype(jnp.int32)
    w_in = draw_w_in(jax.random.fold_in(seeds[8], 71), 0)
    w_dw = normal_values(seeds[3], (K, C), K ** -0.5, 1.0, (), jnp.float32)
    bn_gain = jnp.clip(1.0 + 0.15 * jax.random.normal(seeds[4], (C,), jnp.float32), 0.25, 1.75)
    bn_bias = jnp.clip(jax.random.uniform(seeds[5], (C,), jnp.float32, -1.0, 1.0), -1.0, 1.0)
    w_out = normal_values(seeds[6], (C, C), C ** -0.5, 0.1875)
    cotangent = normal_values(seeds[7], (RECS, LEN, C), 1.0, 6.0, ((0, 8), (1, 4)))
    return {"frames": frames, "lengths": lengths, "w_in": w_in, "w_dw": w_dw, "bn_gain": bn_gain, "bn_bias": bn_bias, "w_out": w_out, "cotangent": cotangent}


def taps_forward(padded, kernel, frame_count):
    summed = jnp.zeros((frame_count, padded.shape[1]), jnp.float32)
    for tap_index in range(kernel.shape[0]):
        summed = summed + kernel[tap_index] * padded[tap_index:tap_index + frame_count].astype(jnp.float32)
    return summed

def taps_backward(padded_grad, kernel, frame_count):
    reach_both = kernel.shape[0] - 1
    summed = jnp.zeros((frame_count, padded_grad.shape[1]), jnp.float32)
    for tap_index in range(kernel.shape[0]):
        begin = reach_both - tap_index
        summed = summed + kernel[tap_index] * padded_grad[begin:begin + frame_count].astype(jnp.float32)
    return summed

def taps_kernel(padded_glu, dconv_rows, kernel_taps, frame_count):
    grad_rows = dconv_rows.astype(jnp.float32)
    tap_rows = []
    for tap_index in range(kernel_taps):
        tap_rows.append(lax.optimization_barrier(jnp.sum(padded_glu[tap_index:tap_index + frame_count].astype(jnp.float32) * grad_rows, axis=0)))
    return jnp.stack(tap_rows)

def front(rec_frames, rec_length, w_in, w_dw):
    live_rows = (jnp.arange(LEN, dtype=jnp.int32) < rec_length).astype(jnp.float32)[:, None]
    pre_act = jnp.dot(rec_frames, w_in, preferred_element_type=jnp.float32)
    linear_half = pre_act[:, :C]
    gate_sig = jax.nn.sigmoid(pre_act[:, C:])
    glu_out = (linear_half * gate_sig * live_rows).astype(jnp.bfloat16)
    padded = jnp.pad(glu_out, ((HALO, HALO), (0, 0)))
    conv_out = taps_forward(padded, w_dw, LEN)
    return (live_rows, linear_half, gate_sig, padded, conv_out)

def middle(conv_out, live_rows, mean_vec, inv_std, bn_gain, bn_bias):
    normed = (conv_out - mean_vec) * inv_std
    shifted = bn_gain * normed + bn_bias
    act_sig = jax.nn.sigmoid(shifted)
    swished = (shifted * act_sig * live_rows).astype(jnp.bfloat16)
    return (normed, shifted, act_sig, swished)

def shift_grad(rec_cot, w_out, live_rows, shifted, act_sig):
    dswish = jnp.dot(rec_cot, w_out.T, preferred_element_type=jnp.float32)
    return live_rows * dswish * act_sig * (1.0 + shifted * (1.0 - act_sig))

def reference(frames, lengths, w_in, w_dw, bn_gain, bn_bias, w_out, cotangent):

    def moments(item):
        rec_frames, rec_length = item
        live_rows, linear_half, gate_sig, padded, conv_out = front(rec_frames, rec_length, w_in, w_dw)
        return (lax.optimization_barrier(jnp.sum(conv_out * live_rows, axis=0)), lax.optimization_barrier(jnp.sum(conv_out * conv_out * live_rows, axis=0)))
    sums_all, squares_all = lax.map(moments, (frames, lengths))
    count = jnp.sum(lengths).astype(jnp.float32)
    mean_vec = lax.optimization_barrier(jnp.sum(sums_all, axis=0)) / count
    variance = lax.optimization_barrier(jnp.sum(squares_all, axis=0)) / count - mean_vec * mean_vec
    inv_std = lax.rsqrt(variance + 1e-05)

    def second(item):
        rec_frames, rec_length, rec_cot = item
        live_rows, linear_half, gate_sig, padded, conv_out = front(rec_frames, rec_length, w_in, w_dw)
        normed, shifted, act_sig, swished = middle(conv_out, live_rows, mean_vec, inv_std, bn_gain, bn_bias)
        out_rows = jnp.dot(swished, w_out, preferred_element_type=jnp.float32).astype(jnp.bfloat16)
        dshift = shift_grad(rec_cot, w_out, live_rows, shifted, act_sig)
        return (out_rows, lax.optimization_barrier(jnp.sum(dshift * normed, axis=0)), lax.optimization_barrier(jnp.sum(dshift, axis=0)))
    output, gain_parts, bias_parts = lax.map(second, (frames, lengths, cotangent))
    sum_gain = lax.optimization_barrier(jnp.sum(gain_parts, axis=0))
    sum_bias = lax.optimization_barrier(jnp.sum(bias_parts, axis=0))

    def third(carry_pair, item):
        weight_sum, kernel_sum = carry_pair
        rec_frames, rec_length, rec_cot = item
        live_rows, linear_half, gate_sig, padded, conv_out = front(rec_frames, rec_length, w_in, w_dw)
        normed, shifted, act_sig, swished = middle(conv_out, live_rows, mean_vec, inv_std, bn_gain, bn_bias)
        dshift = shift_grad(rec_cot, w_out, live_rows, shifted, act_sig)
        dconv = (live_rows * bn_gain * inv_std * (dshift - sum_bias / count - normed * sum_gain / count)).astype(jnp.bfloat16)
        padded_grad = jnp.pad(dconv, ((HALO, HALO), (0, 0)))
        dglu = live_rows * taps_backward(padded_grad, w_dw, LEN)
        dpre = jnp.concatenate([dglu * gate_sig, dglu * linear_half * gate_sig * (1.0 - gate_sig)], axis=1).astype(jnp.bfloat16)
        grad_rows = jnp.dot(dpre, w_in.T, preferred_element_type=jnp.float32).astype(jnp.bfloat16)
        term_in = jnp.dot(rec_frames.T, dpre, preferred_element_type=jnp.float32)
        term_out = jnp.dot(swished.T, rec_cot, preferred_element_type=jnp.float32)
        weight_sum = weight_sum + jnp.concatenate([term_in, term_out], axis=1)
        kernel_sum = kernel_sum + taps_kernel(padded, dconv, K, LEN)
        return ((weight_sum, kernel_sum), grad_rows)
    start_pair = (jnp.zeros((C, 3 * C), jnp.float32), jnp.zeros((K, C), jnp.float32))
    final_pair, grad_frames = lax.scan(third, start_pair, (frames, lengths, cotangent))
    scale = 1.0 / math.sqrt(RECS * LEN)
    weight_sum, kernel_sum = final_pair
    grad_w_in = weight_sum[:, :2 * C] * scale
    grad_w_out = weight_sum[:, 2 * C:] * scale
    return (output, grad_frames, grad_w_in, grad_w_out, kernel_sum * scale, sum_gain * scale, sum_bias * scale)
```

```python
import functools
import math

import jax
import jax.numpy as jnp
from jax import lax
from jax.experimental import pallas as pl
from jax.experimental.pallas import tpu as pltpu
from jax.sharding import PartitionSpec as P

F32 = jnp.float32
BF16 = jnp.bfloat16
LANES = 128
BLOCK = 256
SUB = BLOCK // LANES
WIDE = 32
NEAR = 16
VMEM_LIMIT = 56 << 20


def dot_nn(a, b):
    return lax.dot_general(a, b, (((1,), (0,)), ((), ())), preferred_element_type=F32)


def dot_nt(a, b):
    return lax.dot_general(a, b, (((1,), (1,)), ((), ())), preferred_element_type=F32)


def dot_tn(a, b):
    return lax.dot_general(a, b, (((0,), (0,)), ((), ())), preferred_element_type=F32)


def logistic(x):
    return 1.0 / (1.0 + jnp.exp(-x))


def row_mask(start, count, low, high):
    rows = start + lax.broadcasted_iota(jnp.int32, (count, LANES), 0)
    return (rows >= low) & (rows < high)


def taps_chunk(src, c, begin, count, weight_row, taps):
    tiles = count // 8
    sums = [None] * tiles
    for residue in range(8):
        own = list(range(residue, taps, 8))
        weights = [jnp.broadcast_to(weight_row(k), (8, LANES)) for k in own]
        for q in range(tiles + len(own) - 1):
            tile = src[c, pl.ds(begin + residue + 8 * q, 8), :]
            for i, weight in enumerate(weights):
                u = q - i
                if 0 <= u < tiles:
                    term = weight * tile
                    sums[u] = term if sums[u] is None else sums[u] + term
    return sums


def lanes_of(c):
    return slice(c * LANES, (c + 1) * LANES)


def gate_kernel(span_ref, feats_ref, lin_w_ref, gate_w_ref, glu_ref, first_ref, second_ref):
    rows = feats_ref.shape[0]
    step = 256 if rows % 256 == 0 else rows
    for r in range(0, rows, step):
        lin = dot_nn(feats_ref[r : r + step, :], lin_w_ref[...])
        sig = logistic(dot_nn(feats_ref[r : r + step, :], gate_w_ref[...]))
        for c in range(SUB):
            lin_c, sig_c = lin[:, lanes_of(c)], sig[:, lanes_of(c)]
            live = row_mask(r, step, span_ref[0], span_ref[1])
            sig_c = jnp.where(live, sig_c, 0.0)
            prod = lin_c * sig_c
            glu_ref[c, r : r + step, :] = prod.astype(BF16)
            first_ref[r : r + step, lanes_of(c)] = sig_c.astype(BF16)
            second_ref[r : r + step, lanes_of(c)] = (prod * (1.0 - sig_c)).astype(BF16)


def gated(span, feats, w_in):
    rows, depth = feats.shape
    channels = w_in.shape[1] // 2
    blocks = channels // BLOCK
    return pl.pallas_call(
        gate_kernel,
        grid=(blocks,),
        in_specs=[
            pl.BlockSpec(memory_space=pltpu.SMEM),
            pl.BlockSpec((rows, depth), lambda j: (0, 0)),
            pl.BlockSpec((depth, BLOCK), lambda j: (0, j)),
            pl.BlockSpec((depth, BLOCK), lambda j: (0, j + blocks)),
        ],
        out_specs=[
            pl.BlockSpec((SUB, rows, LANES), lambda j: (j, 0, 0)),
            pl.BlockSpec((rows, BLOCK), lambda j: (0, j)),
            pl.BlockSpec((rows, BLOCK), lambda j: (0, j)),
        ],
        out_shape=[
            jax.ShapeDtypeStruct((channels // LANES, rows, LANES), BF16),
            jax.ShapeDtypeStruct((rows, channels), BF16),
            jax.ShapeDtypeStruct((rows, channels), BF16),
        ],
        compiler_params=pltpu.CompilerParams(vmem_limit_bytes=VMEM_LIMIT),
        cost_estimate=pl.CostEstimate(
            flops=4 * rows * depth * channels, bytes_accessed=14 * rows * channels, transcendentals=rows * channels
        ),
        name="gated",
    )(span, feats, w_in, w_in)


def conv_kernel(span_ref, before_ref, after_ref, lin_w_ref, gate_w_ref, taps_ref, glu_ref, conv_ref, edge_ref, sums_ref, ext):
    rows = glu_ref.shape[1]
    taps = taps_ref.shape[0]
    full = rows + 2 * NEAR
    halo = jnp.concatenate([before_ref[...], after_ref[...]], axis=0)
    lin = dot_nn(halo, lin_w_ref[...])
    sig = logistic(dot_nn(halo, gate_w_ref[...]))
    low, high = span_ref[0], span_ref[1]
    live = jnp.concatenate([row_mask(-WIDE, WIDE, low, high), row_mask(rows, WIDE, low, high)], axis=0)
    for c in range(SUB):
        edge = jnp.where(live, lin[:, lanes_of(c)] * sig[:, lanes_of(c)], 0.0).astype(BF16)
        edge_ref[c] = edge
        edge = edge.astype(F32)
        ext[c, 0:WIDE, :] = edge[:WIDE]
        ext[c, WIDE + rows :, :] = edge[WIDE:]
        ext[c, WIDE : WIDE + rows, :] = glu_ref[c].astype(F32)
    count = 160 if full % 160 == 0 else NEAR
    own_low = jnp.maximum(low, 0) + NEAR
    own_high = jnp.minimum(high, rows) + NEAR
    shift = WIDE - NEAR - (taps - 1) // 2
    for c in range(SUB):

        def chunk(i, carry):
            r = pl.multiple_of(i * count, count)
            tiles = taps_chunk(ext, c, r + shift, count, lambda k: taps_ref[k : k + 1, lanes_of(c)], taps)
            total, square = carry
            for u, tile in enumerate(tiles):
                conv_ref[c, pl.ds(r + 8 * u, 8), :] = tile
                kept = jnp.where(row_mask(r + 8 * u, 8, own_low, own_high), tile, 0.0)
                total = total + kept
                square = square + kept * kept
            return total, square

        zero = jnp.zeros((8, LANES), F32)
        total, square = lax.fori_loop(0, full // count, chunk, (zero, zero))
        sums_ref[0:1, lanes_of(c)] = jnp.sum(total, axis=0, keepdims=True)
        sums_ref[1:2, lanes_of(c)] = jnp.sum(square, axis=0, keepdims=True)
    live_rows = jnp.maximum(own_high - own_low, 0).astype(F32)
    sums_ref[2:3, :] = jnp.full((1, BLOCK), 1.0, F32) * live_rows


def convolved(span, before, after, w_in, w_dw, glu):
    groups, rows, _ = glu.shape
    channels = groups * LANES
    depth = w_in.shape[0]
    taps = w_dw.shape[0]
    blocks = channels // BLOCK
    full = rows + 2 * NEAR
    return pl.pallas_call(
        conv_kernel,
        grid=(blocks,),
        in_specs=[
            pl.BlockSpec(memory_space=pltpu.SMEM),
            pl.BlockSpec((WIDE, depth), lambda j: (0, 0)),
            pl.BlockSpec((WIDE, depth), lambda j: (0, 0)),
            pl.BlockSpec((depth, BLOCK), lambda j: (0, j)),
            pl.BlockSpec((depth, BLOCK), lambda j: (0, j + blocks)),
            pl.BlockSpec((taps, BLOCK), lambda j: (0, j)),
            pl.BlockSpec((SUB, rows, LANES), lambda j: (j, 0, 0)),
        ],
        out_specs=[
            pl.BlockSpec((SUB, full, LANES), lambda j: (j, 0, 0)),
            pl.BlockSpec((SUB, 2 * WIDE, LANES), lambda j: (j, 0, 0)),
            pl.BlockSpec((3, BLOCK), lambda j: (0, j)),
        ],
        out_shape=[
            jax.ShapeDtypeStruct((groups, full, LANES), F32),
            jax.ShapeDtypeStruct((groups, 2 * WIDE, LANES), BF16),
            jax.ShapeDtypeStruct((3, channels), F32),
        ],
        scratch_shapes=[pltpu.VMEM((SUB, rows + 2 * WIDE, LANES), F32)],
        compiler_params=pltpu.CompilerParams(vmem_limit_bytes=VMEM_LIMIT),
        cost_estimate=pl.CostEstimate(
            flops=4 * rows * depth * channels, bytes_accessed=14 * rows * channels, transcendentals=rows * channels
        ),
        name="convolved",
    )(span, before, after, w_in, w_in, w_dw, glu)


def back_kernel(before_ref, own_ref, after_ref, w_ref, out_ref):
    rows = own_ref.shape[0]
    w = w_ref[...]
    for part, at in ((before_ref, 0), (own_ref, NEAR), (after_ref, NEAR + rows)):
        prod = dot_nt(part[...], w)
        for c in range(SUB):
            out_ref[c, at : at + part.shape[0], :] = prod[:, lanes_of(c)]


def back_projected(before, cot, after, w_out):
    rows, features = cot.shape
    channels = w_out.shape[0]
    full = rows + 2 * NEAR
    return pl.pallas_call(
        back_kernel,
        grid=(channels // BLOCK,),
        in_specs=[
            pl.BlockSpec((NEAR, features), lambda j: (0, 0)),
            pl.BlockSpec((rows, features), lambda j: (0, 0)),
            pl.BlockSpec((NEAR, features), lambda j: (0, 0)),
            pl.BlockSpec((BLOCK, features), lambda j: (j, 0)),
        ],
        out_specs=pl.BlockSpec((SUB, full, LANES), lambda j: (j, 0, 0)),
        out_shape=jax.ShapeDtypeStruct((channels // LANES, full, LANES), F32),
        compiler_params=pltpu.CompilerParams(vmem_limit_bytes=VMEM_LIMIT),
        cost_estimate=pl.CostEstimate(
            flops=2 * rows * features * channels, bytes_accessed=8 * rows * channels, transcendentals=0
        ),
        name="back_projected",
    )(before, cot, after, w_out)


def moments(sums_ref, c):
    at = lanes_of(c)
    count = sums_ref[2:3, at]
    mean = sums_ref[0:1, at] / count
    variance = sums_ref[1:2, at] / count - mean * mean
    return mean, lax.rsqrt(variance + 1e-05), count


def swish_kernel(span_ref, sums_ref, gain_ref, bias_ref, conv_ref, back_ref, swished_ref, dshift_ref, terms_ref):
    rows = swished_ref.shape[0]
    low, high = span_ref[0], span_ref[1]
    count = 128 if rows % 128 == 0 else NEAR
    for c in range(SUB):
        mean, inv_std, _ = moments(sums_ref, c)
        gain, bias = gain_ref[:, lanes_of(c)], bias_ref[:, lanes_of(c)]

        def piece(r, size):
            at = pl.ds(r, size)
            normed = (conv_ref[c, at, :] - mean) * inv_std
            shifted = gain * normed + bias
            sig = logistic(shifted)
            live = row_mask(r - NEAR, size, low, high)
            swished = jnp.where(live, shifted * sig, 0.0)
            slope = sig + swished * (1.0 - sig)
            dshift = jnp.where(live, back_ref[c, at, :] * slope, 0.0)
            dshift_ref[c, at, :] = dshift
            return normed, swished, dshift

        def chunk(i, carry):
            r = pl.multiple_of(i * count, count)
            normed, swished, dshift = piece(r + NEAR, count)
            swished_ref[pl.ds(r, count), lanes_of(c)] = swished.astype(BF16)
            by_gain, by_bias = carry
            by_gain = by_gain + jnp.sum((dshift * normed).reshape(count // 8, 8, LANES), axis=0)
            by_bias = by_bias + jnp.sum(dshift.reshape(count // 8, 8, LANES), axis=0)
            return by_gain, by_bias

        zero = jnp.zeros((8, LANES), F32)
        by_gain, by_bias = lax.fori_loop(0, rows // count, chunk, (zero, zero))
        piece(0, NEAR)
        piece(rows + NEAR, NEAR)
        terms_ref[0:1, lanes_of(c)] = jnp.sum(by_gain, axis=0, keepdims=True)
        terms_ref[1:2, lanes_of(c)] = jnp.sum(by_bias, axis=0, keepdims=True)


def swish(span, sums, gain, bias, conv, back):
    groups, full, _ = conv.shape
    rows = full - 2 * NEAR
    channels = groups * LANES
    vector = pl.BlockSpec((1, BLOCK), lambda j: (0, j))
    tall = pl.BlockSpec((SUB, full, LANES), lambda j: (j, 0, 0))
    return pl.pallas_call(
        swish_kernel,
        grid=(channels // BLOCK,),
        in_specs=[
            pl.BlockSpec(memory_space=pltpu.SMEM),
            pl.BlockSpec((3, BLOCK), lambda j: (0, j)),
            vector,
            vector,
            tall,
            tall,
        ],
        out_specs=[
            pl.BlockSpec((rows, BLOCK), lambda j: (0, j)),
            tall,
            pl.BlockSpec((2, BLOCK), lambda j: (0, j)),
        ],
        out_shape=[
            jax.ShapeDtypeStruct((rows, channels), BF16),
            jax.ShapeDtypeStruct((groups, full, LANES), F32),
            jax.ShapeDtypeStruct((2, channels), F32),
        ],
        compiler_params=pltpu.CompilerParams(vmem_limit_bytes=VMEM_LIMIT),
        cost_estimate=pl.CostEstimate(
            flops=30 * rows * channels, bytes_accessed=14 * rows * channels, transcendentals=rows * channels
        ),
        name="swish",
    )(span, sums, gain, bias, conv, back)


def grad_kernel(
    span_ref, sums_ref, terms_ref, gain_ref, taps_ref, conv_ref, dshift_ref, first_ref, second_ref, dpre_ref, dconv_ref, ext
):
    rows = first_ref.shape[0]
    taps = taps_ref.shape[0]
    full = rows + 2 * NEAR
    low, high = span_ref[0], span_ref[1]
    span = 160 if full % 160 == 0 else NEAR
    count = 128 if rows % 128 == 0 else NEAR
    shift = NEAR - (taps - 1) // 2
    for c in range(SUB):
        mean, inv_std, total = moments(sums_ref, c)
        at = lanes_of(c)
        outer = gain_ref[:, at] * inv_std
        by_gain = terms_ref[0:1, at] / total
        by_bias = terms_ref[1:2, at] / total

        @pl.loop(0, full // span)
        def _(i):
            r = pl.multiple_of(i * span, span)
            normed = (conv_ref[c, pl.ds(r, span), :] - mean) * inv_std
            value = outer * (dshift_ref[c, pl.ds(r, span), :] - by_bias - normed * by_gain)
            live = row_mask(r - NEAR, span, low, high)
            ext[c, pl.ds(r, span), :] = jnp.where(live, value, 0.0).astype(BF16).astype(F32)

        dconv_ref[c] = ext[c, NEAR : NEAR + rows, :].astype(BF16)

        @pl.loop(0, rows // count)
        def _(i):
            r = pl.multiple_of(i * count, count)
            tiles = taps_chunk(ext, c, r + shift, count, lambda k: taps_ref[taps - 1 - k : taps - k, at], taps)
            dglu = jnp.concatenate(tiles, axis=0)
            dpre_ref[0, pl.ds(r, count), at] = (dglu * first_ref[pl.ds(r, count), at].astype(F32)).astype(BF16)
            dpre_ref[1, pl.ds(r, count), at] = (dglu * second_ref[pl.ds(r, count), at].astype(F32)).astype(BF16)


def norm_grad(span, sums, terms, gain, w_dw, conv, dshift, first, second):
    groups, full, _ = conv.shape
    rows = full - 2 * NEAR
    channels = groups * LANES
    taps = w_dw.shape[0]
    tall = pl.BlockSpec((SUB, full, LANES), lambda j: (j, 0, 0))
    flat = pl.BlockSpec((rows, BLOCK), lambda j: (0, j))
    return pl.pallas_call(
        grad_kernel,
        grid=(channels // BLOCK,),
        in_specs=[
            pl.BlockSpec(memory_space=pltpu.SMEM),
            pl.BlockSpec((3, BLOCK), lambda j: (0, j)),
            pl.BlockSpec((2, BLOCK), lambda j: (0, j)),
            pl.BlockSpec((1, BLOCK), lambda j: (0, j)),
            pl.BlockSpec((taps, BLOCK), lambda j: (0, j)),
            tall,
            tall,
            flat,
            flat,
        ],
        out_specs=[
            pl.BlockSpec((2, rows, BLOCK), lambda j: (0, 0, j)),
            pl.BlockSpec((SUB, rows, LANES), lambda j: (j, 0, 0)),
        ],
        out_shape=[
            jax.ShapeDtypeStruct((2, rows, channels), BF16),
            jax.ShapeDtypeStruct((groups, rows, LANES), BF16),
        ],
        scratch_shapes=[pltpu.VMEM((SUB, full, LANES), F32)],
        compiler_params=pltpu.CompilerParams(vmem_limit_bytes=VMEM_LIMIT),
        cost_estimate=pl.CostEstimate(
            flops=70 * rows * channels, bytes_accessed=16 * rows * channels, transcendentals=0
        ),
        name="norm_grad",
    )(span, sums, terms, gain, w_dw, conv, dshift, first, second)


def tap_grad_kernel(edge_ref, glu_ref, dconv_ref, out_ref, ext, own):
    rows = glu_ref.shape[1]
    taps = out_ref.shape[0]
    shift = WIDE - (taps - 1) // 2
    tiles = 4 if rows % 32 == 0 else 2
    for c in range(SUB):
        ext[c, 0:WIDE, :] = edge_ref[c, 0:WIDE, :].astype(F32)
        ext[c, WIDE : WIDE + rows, :] = glu_ref[c].astype(F32)
        ext[c, WIDE + rows :, :] = edge_ref[c, WIDE:, :].astype(F32)
        own[c] = dconv_ref[c].astype(F32)
    for c in range(SUB):

        def chunk(i, carry):
            sums = list(carry)
            r = pl.multiple_of(i * 8 * tiles, 8 * tiles)
            grads = [own[c, pl.ds(r + 8 * m, 8), :] for m in range(tiles)]
            for offset in range(taps + 8 * (tiles - 1)):
                held = None
                for m in range(tiles):
                    k = offset - 8 * m
                    if 0 <= k < taps:
                        if held is None:
                            held = ext[c, pl.ds(r + shift + offset, 8), :]
                        sums[k] = sums[k] + held * grads[m]
            return tuple(sums)

        zero = jnp.zeros((8, LANES), F32)
        sums = lax.fori_loop(0, rows // (8 * tiles), chunk, (zero,) * taps)
        for k in range(taps):
            out_ref[k : k + 1, lanes_of(c)] = jnp.sum(sums[k], axis=0, keepdims=True)


def tap_grad(edge, glu, dconv, taps):
    groups, rows, _ = glu.shape
    channels = groups * LANES
    return pl.pallas_call(
        tap_grad_kernel,
        grid=(channels // BLOCK,),
        in_specs=[
            pl.BlockSpec((SUB, 2 * WIDE, LANES), lambda j: (j, 0, 0)),
            pl.BlockSpec((SUB, rows, LANES), lambda j: (j, 0, 0)),
            pl.BlockSpec((SUB, rows, LANES), lambda j: (j, 0, 0)),
        ],
        out_specs=pl.BlockSpec((taps, BLOCK), lambda j: (0, j)),
        out_shape=jax.ShapeDtypeStruct((taps, channels), F32),
        scratch_shapes=[
            pltpu.VMEM((SUB, rows + 2 * WIDE, LANES), F32),
            pltpu.VMEM((SUB, rows, LANES), F32),
        ],
        compiler_params=pltpu.CompilerParams(vmem_limit_bytes=VMEM_LIMIT),
        cost_estimate=pl.CostEstimate(flops=62 * rows * channels, bytes_accessed=4 * rows * channels, transcendentals=0),
        name="tap_grad",
    )(edge, glu, dconv)


def frames_grad_kernel(dpre_ref, w_ref, out_ref):
    channels = dpre_ref.shape[2]
    total = dot_nt(dpre_ref[0], w_ref[:, :channels]) + dot_nt(dpre_ref[1], w_ref[:, channels:])
    out_ref[...] = total.astype(BF16)


def frames_grad(dpre, w_in):
    _, rows, channels = dpre.shape
    depth = w_in.shape[0]
    return pl.pallas_call(
        frames_grad_kernel,
        grid=(depth // BLOCK,),
        in_specs=[
            pl.BlockSpec((2, rows, channels), lambda j: (0, 0, 0)),
            pl.BlockSpec((BLOCK, 2 * channels), lambda j: (j, 0)),
        ],
        out_specs=pl.BlockSpec((rows, BLOCK), lambda j: (0, j)),
        out_shape=jax.ShapeDtypeStruct((rows, depth), BF16),
        compiler_params=pltpu.CompilerParams(vmem_limit_bytes=VMEM_LIMIT),
        cost_estimate=pl.CostEstimate(
            flops=4 * rows * depth * channels, bytes_accessed=10 * rows * depth, transcendentals=0
        ),
        name="frames_grad",
    )(dpre, w_in)


def weight_kernel(owner_rows, core_ref, left_ref, right_ref, send_ref, keep_ref):
    term = dot_tn(left_ref[...], right_ref[0])
    depth, width = term.shape
    term = term.reshape(depth // (2 * owner_rows), 2, owner_rows, width)
    even = term[:, 0].reshape(depth // 2, width)
    odd = term[:, 1].reshape(depth // 2, width)
    is_odd = core_ref[0] == 1
    send_ref[...] = jnp.where(is_odd, even, odd).astype(BF16)
    keep_ref[...] = jnp.where(is_odd, odd, even).astype(BF16)


def weight_term(core, left, right, owner_rows):
    halves, rows, width = right.shape
    depth = left.shape[1]
    step = 512
    per = width // step
    out = pl.BlockSpec((depth // 2, step), lambda j: (0, j))
    shape = jax.ShapeDtypeStruct((depth // 2, halves * width), BF16)
    return pl.pallas_call(
        functools.partial(weight_kernel, owner_rows),
        grid=(halves * per,),
        in_specs=[
            pl.BlockSpec(memory_space=pltpu.SMEM),
            pl.BlockSpec((rows, depth), lambda j: (0, 0)),
            pl.BlockSpec((1, rows, step), lambda j: (j // per, 0, j % per)),
        ],
        out_specs=[out, out],
        out_shape=[shape, shape],
        compiler_params=pltpu.CompilerParams(vmem_limit_bytes=VMEM_LIMIT),
        cost_estimate=pl.CostEstimate(
            flops=2 * halves * rows * depth * width, bytes_accessed=6 * halves * rows * width, transcendentals=0
        ),
        name="weight_term",
    )(core, left, right)


def swap(x, axis, mask):
    return lax.ppermute(x, axis, [(i, i ^ mask) for i in range(lax.axis_size(axis))])


def masks_of(axis):
    return [1 << i for i in range((lax.axis_size(axis) - 1).bit_length())]


def all_sum(x):
    for axis in ("tm", "dp"):
        for mask in masks_of(axis):
            x = x + swap(x, axis, mask)
    return x


def halve_rest(part, order, bits):
    left = list(bits)
    for axis, mask in order:
        dim = left.index((axis, mask))
        mine = (lax.axis_index(axis) & mask) != 0
        low = lax.index_in_dim(part, 0, dim, keepdims=False)
        high = lax.index_in_dim(part, 1, dim, keepdims=False)
        got = swap(jnp.where(mine, low, high), axis, mask)
        part = jnp.where(mine, high, low).astype(F32) + got.astype(F32)
        left.pop(dim)
        if left:
            part = part.astype(BF16)
    return part


def scatter_sum(send, keep, owner_rows):
    bits = [("dp", m) for m in reversed(masks_of("dp"))] + [("tm", m) for m in reversed(masks_of("tm")[1:])]
    got = swap(send, "tm", 1)
    both = (keep.astype(F32) + got.astype(F32)).astype(BF16)
    width = both.shape[1]
    both = both.reshape((2,) * len(bits) + (owner_rows, width))
    along_y = [("tm", m) for m in masks_of("tm")[1:]]
    along = [("dp", m) for m in masks_of("dp")]
    orders = [
        along_y + along,
        along[:1] + along_y + along[1:],
        along[1:2] + along_y + along[:1] + along[2:],
    ]
    tiles = width // LANES
    cuts = [0, -(-3 * tiles // 8) * LANES, 2 * -(-3 * tiles // 8) * LANES, width]
    parts = [halve_rest(both[..., a:b], order, bits) for a, b, order in zip(cuts, cuts[1:], orders)]
    return jnp.concatenate(parts, axis=1)


def local(frames, lengths, w_in, w_dw, bn_gain, bn_bias, w_out, cotangent):
    feats, cot = frames[0], cotangent[0]
    rows, depth = feats.shape
    taps = w_dw.shape[0]
    tm_count = lax.axis_size("tm")
    device_count = lax.axis_size("dp") * tm_count
    owner_rows = depth // device_count
    place = lax.axis_index("tm")
    offset = place * rows
    span = jnp.stack([-offset, lengths[0] - offset]).astype(jnp.int32)
    core = (place & 1).astype(jnp.int32).reshape(1)
    gain, bias = bn_gain[None], bn_bias[None]

    tail = jnp.concatenate([feats[rows - WIDE :], cot[rows - NEAR :]], axis=0)
    head = jnp.concatenate([feats[:WIDE], cot[:NEAR]], axis=0)
    before = lax.ppermute(tail, "tm", [(i, i + 1) for i in range(tm_count - 1)])
    after = lax.ppermute(head, "tm", [(i + 1, i) for i in range(tm_count - 1)])

    glu, first, second = gated(span, feats, w_in)
    conv, edge, sums = convolved(span, before[:WIDE], after[:WIDE], w_in, w_dw, glu)
    sums = all_sum(sums)
    back = back_projected(before[WIDE:], cot, after[WIDE:], w_out)
    swished, dshift, terms = swish(span, sums, gain, bias, conv, back)
    terms = all_sum(terms)
    out_rows = dot_nn(swished, w_out).astype(BF16)
    grad_w_out = scatter_sum(*weight_term(core, swished, cotangent, owner_rows), owner_rows)
    dpre, dconv = norm_grad(span, sums, terms, gain, w_dw, conv, dshift, first, second)
    kernel_sum = lax.psum(tap_grad(edge, glu, dconv, taps), ("dp", "tm"))
    grad_w_in = scatter_sum(*weight_term(core, feats, dpre, owner_rows), owner_rows)
    grad_rows = frames_grad(dpre, w_in)
    scale = 1.0 / math.sqrt(device_count * rows)
    return (
        out_rows[None],
        grad_rows[None],
        grad_w_in * scale,
        grad_w_out * scale,
        kernel_sum * scale,
        terms[0] * scale,
        terms[1] * scale,
    )


def solution(mesh):
    placed = (P("dp", "tm", None), P("dp"), P(), P(), P(), P(), P(), P("dp", "tm", None))
    return jax.shard_map(
        local,
        mesh=mesh,
        in_specs=placed,
        out_specs=(
            P("dp", "tm", None),
            P("dp", "tm", None),
            P(("dp", "tm"), None),
            P(("dp", "tm"), None),
            P(),
            P(),
            P(),
        ),
        check_vma=False,
    )
```

```python
import functools
import math

import jax
import jax.numpy as jnp
from jax import lax
from jax.experimental import pallas as pl
from jax.experimental.pallas import tpu as pltpu
from jax.sharding import PartitionSpec as P

F32 = jnp.float32
BF16 = jnp.bfloat16
LANES = 128
BLOCK = 256
SUB = BLOCK // LANES
WIDE = 32
NEAR = 16
VMEM_LIMIT = 56 << 20


def dot_nn(a, b):
    return lax.dot_general(a, b, (((1,), (0,)), ((), ())), preferred_element_type=F32)


def dot_nt(a, b):
    return lax.dot_general(a, b, (((1,), (1,)), ((), ())), preferred_element_type=F32)


def dot_tn(a, b):
    return lax.dot_general(a, b, (((0,), (0,)), ((), ())), preferred_element_type=F32)


def logistic(x):
    return 1.0 / (1.0 + jnp.exp(-x))


def row_mask(start, count, low, high):
    rows = start + lax.broadcasted_iota(jnp.int32, (count, LANES), 0)
    return (rows >= low) & (rows < high)


def taps_chunk(src, c, begin, count, weight_row, taps):
    tiles = count // 8
    sums = [None] * tiles
    for residue in range(8):
        own = list(range(residue, taps, 8))
        weights = [jnp.broadcast_to(weight_row(k), (8, LANES)) for k in own]
        for q in range(tiles + len(own) - 1):
            tile = src[c, pl.ds(begin + residue + 8 * q, 8), :]
            for i, weight in enumerate(weights):
                u = q - i
                if 0 <= u < tiles:
                    term = weight * tile
                    sums[u] = term if sums[u] is None else sums[u] + term
    return sums


def lanes_of(c):
    return slice(c * LANES, (c + 1) * LANES)


def gate_kernel(span_ref, feats_ref, lin_w_ref, gate_w_ref, glu_ref, first_ref, second_ref):
    rows = feats_ref.shape[0]
    step = 256 if rows % 256 == 0 else rows
    for r in range(0, rows, step):
        lin = dot_nn(feats_ref[r : r + step, :], lin_w_ref[...])
        sig = logistic(dot_nn(feats_ref[r : r + step, :], gate_w_ref[...]))
        for c in range(SUB):
            lin_c, sig_c = lin[:, lanes_of(c)], sig[:, lanes_of(c)]
            live = row_mask(r, step, span_ref[0], span_ref[1])
            sig_c = jnp.where(live, sig_c, 0.0)
            prod = lin_c * sig_c
            glu_ref[c, r : r + step, :] = prod.astype(BF16)
            first_ref[r : r + step, lanes_of(c)] = sig_c.astype(BF16)
            second_ref[r : r + step, lanes_of(c)] = (prod * (1.0 - sig_c)).astype(BF16)


def gated(span, feats, w_in):
    rows, depth = feats.shape
    channels = w_in.shape[1] // 2
    blocks = channels // BLOCK
    return pl.pallas_call(
        gate_kernel,
        grid=(blocks,),
        in_specs=[
            pl.BlockSpec(memory_space=pltpu.SMEM),
            pl.BlockSpec((rows, depth), lambda j: (0, 0)),
            pl.BlockSpec((depth, BLOCK), lambda j: (0, j)),
            pl.BlockSpec((depth, BLOCK), lambda j: (0, j + blocks)),
        ],
        out_specs=[
            pl.BlockSpec((SUB, rows, LANES), lambda j: (j, 0, 0)),
            pl.BlockSpec((rows, BLOCK), lambda j: (0, j)),
            pl.BlockSpec((rows, BLOCK), lambda j: (0, j)),
        ],
        out_shape=[
            jax.ShapeDtypeStruct((channels // LANES, rows, LANES), BF16),
            jax.ShapeDtypeStruct((rows, channels), BF16),
            jax.ShapeDtypeStruct((rows, channels), BF16),
        ],
        compiler_params=pltpu.CompilerParams(vmem_limit_bytes=VMEM_LIMIT),
        cost_estimate=pl.CostEstimate(
            flops=4 * rows * depth * channels, bytes_accessed=14 * rows * channels, transcendentals=rows * channels
        ),
        name="gated",
    )(span, feats, w_in, w_in)


def conv_kernel(span_ref, before_ref, after_ref, lin_w_ref, gate_w_ref, taps_ref, glu_ref, conv_ref, edge_ref, sums_ref, ext):
    rows = glu_ref.shape[1]
    taps = taps_ref.shape[0]
    full = rows + 2 * NEAR
    halo = jnp.concatenate([before_ref[...], after_ref[...]], axis=0)
    lin = dot_nn(halo, lin_w_ref[...])
    sig = logistic(dot_nn(halo, gate_w_ref[...]))
    low, high = span_ref[0], span_ref[1]
    live = jnp.concatenate([row_mask(-WIDE, WIDE, low, high), row_mask(rows, WIDE, low, high)], axis=0)
    for c in range(SUB):
        edge = jnp.where(live, lin[:, lanes_of(c)] * sig[:, lanes_of(c)], 0.0).astype(BF16)
        edge_ref[c] = edge
        edge = edge.astype(F32)
        ext[c, 0:WIDE, :] = edge[:WIDE]
        ext[c, WIDE + rows :, :] = edge[WIDE:]
        ext[c, WIDE : WIDE + rows, :] = glu_ref[c].astype(F32)
    count = 160 if full % 160 == 0 else NEAR
    own_low = jnp.maximum(low, 0) + NEAR
    own_high = jnp.minimum(high, rows) + NEAR
    shift = WIDE - NEAR - (taps - 1) // 2
    for c in range(SUB):

        def chunk(i, carry):
            r = pl.multiple_of(i * count, count)
            tiles = taps_chunk(ext, c, r + shift, count, lambda k: taps_ref[k : k + 1, lanes_of(c)], taps)
            total, square = carry
            for u, tile in enumerate(tiles):
                conv_ref[c, pl.ds(r + 8 * u, 8), :] = tile
                kept = jnp.where(row_mask(r + 8 * u, 8, own_low, own_high), tile, 0.0)
                total = total + kept
                square = square + kept * kept
            return total, square

        zero = jnp.zeros((8, LANES), F32)
        total, square = lax.fori_loop(0, full // count, chunk, (zero, zero))
        sums_ref[0:1, lanes_of(c)] = jnp.sum(total, axis=0, keepdims=True)
        sums_ref[1:2, lanes_of(c)] = jnp.sum(square, axis=0, keepdims=True)
    live_rows = jnp.maximum(own_high - own_low, 0).astype(F32)
    sums_ref[2:3, :] = jnp.full((1, BLOCK), 1.0, F32) * live_rows


def convolved(span, before, after, w_in, w_dw, glu):
    groups, rows, _ = glu.shape
    channels = groups * LANES
    depth = w_in.shape[0]
    taps = w_dw.shape[0]
    blocks = channels // BLOCK
    full = rows + 2 * NEAR
    return pl.pallas_call(
        conv_kernel,
        grid=(blocks,),
        in_specs=[
            pl.BlockSpec(memory_space=pltpu.SMEM),
            pl.BlockSpec((WIDE, depth), lambda j: (0, 0)),
            pl.BlockSpec((WIDE, depth), lambda j: (0, 0)),
            pl.BlockSpec((depth, BLOCK), lambda j: (0, j)),
            pl.BlockSpec((depth, BLOCK), lambda j: (0, j + blocks)),
            pl.BlockSpec((taps, BLOCK), lambda j: (0, j)),
            pl.BlockSpec((SUB, rows, LANES), lambda j: (j, 0, 0)),
        ],
        out_specs=[
            pl.BlockSpec((SUB, full, LANES), lambda j: (j, 0, 0)),
            pl.BlockSpec((SUB, 2 * WIDE, LANES), lambda j: (j, 0, 0)),
            pl.BlockSpec((3, BLOCK), lambda j: (0, j)),
        ],
        out_shape=[
            jax.ShapeDtypeStruct((groups, full, LANES), F32),
            jax.ShapeDtypeStruct((groups, 2 * WIDE, LANES), BF16),
            jax.ShapeDtypeStruct((3, channels), F32),
        ],
        scratch_shapes=[pltpu.VMEM((SUB, rows + 2 * WIDE, LANES), F32)],
        compiler_params=pltpu.CompilerParams(vmem_limit_bytes=VMEM_LIMIT),
        cost_estimate=pl.CostEstimate(
            flops=4 * rows * depth * channels, bytes_accessed=14 * rows * channels, transcendentals=rows * channels
        ),
        name="convolved",
    )(span, before, after, w_in, w_in, w_dw, glu)


def back_kernel(before_ref, own_ref, after_ref, w_ref, out_ref, left):
    rows = own_ref.shape[0]

    @pl.when(pl.program_id(0) == 0)
    def _():
        left[0:NEAR, :] = before_ref[...]
        left[NEAR : NEAR + rows, :] = own_ref[...]
        left[NEAR + rows :, :] = after_ref[...]

    prod = dot_nt(left[...], w_ref[...])
    for c in range(SUB):
        out_ref[c] = prod[:, lanes_of(c)]


def back_projected(before, cot, after, w_out):
    rows, features = cot.shape
    channels = w_out.shape[0]
    full = rows + 2 * NEAR
    return pl.pallas_call(
        back_kernel,
        grid=(channels // BLOCK,),
        in_specs=[
            pl.BlockSpec((NEAR, features), lambda j: (0, 0)),
            pl.BlockSpec((rows, features), lambda j: (0, 0)),
            pl.BlockSpec((NEAR, features), lambda j: (0, 0)),
            pl.BlockSpec((BLOCK, features), lambda j: (j, 0)),
        ],
        out_specs=pl.BlockSpec((SUB, full, LANES), lambda j: (j, 0, 0)),
        out_shape=jax.ShapeDtypeStruct((channels // LANES, full, LANES), F32),
        scratch_shapes=[pltpu.VMEM((full, features), BF16)],
        compiler_params=pltpu.CompilerParams(vmem_limit_bytes=VMEM_LIMIT),
        cost_estimate=pl.CostEstimate(
            flops=2 * rows * features * channels, bytes_accessed=8 * rows * channels, transcendentals=0
        ),
        name="back_projected",
    )(before, cot, after, w_out)


def moments(sums_ref, c):
    at = lanes_of(c)
    count = sums_ref[2:3, at]
    mean = sums_ref[0:1, at] / count
    variance = sums_ref[1:2, at] / count - mean * mean
    return mean, lax.rsqrt(variance + 1e-05), count


def swish_kernel(span_ref, sums_ref, gain_ref, bias_ref, conv_ref, back_ref, swished_ref, dshift_ref, terms_ref):
    rows = swished_ref.shape[0]
    low, high = span_ref[0], span_ref[1]
    count = 128 if rows % 128 == 0 else NEAR
    for c in range(SUB):
        mean, inv_std, _ = moments(sums_ref, c)
        gain, bias = gain_ref[:, lanes_of(c)], bias_ref[:, lanes_of(c)]

        def piece(r, size):
            at = pl.ds(r, size)
            normed = (conv_ref[c, at, :] - mean) * inv_std
            shifted = gain * normed + bias
            sig = logistic(shifted)
            live = row_mask(r - NEAR, size, low, high)
            swished = jnp.where(live, shifted * sig, 0.0)
            slope = sig + swished * (1.0 - sig)
            dshift = jnp.where(live, back_ref[c, at, :] * slope, 0.0)
            dshift_ref[c, at, :] = dshift
            return normed, swished, dshift

        def chunk(i, carry):
            r = pl.multiple_of(i * count, count)
            normed, swished, dshift = piece(r + NEAR, count)
            swished_ref[pl.ds(r, count), lanes_of(c)] = swished.astype(BF16)
            by_gain, by_bias = carry
            by_gain = by_gain + jnp.sum((dshift * normed).reshape(count // 8, 8, LANES), axis=0)
            by_bias = by_bias + jnp.sum(dshift.reshape(count // 8, 8, LANES), axis=0)
            return by_gain, by_bias

        zero = jnp.zeros((8, LANES), F32)
        by_gain, by_bias = lax.fori_loop(0, rows // count, chunk, (zero, zero))
        piece(0, NEAR)
        piece(rows + NEAR, NEAR)
        terms_ref[0:1, lanes_of(c)] = jnp.sum(by_gain, axis=0, keepdims=True)
        terms_ref[1:2, lanes_of(c)] = jnp.sum(by_bias, axis=0, keepdims=True)


def swish(span, sums, gain, bias, conv, back):
    groups, full, _ = conv.shape
    rows = full - 2 * NEAR
    channels = groups * LANES
    vector = pl.BlockSpec((1, BLOCK), lambda j: (0, j))
    tall = pl.BlockSpec((SUB, full, LANES), lambda j: (j, 0, 0))
    return pl.pallas_call(
        swish_kernel,
        grid=(channels // BLOCK,),
        in_specs=[
            pl.BlockSpec(memory_space=pltpu.SMEM),
            pl.BlockSpec((3, BLOCK), lambda j: (0, j)),
            vector,
            vector,
            tall,
            tall,
        ],
        out_specs=[
            pl.BlockSpec((rows, BLOCK), lambda j: (0, j)),
            tall,
            pl.BlockSpec((2, BLOCK), lambda j: (0, j)),
        ],
        out_shape=[
            jax.ShapeDtypeStruct((rows, channels), BF16),
            jax.ShapeDtypeStruct((groups, full, LANES), F32),
            jax.ShapeDtypeStruct((2, channels), F32),
        ],
        compiler_params=pltpu.CompilerParams(vmem_limit_bytes=VMEM_LIMIT),
        cost_estimate=pl.CostEstimate(
            flops=30 * rows * channels, bytes_accessed=14 * rows * channels, transcendentals=rows * channels
        ),
        name="swish",
    )(span, sums, gain, bias, conv, back)


def grad_kernel(
    span_ref, sums_ref, terms_ref, gain_ref, taps_ref, conv_ref, dshift_ref, first_ref, second_ref, dpre_ref, dconv_ref, ext
):
    rows = first_ref.shape[0]
    taps = taps_ref.shape[0]
    full = rows + 2 * NEAR
    low, high = span_ref[0], span_ref[1]
    span = 160 if full % 160 == 0 else NEAR
    count = 128 if rows % 128 == 0 else NEAR
    shift = NEAR - (taps - 1) // 2
    for c in range(SUB):
        mean, inv_std, total = moments(sums_ref, c)
        at = lanes_of(c)
        outer = gain_ref[:, at] * inv_std
        by_gain = terms_ref[0:1, at] / total
        by_bias = terms_ref[1:2, at] / total

        @pl.loop(0, full // span)
        def _(i):
            r = pl.multiple_of(i * span, span)
            normed = (conv_ref[c, pl.ds(r, span), :] - mean) * inv_std
            value = outer * (dshift_ref[c, pl.ds(r, span), :] - by_bias - normed * by_gain)
            live = row_mask(r - NEAR, span, low, high)
            ext[c, pl.ds(r, span), :] = jnp.where(live, value, 0.0).astype(BF16).astype(F32)

        dconv_ref[c] = ext[c, NEAR : NEAR + rows, :].astype(BF16)

        @pl.loop(0, rows // count)
        def _(i):
            r = pl.multiple_of(i * count, count)
            tiles = taps_chunk(ext, c, r + shift, count, lambda k: taps_ref[taps - 1 - k : taps - k, at], taps)
            dglu = jnp.concatenate(tiles, axis=0)
            dpre_ref[0, pl.ds(r, count), at] = (dglu * first_ref[pl.ds(r, count), at].astype(F32)).astype(BF16)
            dpre_ref[1, pl.ds(r, count), at] = (dglu * second_ref[pl.ds(r, count), at].astype(F32)).astype(BF16)


def norm_grad(span, sums, terms, gain, w_dw, conv, dshift, first, second):
    groups, full, _ = conv.shape
    rows = full - 2 * NEAR
    channels = groups * LANES
    taps = w_dw.shape[0]
    tall = pl.BlockSpec((SUB, full, LANES), lambda j: (j, 0, 0))
    flat = pl.BlockSpec((rows, BLOCK), lambda j: (0, j))
    return pl.pallas_call(
        grad_kernel,
        grid=(channels // BLOCK,),
        in_specs=[
            pl.BlockSpec(memory_space=pltpu.SMEM),
            pl.BlockSpec((3, BLOCK), lambda j: (0, j)),
            pl.BlockSpec((2, BLOCK), lambda j: (0, j)),
            pl.BlockSpec((1, BLOCK), lambda j: (0, j)),
            pl.BlockSpec((taps, BLOCK), lambda j: (0, j)),
            tall,
            tall,
            flat,
            flat,
        ],
        out_specs=[
            pl.BlockSpec((2, rows, BLOCK), lambda j: (0, 0, j)),
            pl.BlockSpec((SUB, rows, LANES), lambda j: (j, 0, 0)),
        ],
        out_shape=[
            jax.ShapeDtypeStruct((2, rows, channels), BF16),
            jax.ShapeDtypeStruct((groups, rows, LANES), BF16),
        ],
        scratch_shapes=[pltpu.VMEM((SUB, full, LANES), F32)],
        compiler_params=pltpu.CompilerParams(vmem_limit_bytes=VMEM_LIMIT),
        cost_estimate=pl.CostEstimate(
            flops=70 * rows * channels, bytes_accessed=16 * rows * channels, transcendentals=0
        ),
        name="norm_grad",
    )(span, sums, terms, gain, w_dw, conv, dshift, first, second)


def tap_grad_kernel(edge_ref, glu_ref, dconv_ref, out_ref, ext, own):
    rows = glu_ref.shape[1]
    taps = out_ref.shape[0]
    shift = WIDE - (taps - 1) // 2
    tiles = 4 if rows % 32 == 0 else 2
    for c in range(SUB):
        ext[c, 0:WIDE, :] = edge_ref[c, 0:WIDE, :].astype(F32)
        ext[c, WIDE : WIDE + rows, :] = glu_ref[c].astype(F32)
        ext[c, WIDE + rows :, :] = edge_ref[c, WIDE:, :].astype(F32)
        own[c] = dconv_ref[c].astype(F32)
    for c in range(SUB):

        def chunk(i, carry):
            sums = list(carry)
            r = pl.multiple_of(i * 8 * tiles, 8 * tiles)
            grads = [own[c, pl.ds(r + 8 * m, 8), :] for m in range(tiles)]
            for offset in range(taps + 8 * (tiles - 1)):
                held = None
                for m in range(tiles):
                    k = offset - 8 * m
                    if 0 <= k < taps:
                        if held is None:
                            held = ext[c, pl.ds(r + shift + offset, 8), :]
                        sums[k] = sums[k] + held * grads[m]
            return tuple(sums)

        zero = jnp.zeros((8, LANES), F32)
        sums = lax.fori_loop(0, rows // (8 * tiles), chunk, (zero,) * taps)
        for k in range(taps):
            out_ref[k : k + 1, lanes_of(c)] = jnp.sum(sums[k], axis=0, keepdims=True)


def tap_grad(edge, glu, dconv, taps):
    groups, rows, _ = glu.shape
    channels = groups * LANES
    return pl.pallas_call(
        tap_grad_kernel,
        grid=(channels // BLOCK,),
        in_specs=[
            pl.BlockSpec((SUB, 2 * WIDE, LANES), lambda j: (j, 0, 0)),
            pl.BlockSpec((SUB, rows, LANES), lambda j: (j, 0, 0)),
            pl.BlockSpec((SUB, rows, LANES), lambda j: (j, 0, 0)),
        ],
        out_specs=pl.BlockSpec((taps, BLOCK), lambda j: (0, j)),
        out_shape=jax.ShapeDtypeStruct((taps, channels), F32),
        scratch_shapes=[
            pltpu.VMEM((SUB, rows + 2 * WIDE, LANES), F32),
            pltpu.VMEM((SUB, rows, LANES), F32),
        ],
        compiler_params=pltpu.CompilerParams(vmem_limit_bytes=VMEM_LIMIT),
        cost_estimate=pl.CostEstimate(flops=62 * rows * channels, bytes_accessed=4 * rows * channels, transcendentals=0),
        name="tap_grad",
    )(edge, glu, dconv)


def frames_grad_kernel(dpre_ref, w_ref, out_ref):
    channels = dpre_ref.shape[2]
    total = dot_nt(dpre_ref[0], w_ref[:, :channels]) + dot_nt(dpre_ref[1], w_ref[:, channels:])
    out_ref[...] = total.astype(BF16)


def frames_grad(dpre, w_in):
    _, rows, channels = dpre.shape
    depth = w_in.shape[0]
    return pl.pallas_call(
        frames_grad_kernel,
        grid=(depth // BLOCK,),
        in_specs=[
            pl.BlockSpec((2, rows, channels), lambda j: (0, 0, 0)),
            pl.BlockSpec((BLOCK, 2 * channels), lambda j: (j, 0)),
        ],
        out_specs=pl.BlockSpec((rows, BLOCK), lambda j: (0, j)),
        out_shape=jax.ShapeDtypeStruct((rows, depth), BF16),
        compiler_params=pltpu.CompilerParams(vmem_limit_bytes=VMEM_LIMIT),
        cost_estimate=pl.CostEstimate(
            flops=4 * rows * depth * channels, bytes_accessed=10 * rows * depth, transcendentals=0
        ),
        name="frames_grad",
    )(dpre, w_in)


def weight_kernel(owner_rows, orders, core_ref, left_ref, right_ref, send_ref, keep_ref):
    term = dot_tn(left_ref[...], right_ref[0])
    is_odd = core_ref[0] == 1
    for p, (even, odd) in enumerate(zip(*orders)):
        even = term[even * owner_rows : (even + 1) * owner_rows]
        odd = term[odd * owner_rows : (odd + 1) * owner_rows]
        at = slice(p * owner_rows, (p + 1) * owner_rows)
        send_ref[at, :] = jnp.where(is_odd, even, odd).astype(BF16)
        keep_ref[at, :] = jnp.where(is_odd, odd, even).astype(BF16)


def weight_term(core, left, right, plan):
    halves, rows, width = right.shape
    depth = left.shape[1]
    step = 512
    per = width // step
    out = pl.BlockSpec((depth // 2, step), lambda j: (0, j))
    shape = jax.ShapeDtypeStruct((depth // 2, halves * width), BF16)
    owner_rows = depth // (2 * len(plan.blocks[0]))
    return pl.pallas_call(
        functools.partial(weight_kernel, owner_rows, plan.blocks),
        grid=(halves * per,),
        in_specs=[
            pl.BlockSpec(memory_space=pltpu.SMEM),
            pl.BlockSpec((rows, depth), lambda j: (0, 0)),
            pl.BlockSpec((1, rows, step), lambda j: (j // per, 0, j % per)),
        ],
        out_specs=[out, out],
        out_shape=[shape, shape],
        compiler_params=pltpu.CompilerParams(vmem_limit_bytes=VMEM_LIMIT),
        cost_estimate=pl.CostEstimate(
            flops=2 * halves * rows * depth * width, bytes_accessed=6 * halves * rows * width, transcendentals=0
        ),
        name="weight_term",
    )(core, left, right)


class Halving:
    def __init__(self, dp_count, tm_count):
        near = [1 << i for i in range(1, (tm_count - 1).bit_length())]
        far = [tm_count << i for i in range((dp_count - 1).bit_length())]
        self.count = dp_count * tm_count
        self.masks = (near + far, far[: len(near)] + near + far[len(near) :])
        self.blocks = tuple(
            [self.block(core, masks, p) for p in range(self.count // 2)] for core, masks in enumerate(self.masks)
        )

    def block(self, core, masks, p):
        return core + sum(mask for i, mask in enumerate(masks) if p >> (len(masks) - 1 - i) & 1)

    def perm(self, step):
        if step < 0:
            return [(i, i ^ 1) for i in range(self.count)]
        return [(i, i ^ self.masks[i & 1][step]) for i in range(self.count)]

    def own_half(self, step, place):
        mask = jnp.where(place & 1 == 1, self.masks[1][step], self.masks[0][step])
        return ((place & mask) != 0).astype(jnp.int32)


def combine_kernel(half_ref, keep_other, got_other, keep_mine, got_mine, send_ref, keep_ref):
    send_ref[...] = (keep_other[...].astype(F32) + got_other[...].astype(F32)).astype(BF16)
    keep_ref[...] = (keep_mine[...].astype(F32) + got_mine[...].astype(F32)).astype(BF16)


def combine(half, keep, got):
    rows, width = keep.shape
    step = 512
    other = pl.BlockSpec((rows // 2, step), lambda j, half: (1 - half[0], j))
    mine = pl.BlockSpec((rows // 2, step), lambda j, half: (half[0], j))
    out = pl.BlockSpec((rows // 2, step), lambda j, half: (0, j))
    shape = jax.ShapeDtypeStruct((rows // 2, width), BF16)
    return pl.pallas_call(
        combine_kernel,
        grid_spec=pltpu.PrefetchScalarGridSpec(
            num_scalar_prefetch=1,
            grid=(width // step,),
            in_specs=[other, other, mine, mine],
            out_specs=[out, out],
        ),
        out_shape=[shape, shape],
        compiler_params=pltpu.CompilerParams(vmem_limit_bytes=VMEM_LIMIT),
        cost_estimate=pl.CostEstimate(flops=rows * width, bytes_accessed=6 * rows * width, transcendentals=0),
        name="combine",
    )(half.reshape(1), keep, got, keep, got)


def scatter_sum(plan, place, send, keep):
    everyone = ("dp", "tm")
    got = lax.ppermute(send, everyone, plan.perm(-1))
    steps = len(plan.masks[0])
    for step in range(steps):
        half = plan.own_half(step, place)
        if step == 0:
            send, keep = combine(half, keep, got)
        else:
            both = keep.astype(F32) + got.astype(F32)
            rows = both.shape[0] // 2
            low, high = both[:rows].astype(BF16), both[rows:].astype(BF16)
            send = jnp.where(half == 1, low, high)
            keep = jnp.where(half == 1, high, low)
        got = lax.ppermute(send, everyone, plan.perm(step))
    return keep.astype(F32) + got.astype(F32)


def all_sum(x):
    everyone = ("dp", "tm")
    count = lax.axis_size("dp") * lax.axis_size("tm")
    copies = jnp.broadcast_to(x[None], (count,) + x.shape)
    return jnp.sum(lax.all_to_all(copies, everyone, 0, 0, tiled=True), axis=0)


def butterfly_sum(x):
    for axis in ("tm", "dp"):
        count = lax.axis_size(axis)
        for i in range((count - 1).bit_length()):
            x = x + lax.ppermute(x, axis, [(j, j ^ (1 << i)) for j in range(count)])
    return x


def local(frames, lengths, w_in, w_dw, bn_gain, bn_bias, w_out, cotangent):
    feats, cot = frames[0], cotangent[0]
    rows, depth = feats.shape
    taps = w_dw.shape[0]
    tm_count = lax.axis_size("tm")
    device_count = lax.axis_size("dp") * tm_count
    plan = Halving(lax.axis_size("dp"), tm_count)
    place = lax.axis_index(("dp", "tm"))
    offset = lax.axis_index("tm") * rows
    span = jnp.stack([-offset, lengths[0] - offset]).astype(jnp.int32)
    core = (place & 1).astype(jnp.int32).reshape(1)
    gain, bias = bn_gain[None], bn_bias[None]

    tail = jnp.concatenate([feats[rows - WIDE :], cot[rows - NEAR :]], axis=0)
    head = jnp.concatenate([feats[:WIDE], cot[:NEAR]], axis=0)
    before = lax.ppermute(tail, "tm", [(i, i + 1) for i in range(tm_count - 1)])
    after = lax.ppermute(head, "tm", [(i + 1, i) for i in range(tm_count - 1)])

    glu, first, second = gated(span, feats, w_in)
    conv, edge, sums = convolved(span, before[:WIDE], after[:WIDE], w_in, w_dw, glu)
    sums = all_sum(sums)
    back = back_projected(before[WIDE:], cot, after[WIDE:], w_out)
    swished, dshift, terms = swish(span, sums, gain, bias, conv, back)
    terms = all_sum(terms)
    out_rows = dot_nn(swished, w_out).astype(BF16)
    grad_w_out = scatter_sum(plan, place, *weight_term(core, swished, cotangent, plan))
    dpre, dconv = norm_grad(span, sums, terms, gain, w_dw, conv, dshift, first, second)
    kernel_sum = butterfly_sum(tap_grad(edge, glu, dconv, taps))
    grad_w_in = scatter_sum(plan, place, *weight_term(core, feats, dpre, plan))
    grad_rows = frames_grad(dpre, w_in)
    scale = 1.0 / math.sqrt(device_count * rows)
    return (
        out_rows[None],
        grad_rows[None],
        grad_w_in * scale,
        grad_w_out * scale,
        kernel_sum * scale,
        terms[0] * scale,
        terms[1] * scale,
    )


def solution(mesh):
    placed = (P("dp", "tm", None), P("dp"), P(), P(), P(), P(), P(), P("dp", "tm", None))
    return jax.shard_map(
        local,
        mesh=mesh,
        in_specs=placed,
        out_specs=(
            P("dp", "tm", None),
            P("dp", "tm", None),
            P(("dp", "tm"), None),
            P(("dp", "tm"), None),
            P(),
            P(),
            P(),
        ),
        check_vma=False,
    )
```

```python
import functools
import math

import jax
import jax.numpy as jnp
from jax import lax
from jax.experimental import pallas as pl
from jax.experimental.pallas import tpu as pltpu
from jax.sharding import PartitionSpec as P

F32 = jnp.float32
BF16 = jnp.bfloat16
LANES = 128
BLOCK = 256
SUB = BLOCK // LANES
WIDE = 32
NEAR = 16
VMEM_LIMIT = 56 << 20


def dot_nn(a, b):
    return lax.dot_general(a, b, (((1,), (0,)), ((), ())), preferred_element_type=F32)


def dot_nt(a, b):
    return lax.dot_general(a, b, (((1,), (1,)), ((), ())), preferred_element_type=F32)


def dot_tn(a, b):
    return lax.dot_general(a, b, (((0,), (0,)), ((), ())), preferred_element_type=F32)


def logistic(x):
    return 1.0 / (1.0 + jnp.exp(-x))


def row_mask(start, count, low, high):
    rows = start + lax.broadcasted_iota(jnp.int32, (count, LANES), 0)
    return (rows >= low) & (rows < high)


def taps_chunk(src, c, begin, count, weight_row, taps):
    tiles = count // 8
    sums = [None] * tiles
    for residue in range(8):
        own = list(range(residue, taps, 8))
        weights = [jnp.broadcast_to(weight_row(k), (8, LANES)) for k in own]
        for q in range(tiles + len(own) - 1):
            tile = src[c, pl.ds(begin + residue + 8 * q, 8), :]
            for i, weight in enumerate(weights):
                u = q - i
                if 0 <= u < tiles:
                    term = weight * tile
                    sums[u] = term if sums[u] is None else sums[u] + term
    return sums


def lanes_of(c):
    return slice(c * LANES, (c + 1) * LANES)


def spread(copies_ref, c, lines):
    lines = jnp.concatenate(lines, axis=0)
    copies_ref[:, :, lanes_of(c)] = jnp.broadcast_to(lines[None], (copies_ref.shape[0],) + lines.shape)


def gate_kernel(span_ref, feats_ref, lin_w_ref, gate_w_ref, glu_ref, first_ref, second_ref):
    rows = feats_ref.shape[0]
    step = 256 if rows % 256 == 0 else rows
    for r in range(0, rows, step):
        lin = dot_nn(feats_ref[r : r + step, :], lin_w_ref[...])
        sig = logistic(dot_nn(feats_ref[r : r + step, :], gate_w_ref[...]))
        for c in range(SUB):
            lin_c, sig_c = lin[:, lanes_of(c)], sig[:, lanes_of(c)]
            live = row_mask(r, step, span_ref[0], span_ref[1])
            sig_c = jnp.where(live, sig_c, 0.0)
            prod = lin_c * sig_c
            glu_ref[c, r : r + step, :] = prod.astype(BF16)
            first_ref[r : r + step, lanes_of(c)] = sig_c.astype(BF16)
            second_ref[r : r + step, lanes_of(c)] = (prod * (1.0 - sig_c)).astype(BF16)


def gated(span, feats, w_in):
    rows, depth = feats.shape
    channels = w_in.shape[1] // 2
    blocks = channels // BLOCK
    return pl.pallas_call(
        gate_kernel,
        grid=(blocks,),
        in_specs=[
            pl.BlockSpec(memory_space=pltpu.SMEM),
            pl.BlockSpec((rows, depth), lambda j: (0, 0)),
            pl.BlockSpec((depth, BLOCK), lambda j: (0, j)),
            pl.BlockSpec((depth, BLOCK), lambda j: (0, j + blocks)),
        ],
        out_specs=[
            pl.BlockSpec((SUB, rows, LANES), lambda j: (j, 0, 0)),
            pl.BlockSpec((rows, BLOCK), lambda j: (0, j)),
            pl.BlockSpec((rows, BLOCK), lambda j: (0, j)),
        ],
        out_shape=[
            jax.ShapeDtypeStruct((channels // LANES, rows, LANES), BF16),
            jax.ShapeDtypeStruct((rows, channels), BF16),
            jax.ShapeDtypeStruct((rows, channels), BF16),
        ],
        compiler_params=pltpu.CompilerParams(vmem_limit_bytes=VMEM_LIMIT),
        cost_estimate=pl.CostEstimate(
            flops=4 * rows * depth * channels, bytes_accessed=14 * rows * channels, transcendentals=rows * channels
        ),
        name="gated",
    )(span, feats, w_in, w_in)


def conv_kernel(span_ref, before_ref, after_ref, lin_w_ref, gate_w_ref, taps_ref, glu_ref, conv_ref, edge_ref, sums_ref, ext):
    rows = glu_ref.shape[1]
    taps = taps_ref.shape[0]
    full = rows + 2 * NEAR
    halo = jnp.concatenate([before_ref[...], after_ref[...]], axis=0)
    lin = dot_nn(halo, lin_w_ref[...])
    sig = logistic(dot_nn(halo, gate_w_ref[...]))
    low, high = span_ref[0], span_ref[1]
    live = jnp.concatenate([row_mask(-WIDE, WIDE, low, high), row_mask(rows, WIDE, low, high)], axis=0)
    for c in range(SUB):
        edge = jnp.where(live, lin[:, lanes_of(c)] * sig[:, lanes_of(c)], 0.0).astype(BF16)
        edge_ref[c] = edge
        edge = edge.astype(F32)
        ext[c, 0:WIDE, :] = edge[:WIDE]
        ext[c, WIDE + rows :, :] = edge[WIDE:]
        ext[c, WIDE : WIDE + rows, :] = glu_ref[c].astype(F32)
    count = 160 if full % 160 == 0 else NEAR
    own_low = jnp.maximum(low, 0) + NEAR
    own_high = jnp.minimum(high, rows) + NEAR
    shift = WIDE - NEAR - (taps - 1) // 2
    for c in range(SUB):

        def chunk(i, carry):
            r = pl.multiple_of(i * count, count)
            tiles = taps_chunk(ext, c, r + shift, count, lambda k: taps_ref[k : k + 1, lanes_of(c)], taps)
            total, square = carry
            for u, tile in enumerate(tiles):
                conv_ref[c, pl.ds(r + 8 * u, 8), :] = tile
                kept = jnp.where(row_mask(r + 8 * u, 8, own_low, own_high), tile, 0.0)
                total = total + kept
                square = square + kept * kept
            return total, square

        zero = jnp.zeros((8, LANES), F32)
        total, square = lax.fori_loop(0, full // count, chunk, (zero, zero))
        total = jnp.sum(total, axis=0, keepdims=True)
        square = jnp.sum(square, axis=0, keepdims=True)
        live_rows = jnp.full((1, LANES), 1.0, F32) * jnp.maximum(own_high - own_low, 0).astype(F32)
        spread(sums_ref, c, (total, square, live_rows))


def convolved(span, before, after, w_in, w_dw, glu, devices):
    groups, rows, _ = glu.shape
    channels = groups * LANES
    depth = w_in.shape[0]
    taps = w_dw.shape[0]
    blocks = channels // BLOCK
    full = rows + 2 * NEAR
    return pl.pallas_call(
        conv_kernel,
        grid=(blocks,),
        in_specs=[
            pl.BlockSpec(memory_space=pltpu.SMEM),
            pl.BlockSpec((WIDE, depth), lambda j: (0, 0)),
            pl.BlockSpec((WIDE, depth), lambda j: (0, 0)),
            pl.BlockSpec((depth, BLOCK), lambda j: (0, j)),
            pl.BlockSpec((depth, BLOCK), lambda j: (0, j + blocks)),
            pl.BlockSpec((taps, BLOCK), lambda j: (0, j)),
            pl.BlockSpec((SUB, rows, LANES), lambda j: (j, 0, 0)),
        ],
        out_specs=[
            pl.BlockSpec((SUB, full, LANES), lambda j: (j, 0, 0)),
            pl.BlockSpec((SUB, 2 * WIDE, LANES), lambda j: (j, 0, 0)),
            pl.BlockSpec((devices, 3, BLOCK), lambda j: (0, 0, j)),
        ],
        out_shape=[
            jax.ShapeDtypeStruct((groups, full, LANES), F32),
            jax.ShapeDtypeStruct((groups, 2 * WIDE, LANES), BF16),
            jax.ShapeDtypeStruct((devices, 3, channels), F32),
        ],
        scratch_shapes=[pltpu.VMEM((SUB, rows + 2 * WIDE, LANES), F32)],
        compiler_params=pltpu.CompilerParams(vmem_limit_bytes=VMEM_LIMIT),
        cost_estimate=pl.CostEstimate(
            flops=4 * rows * depth * channels, bytes_accessed=14 * rows * channels, transcendentals=rows * channels
        ),
        name="convolved",
    )(span, before, after, w_in, w_in, w_dw, glu)


def back_kernel(before_ref, own_ref, after_ref, w_ref, out_ref, left):
    rows = own_ref.shape[0]

    @pl.when(pl.program_id(0) == 0)
    def _():
        left[0:NEAR, :] = before_ref[...]
        left[NEAR : NEAR + rows, :] = own_ref[...]
        left[NEAR + rows :, :] = after_ref[...]

    prod = dot_nt(left[...], w_ref[...])
    for c in range(SUB):
        out_ref[c] = prod[:, lanes_of(c)]


def back_projected(before, cot, after, w_out):
    rows, features = cot.shape
    channels = w_out.shape[0]
    full = rows + 2 * NEAR
    return pl.pallas_call(
        back_kernel,
        grid=(channels // BLOCK,),
        in_specs=[
            pl.BlockSpec((NEAR, features), lambda j: (WIDE // NEAR, 0)),
            pl.BlockSpec((rows, features), lambda j: (0, 0)),
            pl.BlockSpec((NEAR, features), lambda j: (WIDE // NEAR, 0)),
            pl.BlockSpec((BLOCK, features), lambda j: (j, 0)),
        ],
        out_specs=pl.BlockSpec((SUB, full, LANES), lambda j: (j, 0, 0)),
        out_shape=jax.ShapeDtypeStruct((channels // LANES, full, LANES), F32),
        scratch_shapes=[pltpu.VMEM((full, features), BF16)],
        compiler_params=pltpu.CompilerParams(vmem_limit_bytes=VMEM_LIMIT),
        cost_estimate=pl.CostEstimate(
            flops=2 * rows * features * channels, bytes_accessed=8 * rows * channels, transcendentals=0
        ),
        name="back_projected",
    )(before, cot, after, w_out)


def moments(sums_ref, c):
    sums = jnp.sum(sums_ref[:, :, lanes_of(c)], axis=0)
    count = sums[2:3]
    mean = sums[0:1] / count
    variance = sums[1:2] / count - mean * mean
    return mean, lax.rsqrt(variance + 1e-05), count


def swish_kernel(span_ref, sums_ref, gain_ref, bias_ref, conv_ref, back_ref, swished_ref, dshift_ref, terms_ref):
    rows = swished_ref.shape[0]
    low, high = span_ref[0], span_ref[1]
    count = 128 if rows % 128 == 0 else NEAR
    for c in range(SUB):
        mean, inv_std, _ = moments(sums_ref, c)
        gain, bias = gain_ref[:, lanes_of(c)], bias_ref[:, lanes_of(c)]

        def piece(r, size):
            at = pl.ds(r, size)
            normed = (conv_ref[c, at, :] - mean) * inv_std
            shifted = gain * normed + bias
            sig = logistic(shifted)
            live = row_mask(r - NEAR, size, low, high)
            swished = jnp.where(live, shifted * sig, 0.0)
            slope = sig + swished * (1.0 - sig)
            dshift = jnp.where(live, back_ref[c, at, :] * slope, 0.0)
            dshift_ref[c, at, :] = dshift
            return normed, swished, dshift

        def chunk(i, carry):
            r = pl.multiple_of(i * count, count)
            normed, swished, dshift = piece(r + NEAR, count)
            swished_ref[pl.ds(r, count), lanes_of(c)] = swished.astype(BF16)
            by_gain, by_bias = carry
            by_gain = by_gain + jnp.sum((dshift * normed).reshape(count // 8, 8, LANES), axis=0)
            by_bias = by_bias + jnp.sum(dshift.reshape(count // 8, 8, LANES), axis=0)
            return by_gain, by_bias

        zero = jnp.zeros((8, LANES), F32)
        by_gain, by_bias = lax.fori_loop(0, rows // count, chunk, (zero, zero))
        piece(0, NEAR)
        piece(rows + NEAR, NEAR)
        by_gain = jnp.sum(by_gain, axis=0, keepdims=True)
        by_bias = jnp.sum(by_bias, axis=0, keepdims=True)
        spread(terms_ref, c, (by_gain, by_bias))


def swish(span, sums, gain, bias, conv, back):
    groups, full, _ = conv.shape
    devices = sums.shape[0]
    rows = full - 2 * NEAR
    channels = groups * LANES
    vector = pl.BlockSpec((1, BLOCK), lambda j: (0, j))
    tall = pl.BlockSpec((SUB, full, LANES), lambda j: (j, 0, 0))
    return pl.pallas_call(
        swish_kernel,
        grid=(channels // BLOCK,),
        in_specs=[
            pl.BlockSpec(memory_space=pltpu.SMEM),
            pl.BlockSpec((devices, 3, BLOCK), lambda j: (0, 0, j)),
            vector,
            vector,
            tall,
            tall,
        ],
        out_specs=[
            pl.BlockSpec((rows, BLOCK), lambda j: (0, j)),
            tall,
            pl.BlockSpec((devices, 2, BLOCK), lambda j: (0, 0, j)),
        ],
        out_shape=[
            jax.ShapeDtypeStruct((rows, channels), BF16),
            jax.ShapeDtypeStruct((groups, full, LANES), F32),
            jax.ShapeDtypeStruct((devices, 2, channels), F32),
        ],
        compiler_params=pltpu.CompilerParams(vmem_limit_bytes=VMEM_LIMIT),
        cost_estimate=pl.CostEstimate(
            flops=30 * rows * channels, bytes_accessed=14 * rows * channels, transcendentals=rows * channels
        ),
        name="swish",
    )(span, sums, gain, bias, conv, back)


def grad_kernel(
    span_ref, sums_ref, terms_ref, gain_ref, taps_ref, conv_ref, dshift_ref, first_ref, second_ref, dpre_ref, dconv_ref, ext
):
    rows = first_ref.shape[0]
    taps = taps_ref.shape[0]
    full = rows + 2 * NEAR
    low, high = span_ref[0], span_ref[1]
    span = 160 if full % 160 == 0 else NEAR
    count = 128 if rows % 128 == 0 else NEAR
    shift = NEAR - (taps - 1) // 2
    for c in range(SUB):
        mean, inv_std, total = moments(sums_ref, c)
        at = lanes_of(c)
        outer = gain_ref[:, at] * inv_std
        terms = jnp.sum(terms_ref[:, :, at], axis=0)
        by_gain = terms[0:1] / total
        by_bias = terms[1:2] / total

        @pl.loop(0, full // span)
        def _(i):
            r = pl.multiple_of(i * span, span)
            normed = (conv_ref[c, pl.ds(r, span), :] - mean) * inv_std
            value = outer * (dshift_ref[c, pl.ds(r, span), :] - by_bias - normed * by_gain)
            live = row_mask(r - NEAR, span, low, high)
            ext[c, pl.ds(r, span), :] = jnp.where(live, value, 0.0).astype(BF16).astype(F32)

        dconv_ref[c] = ext[c, NEAR : NEAR + rows, :].astype(BF16)

        @pl.loop(0, rows // count)
        def _(i):
            r = pl.multiple_of(i * count, count)
            tiles = taps_chunk(ext, c, r + shift, count, lambda k: taps_ref[taps - 1 - k : taps - k, at], taps)
            dglu = jnp.concatenate(tiles, axis=0)
            dpre_ref[0, pl.ds(r, count), at] = (dglu * first_ref[pl.ds(r, count), at].astype(F32)).astype(BF16)
            dpre_ref[1, pl.ds(r, count), at] = (dglu * second_ref[pl.ds(r, count), at].astype(F32)).astype(BF16)


def norm_grad(span, sums, terms, gain, w_dw, conv, dshift, first, second, part, parts):
    groups, full, _ = conv.shape
    devices = sums.shape[0]
    rows = full - 2 * NEAR
    channels = groups * LANES // parts
    taps = w_dw.shape[0]
    blocks = channels // BLOCK
    at = part * blocks
    tall = pl.BlockSpec((SUB, full, LANES), lambda j: (j + at, 0, 0))
    flat = pl.BlockSpec((rows, BLOCK), lambda j: (0, j + at))
    return pl.pallas_call(
        grad_kernel,
        grid=(blocks,),
        in_specs=[
            pl.BlockSpec(memory_space=pltpu.SMEM),
            pl.BlockSpec((devices, 3, BLOCK), lambda j: (0, 0, j + at)),
            pl.BlockSpec((devices, 2, BLOCK), lambda j: (0, 0, j + at)),
            pl.BlockSpec((1, BLOCK), lambda j: (0, j + at)),
            pl.BlockSpec((taps, BLOCK), lambda j: (0, j + at)),
            tall,
            tall,
            flat,
            flat,
        ],
        out_specs=[
            pl.BlockSpec((2, rows, BLOCK), lambda j: (0, 0, j)),
            pl.BlockSpec((SUB, rows, LANES), lambda j: (j, 0, 0)),
        ],
        out_shape=[
            jax.ShapeDtypeStruct((2, rows, channels), BF16),
            jax.ShapeDtypeStruct((channels // LANES, rows, LANES), BF16),
        ],
        scratch_shapes=[pltpu.VMEM((SUB, full, LANES), F32)],
        compiler_params=pltpu.CompilerParams(vmem_limit_bytes=VMEM_LIMIT),
        cost_estimate=pl.CostEstimate(
            flops=70 * rows * channels, bytes_accessed=16 * rows * channels, transcendentals=0
        ),
        name="norm_grad",
    )(span, sums, terms, gain, w_dw, conv, dshift, first, second)


def tap_grad_kernel(edge_ref, glu_ref, dconv_ref, out_ref, ext, own):
    rows = glu_ref.shape[1]
    taps = out_ref.shape[0]
    shift = WIDE - (taps - 1) // 2
    tiles = 4 if rows % 32 == 0 else 2
    for c in range(SUB):
        ext[c, 0:WIDE, :] = edge_ref[c, 0:WIDE, :].astype(F32)
        ext[c, WIDE : WIDE + rows, :] = glu_ref[c].astype(F32)
        ext[c, WIDE + rows :, :] = edge_ref[c, WIDE:, :].astype(F32)
        own[c] = dconv_ref[c].astype(F32)
    for c in range(SUB):

        def chunk(i, carry):
            sums = list(carry)
            r = pl.multiple_of(i * 8 * tiles, 8 * tiles)
            grads = [own[c, pl.ds(r + 8 * m, 8), :] for m in range(tiles)]
            for offset in range(taps + 8 * (tiles - 1)):
                held = None
                for m in range(tiles):
                    k = offset - 8 * m
                    if 0 <= k < taps:
                        if held is None:
                            held = ext[c, pl.ds(r + shift + offset, 8), :]
                        sums[k] = sums[k] + held * grads[m]
            return tuple(sums)

        zero = jnp.zeros((8, LANES), F32)
        sums = lax.fori_loop(0, rows // (8 * tiles), chunk, (zero,) * taps)
        for k in range(taps):
            out_ref[k : k + 1, lanes_of(c)] = jnp.sum(sums[k], axis=0, keepdims=True)


def tap_grad(edge, glu, dconv, taps, part):
    groups, rows, _ = dconv.shape
    channels = groups * LANES
    at = part * (groups // SUB)
    return pl.pallas_call(
        tap_grad_kernel,
        grid=(groups // SUB,),
        in_specs=[
            pl.BlockSpec((SUB, 2 * WIDE, LANES), lambda j: (j + at, 0, 0)),
            pl.BlockSpec((SUB, rows, LANES), lambda j: (j + at, 0, 0)),
            pl.BlockSpec((SUB, rows, LANES), lambda j: (j, 0, 0)),
        ],
        out_specs=pl.BlockSpec((taps, BLOCK), lambda j: (0, j)),
        out_shape=jax.ShapeDtypeStruct((taps, channels), F32),
        scratch_shapes=[
            pltpu.VMEM((SUB, rows + 2 * WIDE, LANES), F32),
            pltpu.VMEM((SUB, rows, LANES), F32),
        ],
        compiler_params=pltpu.CompilerParams(vmem_limit_bytes=VMEM_LIMIT),
        cost_estimate=pl.CostEstimate(flops=62 * rows * channels, bytes_accessed=4 * rows * channels, transcendentals=0),
        name="tap_grad",
    )(edge, glu, dconv)


def frames_grad_kernel(*refs):
    *dpre_refs, w_ref, out_ref = refs
    width = dpre_refs[0].shape[2]
    channels = width * len(dpre_refs)
    total = 0.0
    for i, dpre_ref in enumerate(dpre_refs):
        for half in range(2):
            at = half * channels + i * width
            total = total + dot_nt(dpre_ref[half], w_ref[:, at : at + width])
    out_ref[...] = total.astype(BF16)


def frames_grad(dpre_parts, w_in):
    _, rows, width = dpre_parts[0].shape
    depth, outputs = w_in.shape
    whole = pl.BlockSpec((2, rows, width), lambda j: (0, 0, 0))
    return pl.pallas_call(
        frames_grad_kernel,
        grid=(depth // BLOCK,),
        in_specs=[whole] * len(dpre_parts) + [pl.BlockSpec((BLOCK, outputs), lambda j: (j, 0))],
        out_specs=pl.BlockSpec((rows, BLOCK), lambda j: (0, j)),
        out_shape=jax.ShapeDtypeStruct((rows, depth), BF16),
        compiler_params=pltpu.CompilerParams(vmem_limit_bytes=VMEM_LIMIT),
        cost_estimate=pl.CostEstimate(
            flops=2 * rows * depth * outputs, bytes_accessed=10 * rows * depth, transcendentals=0
        ),
        name="frames_grad",
    )(*dpre_parts, w_in)


def flip_kernel(owner_rows, orders, core_ref, left_ref, mine_ref, other_ref):
    flat = left_ref[...].astype(F32).T
    is_odd = core_ref[0] == 1

    def rows_of(order):
        return jnp.concatenate([flat[p * owner_rows : (p + 1) * owner_rows] for p in order], axis=0).astype(BF16)

    even, odd = rows_of(orders[0]), rows_of(orders[1])
    mine_ref[...] = jnp.where(is_odd, odd, even)
    other_ref[...] = jnp.where(is_odd, even, odd)


def flipped(core, left, plan):
    rows, depth = left.shape
    owner_rows = depth // (2 * len(plan.blocks[0]))
    shape = jax.ShapeDtypeStruct((depth // 2, rows), BF16)
    return pl.pallas_call(
        functools.partial(flip_kernel, owner_rows, plan.blocks),
        in_specs=[pl.BlockSpec(memory_space=pltpu.SMEM), pl.BlockSpec(memory_space=pltpu.VMEM)],
        out_specs=[pl.BlockSpec(memory_space=pltpu.VMEM)] * 2,
        out_shape=[shape, shape],
        compiler_params=pltpu.CompilerParams(vmem_limit_bytes=VMEM_LIMIT),
        cost_estimate=pl.CostEstimate(flops=4 * rows * depth, bytes_accessed=4 * rows * depth, transcendentals=0),
        name="flipped",
    )(core, left)


def pair_kernel(half_ref, left_own, left_got, *refs):
    *right_refs, send_ref, keep_ref = refs
    j = pl.program_id(0)
    rows = send_ref.shape[0]
    for part in range(len(right_refs) // 2):

        @pl.when(j // 2 == part)
        def _(own=right_refs[2 * part], got=right_refs[2 * part + 1]):
            term = dot_nn(left_own[...], own[0]) + dot_nn(left_got[...], got[0])
            low, high = term[:rows], term[rows:]
            upper = half_ref[0] == 1
            send_ref[...] = jnp.where(upper, low, high).astype(BF16)
            keep_ref[...] = jnp.where(upper, high, low).astype(BF16)


def pair_term(half, left_own, left_got, right_own, right_got):
    parts = len(right_own)
    _, rows, width = right_own[0].shape
    depth = left_own.shape[0]
    left = pl.BlockSpec((depth, rows), lambda j: (0, 0))
    out = pl.BlockSpec((depth // 2, width), lambda j: (0, (j % 2) * parts + j // 2))
    shape = jax.ShapeDtypeStruct((depth // 2, 2 * parts * width), BF16)
    rights, specs = [], []
    for part in range(parts):
        rights += [right_own[part], right_got[part]]
        specs += [pl.BlockSpec((1, rows, width), lambda j, part=part: (jnp.clip(j - 2 * part, 0, 1), 0, 0))] * 2
    return pl.pallas_call(
        pair_kernel,
        grid=(2 * parts,),
        in_specs=[pl.BlockSpec(memory_space=pltpu.SMEM), left, left] + specs,
        out_specs=[out, out],
        out_shape=[shape, shape],
        compiler_params=pltpu.CompilerParams(vmem_limit_bytes=VMEM_LIMIT),
        cost_estimate=pl.CostEstimate(
            flops=8 * parts * rows * depth * width, bytes_accessed=16 * parts * rows * width, transcendentals=0
        ),
        name="pair_term",
    )(half.reshape(1), left_own, left_got, *rights)


def weight_kernel(owner_rows, orders, core_ref, left_ref, right_ref, send_ref, keep_ref):
    term = dot_tn(left_ref[...], right_ref[0])
    is_odd = core_ref[0] == 1
    send, keep = [], []
    for p, (even, odd) in enumerate(zip(*orders)):
        even = term[even * owner_rows : (even + 1) * owner_rows]
        odd = term[odd * owner_rows : (odd + 1) * owner_rows]
        send.append(jnp.where(is_odd, even, odd))
        keep.append(jnp.where(is_odd, odd, even))
    send_ref[...] = jnp.concatenate(send, axis=0).astype(BF16)
    keep_ref[...] = jnp.concatenate(keep, axis=0).astype(BF16)


def weight_term(core, left, right, plan):
    halves, rows, width = right.shape
    depth = left.shape[1]
    step = 512
    per = width // step
    out = pl.BlockSpec((depth // 2, step), lambda j: (0, j))
    shape = jax.ShapeDtypeStruct((depth // 2, halves * width), BF16)
    owner_rows = depth // (2 * len(plan.blocks[0]))
    return pl.pallas_call(
        functools.partial(weight_kernel, owner_rows, plan.blocks),
        grid=(halves * per,),
        in_specs=[
            pl.BlockSpec(memory_space=pltpu.SMEM),
            pl.BlockSpec((rows, depth), lambda j: (0, 0)),
            pl.BlockSpec((1, rows, step), lambda j: (j // per, 0, j % per)),
        ],
        out_specs=[out, out],
        out_shape=[shape, shape],
        compiler_params=pltpu.CompilerParams(vmem_limit_bytes=VMEM_LIMIT),
        cost_estimate=pl.CostEstimate(
            flops=2 * halves * rows * depth * width, bytes_accessed=6 * halves * rows * width, transcendentals=0
        ),
        name="weight_term",
    )(core, left, right)


class Halving:
    def __init__(self, dp_count, tm_count):
        near = [1 << i for i in range(1, (tm_count - 1).bit_length())]
        far = [tm_count << i for i in range((dp_count - 1).bit_length())]
        self.count = dp_count * tm_count
        self.masks = (near + far, far[: len(near)] + near + far[len(near) :])
        self.blocks = tuple(
            [self.block(core, masks, p) for p in range(self.count // 2)] for core, masks in enumerate(self.masks)
        )

    def block(self, core, masks, p):
        return core + sum(mask for i, mask in enumerate(masks) if p >> (len(masks) - 1 - i) & 1)

    def perm(self, step):
        if step < 0:
            return [(i, i ^ 1) for i in range(self.count)]
        return [(i, i ^ self.masks[i & 1][step]) for i in range(self.count)]

    def own_half(self, step, place):
        mask = jnp.where(place & 1 == 1, self.masks[1][step], self.masks[0][step])
        return ((place & mask) != 0).astype(jnp.int32)


def combine_kernel(half_ref, keep_other, got_other, keep_mine, got_mine, send_ref, keep_ref):
    send_ref[...] = (keep_other[...].astype(F32) + got_other[...].astype(F32)).astype(BF16)
    keep_ref[...] = (keep_mine[...].astype(F32) + got_mine[...].astype(F32)).astype(BF16)


def combine(half, keep, got):
    rows, width = keep.shape
    step = 512
    other = pl.BlockSpec((rows // 2, step), lambda j, half: (1 - half[0], j))
    mine = pl.BlockSpec((rows // 2, step), lambda j, half: (half[0], j))
    out = pl.BlockSpec((rows // 2, step), lambda j, half: (0, j))
    shape = jax.ShapeDtypeStruct((rows // 2, width), BF16)
    return pl.pallas_call(
        combine_kernel,
        grid_spec=pltpu.PrefetchScalarGridSpec(
            num_scalar_prefetch=1,
            grid=(width // step,),
            in_specs=[other, other, mine, mine],
            out_specs=[out, out],
        ),
        out_shape=[shape, shape],
        compiler_params=pltpu.CompilerParams(vmem_limit_bytes=VMEM_LIMIT),
        cost_estimate=pl.CostEstimate(flops=rows * width, bytes_accessed=6 * rows * width, transcendentals=0),
        name="combine",
    )(half.reshape(1), keep, got, keep, got)


def scatter_rest(plan, place, send, keep):
    everyone = ("dp", "tm")
    got = lax.ppermute(send, everyone, plan.perm(0))
    for step in range(1, len(plan.masks[0])):
        half = plan.own_half(step, place)
        both = keep.astype(F32) + got.astype(F32)
        rows = both.shape[0] // 2
        low, high = both[:rows].astype(BF16), both[rows:].astype(BF16)
        send = jnp.where(half == 1, low, high)
        keep = jnp.where(half == 1, high, low)
        got = lax.ppermute(send, everyone, plan.perm(step))
    return keep.astype(F32) + got.astype(F32)


def from_all(copies):
    return lax.all_to_all(copies, ("dp", "tm"), 0, 0, tiled=True)


def butterfly_sum(x):
    for axis in ("tm", "dp"):
        count = lax.axis_size(axis)
        for i in range((count - 1).bit_length()):
            x = x + lax.ppermute(x, axis, [(j, j ^ (1 << i)) for j in range(count)])
    return x


def local(frames, lengths, w_in, w_dw, bn_gain, bn_bias, w_out, cotangent):
    feats, cot = frames[0], cotangent[0]
    rows, depth = feats.shape
    taps = w_dw.shape[0]
    tm_count = lax.axis_size("tm")
    device_count = lax.axis_size("dp") * tm_count
    plan = Halving(lax.axis_size("dp"), tm_count)
    place = lax.axis_index(("dp", "tm"))
    offset = lax.axis_index("tm") * rows
    span = jnp.stack([-offset, lengths[0] - offset]).astype(jnp.int32)
    core = (place & 1).astype(jnp.int32).reshape(1)
    gain, bias = bn_gain[None], bn_bias[None]

    everyone = ("dp", "tm")
    tail = jnp.concatenate([feats[rows - WIDE :], cot[rows - NEAR :]], axis=0)
    head = jnp.concatenate([feats[:WIDE], cot[:NEAR]], axis=0)
    before = lax.ppermute(tail, "tm", [(i, i + 1) for i in range(tm_count - 1)])
    after = lax.ppermute(head, "tm", [(i + 1, i) for i in range(tm_count - 1)])

    glu, first, second = gated(span, feats, w_in)
    conv, edge, sums = convolved(span, before, after, w_in, w_dw, glu, device_count)
    sums = from_all(sums)
    back = back_projected(before, cot, after, w_out)
    left_own, left_other = flipped(core, feats, plan)
    sums, back, left_other = lax.optimization_barrier((sums, back, left_other))
    left_got = lax.ppermute(left_other, everyone, plan.perm(-1))

    swished, dshift, terms = swish(span, sums, gain, bias, conv, back)
    terms = from_all(terms)
    out_rows = dot_nn(swished, w_out).astype(BF16)
    out_send, out_keep = weight_term(core, swished, cotangent, plan)
    terms, out_rows, out_send = lax.optimization_barrier((terms, out_rows, out_send))
    out_got = lax.ppermute(out_send, everyone, plan.perm(-1))

    first_half = plan.own_half(0, place)
    parts = 2
    dpre_own, dpre_got, taps_sum = [], [], []
    for part in range(parts):
        dpre, dconv = norm_grad(span, sums, terms, gain, w_dw, conv, dshift, first, second, part, parts)
        dpre_own.append(dpre)
        dpre_got.append(lax.ppermute(dpre, everyone, plan.perm(-1)))
        taps_sum.append(tap_grad(edge, glu, dconv, taps, part))
    kernel_sum = butterfly_sum(jnp.concatenate(taps_sum, axis=1))
    grad_w_out = scatter_rest(plan, place, *combine(first_half, out_keep, out_got))
    grad_w_in = scatter_rest(plan, place, *pair_term(first_half, left_own, left_got, dpre_own, dpre_got))
    grad_rows = frames_grad(dpre_own, w_in)
    by_gain, by_bias = jnp.sum(terms, axis=0)
    scale = 1.0 / math.sqrt(device_count * rows)
    return (
        out_rows[None],
        grad_rows[None],
        grad_w_in * scale,
        grad_w_out * scale,
        kernel_sum * scale,
        by_gain * scale,
        by_bias * scale,
    )


def solution(mesh):
    placed = (P("dp", "tm", None), P("dp"), P(), P(), P(), P(), P(), P("dp", "tm", None))
    return jax.shard_map(
        local,
        mesh=mesh,
        in_specs=placed,
        out_specs=(
            P("dp", "tm", None),
            P("dp", "tm", None),
            P(("dp", "tm"), None),
            P(("dp", "tm"), None),
            P(),
            P(),
            P(),
        ),
        check_vma=False,
    )
```

```python
import functools
import math

import jax
import jax.numpy as jnp
from jax import lax
from jax.experimental import pallas as pl
from jax.experimental.pallas import tpu as pltpu
from jax.sharding import PartitionSpec as P

F32 = jnp.float32
BF16 = jnp.bfloat16
LANES = 128
BLOCK = 256
SUB = BLOCK // LANES
WIDE = 32
NEAR = 16
VMEM_LIMIT = 56 << 20


def dot_nn(a, b):
    return lax.dot_general(a, b, (((1,), (0,)), ((), ())), preferred_element_type=F32)


def dot_nt(a, b):
    return lax.dot_general(a, b, (((1,), (1,)), ((), ())), preferred_element_type=F32)


def dot_tn(a, b):
    return lax.dot_general(a, b, (((0,), (0,)), ((), ())), preferred_element_type=F32)


def logistic(x):
    return 1.0 / (1.0 + jnp.exp(-x))


def row_mask(start, count, low, high):
    rows = start + lax.broadcasted_iota(jnp.int32, (count, LANES), 0)
    return (rows >= low) & (rows < high)


def taps_chunk(src, c, begin, count, weight_row, taps):
    tiles = count // 8
    sums = [None] * tiles
    for residue in range(8):
        own = list(range(residue, taps, 8))
        weights = [jnp.broadcast_to(weight_row(k), (8, LANES)) for k in own]
        for q in range(tiles + len(own) - 1):
            tile = src[c, pl.ds(begin + residue + 8 * q, 8), :]
            for i, weight in enumerate(weights):
                u = q - i
                if 0 <= u < tiles:
                    term = weight * tile
                    sums[u] = term if sums[u] is None else sums[u] + term
    return sums


def lanes_of(c):
    return slice(c * LANES, (c + 1) * LANES)


def spread(copies_ref, c, lines):
    lines = jnp.concatenate(lines, axis=0)
    copies_ref[:, :, lanes_of(c)] = jnp.broadcast_to(lines[None], (copies_ref.shape[0],) + lines.shape)


def gate_kernel(span_ref, feats_ref, lin_w_ref, gate_w_ref, glu_ref, first_ref, second_ref):
    rows = feats_ref.shape[0]
    step = 256 if rows % 256 == 0 else rows
    for r in range(0, rows, step):
        lin = dot_nn(feats_ref[r : r + step, :], lin_w_ref[...])
        sig = logistic(dot_nn(feats_ref[r : r + step, :], gate_w_ref[...]))
        for c in range(SUB):
            lin_c, sig_c = lin[:, lanes_of(c)], sig[:, lanes_of(c)]
            live = row_mask(r, step, span_ref[0], span_ref[1])
            sig_c = jnp.where(live, sig_c, 0.0)
            prod = lin_c * sig_c
            glu_ref[c, r : r + step, :] = prod.astype(BF16)
            first_ref[r : r + step, lanes_of(c)] = sig_c.astype(BF16)
            second_ref[r : r + step, lanes_of(c)] = (prod * (1.0 - sig_c)).astype(BF16)


def gated(span, feats, w_in):
    rows, depth = feats.shape
    channels = w_in.shape[1] // 2
    blocks = channels // BLOCK
    return pl.pallas_call(
        gate_kernel,
        grid=(blocks,),
        in_specs=[
            pl.BlockSpec(memory_space=pltpu.SMEM),
            pl.BlockSpec((rows, depth), lambda j: (0, 0)),
            pl.BlockSpec((depth, BLOCK), lambda j: (0, j)),
            pl.BlockSpec((depth, BLOCK), lambda j: (0, j + blocks)),
        ],
        out_specs=[
            pl.BlockSpec((SUB, rows, LANES), lambda j: (j, 0, 0)),
            pl.BlockSpec((rows, BLOCK), lambda j: (0, j)),
            pl.BlockSpec((rows, BLOCK), lambda j: (0, j)),
        ],
        out_shape=[
            jax.ShapeDtypeStruct((channels // LANES, rows, LANES), BF16),
            jax.ShapeDtypeStruct((rows, channels), BF16),
            jax.ShapeDtypeStruct((rows, channels), BF16),
        ],
        compiler_params=pltpu.CompilerParams(vmem_limit_bytes=VMEM_LIMIT),
        cost_estimate=pl.CostEstimate(
            flops=4 * rows * depth * channels, bytes_accessed=14 * rows * channels, transcendentals=rows * channels
        ),
        name="gated",
    )(span, feats, w_in, w_in)


def conv_kernel(span_ref, before_ref, after_ref, lin_w_ref, gate_w_ref, taps_ref, glu_ref, conv_ref, edge_ref, sums_ref, ext):
    rows = glu_ref.shape[1]
    taps = taps_ref.shape[0]
    full = rows + 2 * NEAR
    halo = jnp.concatenate([before_ref[...], after_ref[...]], axis=0)
    lin = dot_nn(halo, lin_w_ref[...])
    sig = logistic(dot_nn(halo, gate_w_ref[...]))
    low, high = span_ref[0], span_ref[1]
    live = jnp.concatenate([row_mask(-WIDE, WIDE, low, high), row_mask(rows, WIDE, low, high)], axis=0)
    for c in range(SUB):
        edge = jnp.where(live, lin[:, lanes_of(c)] * sig[:, lanes_of(c)], 0.0).astype(BF16)
        edge_ref[c] = edge
        edge = edge.astype(F32)
        ext[c, 0:WIDE, :] = edge[:WIDE]
        ext[c, WIDE + rows :, :] = edge[WIDE:]
        ext[c, WIDE : WIDE + rows, :] = glu_ref[c].astype(F32)
    count = 160 if full % 160 == 0 else NEAR
    own_low = jnp.maximum(low, 0) + NEAR
    own_high = jnp.minimum(high, rows) + NEAR
    shift = WIDE - NEAR - (taps - 1) // 2
    for c in range(SUB):

        def chunk(i, carry):
            r = pl.multiple_of(i * count, count)
            tiles = taps_chunk(ext, c, r + shift, count, lambda k: taps_ref[k : k + 1, lanes_of(c)], taps)
            total, square = carry
            for u, tile in enumerate(tiles):
                conv_ref[c, pl.ds(r + 8 * u, 8), :] = tile
                kept = jnp.where(row_mask(r + 8 * u, 8, own_low, own_high), tile, 0.0)
                total = total + kept
                square = square + kept * kept
            return total, square

        zero = jnp.zeros((8, LANES), F32)
        total, square = lax.fori_loop(0, full // count, chunk, (zero, zero))
        total = jnp.sum(total, axis=0, keepdims=True)
        square = jnp.sum(square, axis=0, keepdims=True)
        live_rows = jnp.full((1, LANES), 1.0, F32) * jnp.maximum(own_high - own_low, 0).astype(F32)
        spread(sums_ref, c, (total, square, live_rows))


def convolved(span, before, after, w_in, w_dw, glu, devices):
    groups, rows, _ = glu.shape
    channels = groups * LANES
    depth = w_in.shape[0]
    taps = w_dw.shape[0]
    blocks = channels // BLOCK
    full = rows + 2 * NEAR
    return pl.pallas_call(
        conv_kernel,
        grid=(blocks,),
        in_specs=[
            pl.BlockSpec(memory_space=pltpu.SMEM),
            pl.BlockSpec((WIDE, depth), lambda j: (0, 0)),
            pl.BlockSpec((WIDE, depth), lambda j: (0, 0)),
            pl.BlockSpec((depth, BLOCK), lambda j: (0, j)),
            pl.BlockSpec((depth, BLOCK), lambda j: (0, j + blocks)),
            pl.BlockSpec((taps, BLOCK), lambda j: (0, j)),
            pl.BlockSpec((SUB, rows, LANES), lambda j: (j, 0, 0)),
        ],
        out_specs=[
            pl.BlockSpec((SUB, full, LANES), lambda j: (j, 0, 0)),
            pl.BlockSpec((SUB, 2 * WIDE, LANES), lambda j: (j, 0, 0)),
            pl.BlockSpec((devices, 3, BLOCK), lambda j: (0, 0, j)),
        ],
        out_shape=[
            jax.ShapeDtypeStruct((groups, full, LANES), F32),
            jax.ShapeDtypeStruct((groups, 2 * WIDE, LANES), BF16),
            jax.ShapeDtypeStruct((devices, 3, channels), F32),
        ],
        scratch_shapes=[pltpu.VMEM((SUB, rows + 2 * WIDE, LANES), F32)],
        compiler_params=pltpu.CompilerParams(vmem_limit_bytes=VMEM_LIMIT),
        cost_estimate=pl.CostEstimate(
            flops=4 * rows * depth * channels, bytes_accessed=14 * rows * channels, transcendentals=rows * channels
        ),
        name="convolved",
    )(span, before, after, w_in, w_in, w_dw, glu)


def back_kernel(before_ref, own_ref, after_ref, w_ref, out_ref, left):
    rows = own_ref.shape[0]

    @pl.when(pl.program_id(0) == 0)
    def _():
        left[0:NEAR, :] = before_ref[...]
        left[NEAR : NEAR + rows, :] = own_ref[...]
        left[NEAR + rows :, :] = after_ref[...]

    prod = dot_nt(left[...], w_ref[...])
    for c in range(SUB):
        out_ref[c] = prod[:, lanes_of(c)].astype(BF16)


def back_projected(before, cot, after, w_out):
    rows, features = cot.shape
    channels = w_out.shape[0]
    full = rows + 2 * NEAR
    return pl.pallas_call(
        back_kernel,
        grid=(channels // BLOCK,),
        in_specs=[
            pl.BlockSpec((NEAR, features), lambda j: (WIDE // NEAR, 0)),
            pl.BlockSpec((rows, features), lambda j: (0, 0)),
            pl.BlockSpec((NEAR, features), lambda j: (WIDE // NEAR, 0)),
            pl.BlockSpec((BLOCK, features), lambda j: (j, 0)),
        ],
        out_specs=pl.BlockSpec((SUB, full, LANES), lambda j: (j, 0, 0)),
        out_shape=jax.ShapeDtypeStruct((channels // LANES, full, LANES), BF16),
        scratch_shapes=[pltpu.VMEM((full, features), BF16)],
        compiler_params=pltpu.CompilerParams(vmem_limit_bytes=VMEM_LIMIT),
        cost_estimate=pl.CostEstimate(
            flops=2 * rows * features * channels, bytes_accessed=8 * rows * channels, transcendentals=0
        ),
        name="back_projected",
    )(before, cot, after, w_out)


def moments(sums_ref, c):
    sums = jnp.sum(sums_ref[:, :, lanes_of(c)], axis=0)
    count = sums[2:3]
    mean = sums[0:1] / count
    variance = sums[1:2] / count - mean * mean
    return mean, lax.rsqrt(variance + 1e-05), count


def swish_kernel(span_ref, sums_ref, gain_ref, bias_ref, conv_ref, back_ref, swished_ref, dshift_ref, terms_ref):
    rows = swished_ref.shape[0]
    low, high = span_ref[0], span_ref[1]
    count = 128 if rows % 128 == 0 else NEAR
    for c in range(SUB):
        mean, inv_std, _ = moments(sums_ref, c)
        gain, bias = gain_ref[:, lanes_of(c)], bias_ref[:, lanes_of(c)]

        def piece(r, size):
            at = pl.ds(r, size)
            normed = (conv_ref[c, at, :] - mean) * inv_std
            shifted = gain * normed + bias
            sig = logistic(shifted)
            live = row_mask(r - NEAR, size, low, high)
            swished = jnp.where(live, shifted * sig, 0.0)
            slope = sig + swished * (1.0 - sig)
            dshift = jnp.where(live, back_ref[c, at, :].astype(F32) * slope, 0.0)
            dshift_ref[c, at, :] = dshift.astype(BF16)
            return normed, swished, dshift

        def chunk(i, carry):
            r = pl.multiple_of(i * count, count)
            normed, swished, dshift = piece(r + NEAR, count)
            swished_ref[pl.ds(r, count), lanes_of(c)] = swished.astype(BF16)
            by_gain, by_bias = carry
            by_gain = by_gain + jnp.sum((dshift * normed).reshape(count // 8, 8, LANES), axis=0)
            by_bias = by_bias + jnp.sum(dshift.reshape(count // 8, 8, LANES), axis=0)
            return by_gain, by_bias

        zero = jnp.zeros((8, LANES), F32)
        by_gain, by_bias = lax.fori_loop(0, rows // count, chunk, (zero, zero))
        piece(0, NEAR)
        piece(rows + NEAR, NEAR)
        by_gain = jnp.sum(by_gain, axis=0, keepdims=True)
        by_bias = jnp.sum(by_bias, axis=0, keepdims=True)
        spread(terms_ref, c, (by_gain, by_bias))


def swish(span, sums, gain, bias, conv, back):
    groups, full, _ = conv.shape
    devices = sums.shape[0]
    rows = full - 2 * NEAR
    channels = groups * LANES
    vector = pl.BlockSpec((1, BLOCK), lambda j: (0, j))
    tall = pl.BlockSpec((SUB, full, LANES), lambda j: (j, 0, 0))
    return pl.pallas_call(
        swish_kernel,
        grid=(channels // BLOCK,),
        in_specs=[
            pl.BlockSpec(memory_space=pltpu.SMEM),
            pl.BlockSpec((devices, 3, BLOCK), lambda j: (0, 0, j)),
            vector,
            vector,
            tall,
            tall,
        ],
        out_specs=[
            pl.BlockSpec((rows, BLOCK), lambda j: (0, j)),
            tall,
            pl.BlockSpec((devices, 2, BLOCK), lambda j: (0, 0, j)),
        ],
        out_shape=[
            jax.ShapeDtypeStruct((rows, channels), BF16),
            jax.ShapeDtypeStruct((groups, full, LANES), BF16),
            jax.ShapeDtypeStruct((devices, 2, channels), F32),
        ],
        compiler_params=pltpu.CompilerParams(vmem_limit_bytes=VMEM_LIMIT),
        cost_estimate=pl.CostEstimate(
            flops=30 * rows * channels, bytes_accessed=14 * rows * channels, transcendentals=rows * channels
        ),
        name="swish",
    )(span, sums, gain, bias, conv, back)


def grad_kernel(
    span_ref, sums_ref, terms_ref, gain_ref, taps_ref, conv_ref, dshift_ref, first_ref, second_ref, dpre_ref, dconv_ref, ext
):
    rows = first_ref.shape[0]
    taps = taps_ref.shape[0]
    full = rows + 2 * NEAR
    low, high = span_ref[0], span_ref[1]
    span = 160 if full % 160 == 0 else NEAR
    count = 128 if rows % 128 == 0 else NEAR
    shift = NEAR - (taps - 1) // 2
    for c in range(SUB):
        mean, inv_std, total = moments(sums_ref, c)
        at = lanes_of(c)
        outer = gain_ref[:, at] * inv_std
        terms = jnp.sum(terms_ref[:, :, at], axis=0)
        by_gain = terms[0:1] / total
        by_bias = terms[1:2] / total

        @pl.loop(0, full // span)
        def _(i):
            r = pl.multiple_of(i * span, span)
            normed = (conv_ref[c, pl.ds(r, span), :] - mean) * inv_std
            value = outer * (dshift_ref[c, pl.ds(r, span), :].astype(F32) - by_bias - normed * by_gain)
            live = row_mask(r - NEAR, span, low, high)
            ext[c, pl.ds(r, span), :] = jnp.where(live, value, 0.0).astype(BF16).astype(F32)

        dconv_ref[c] = ext[c, NEAR : NEAR + rows, :].astype(BF16)

        @pl.loop(0, rows // count)
        def _(i):
            r = pl.multiple_of(i * count, count)
            tiles = taps_chunk(ext, c, r + shift, count, lambda k: taps_ref[taps - 1 - k : taps - k, at], taps)
            dglu = jnp.concatenate(tiles, axis=0)
            dpre_ref[0, pl.ds(r, count), at] = (dglu * first_ref[pl.ds(r, count), at].astype(F32)).astype(BF16)
            dpre_ref[1, pl.ds(r, count), at] = (dglu * second_ref[pl.ds(r, count), at].astype(F32)).astype(BF16)


def norm_grad(span, sums, terms, gain, w_dw, conv, dshift, first, second, part, parts):
    groups, full, _ = conv.shape
    devices = sums.shape[0]
    rows = full - 2 * NEAR
    channels = groups * LANES // parts
    taps = w_dw.shape[0]
    blocks = channels // BLOCK
    at = part * blocks
    tall = pl.BlockSpec((SUB, full, LANES), lambda j: (j + at, 0, 0))
    flat = pl.BlockSpec((rows, BLOCK), lambda j: (0, j + at))
    return pl.pallas_call(
        grad_kernel,
        grid=(blocks,),
        in_specs=[
            pl.BlockSpec(memory_space=pltpu.SMEM),
            pl.BlockSpec((devices, 3, BLOCK), lambda j: (0, 0, j + at)),
            pl.BlockSpec((devices, 2, BLOCK), lambda j: (0, 0, j + at)),
            pl.BlockSpec((1, BLOCK), lambda j: (0, j + at)),
            pl.BlockSpec((taps, BLOCK), lambda j: (0, j + at)),
            tall,
            tall,
            flat,
            flat,
        ],
        out_specs=[
            pl.BlockSpec((2, rows, BLOCK), lambda j: (0, 0, j)),
            pl.BlockSpec((SUB, rows, LANES), lambda j: (j, 0, 0)),
        ],
        out_shape=[
            jax.ShapeDtypeStruct((2, rows, channels), BF16),
            jax.ShapeDtypeStruct((channels // LANES, rows, LANES), BF16),
        ],
        scratch_shapes=[pltpu.VMEM((SUB, full, LANES), F32)],
        compiler_params=pltpu.CompilerParams(vmem_limit_bytes=VMEM_LIMIT),
        cost_estimate=pl.CostEstimate(
            flops=70 * rows * channels, bytes_accessed=16 * rows * channels, transcendentals=0
        ),
        name="norm_grad",
    )(span, sums, terms, gain, w_dw, conv, dshift, first, second)


def tap_grad_kernel(taps, edge_ref, glu_ref, *refs):
    *dconv_refs, out_ref, ext, own = refs
    rows = glu_ref.shape[1]
    shift = WIDE - (taps - 1) // 2
    tiles = 4 if rows % 32 == 0 else 2
    per = pl.num_programs(0) // len(dconv_refs)
    for part, dconv_ref in enumerate(dconv_refs):

        @pl.when(pl.program_id(0) // per == part)
        def _(dconv_ref=dconv_ref):
            for c in range(SUB):
                own[c] = dconv_ref[c].astype(F32)

    for c in range(SUB):
        ext[c, 0:WIDE, :] = edge_ref[c, 0:WIDE, :].astype(F32)
        ext[c, WIDE : WIDE + rows, :] = glu_ref[c].astype(F32)
        ext[c, WIDE + rows :, :] = edge_ref[c, WIDE:, :].astype(F32)
    for c in range(SUB):

        def chunk(i, carry):
            sums = list(carry)
            r = pl.multiple_of(i * 8 * tiles, 8 * tiles)
            grads = [own[c, pl.ds(r + 8 * m, 8), :] for m in range(tiles)]
            for offset in range(taps + 8 * (tiles - 1)):
                held = None
                for m in range(tiles):
                    k = offset - 8 * m
                    if 0 <= k < taps:
                        if held is None:
                            held = ext[c, pl.ds(r + shift + offset, 8), :]
                        sums[k] = sums[k] + held * grads[m]
            return tuple(sums)

        zero = jnp.zeros((8, LANES), F32)
        sums = lax.fori_loop(0, rows // (8 * tiles), chunk, (zero,) * taps)
        out_ref[c] = jnp.zeros(out_ref.shape[1:], F32)
        for k in range(taps):
            out_ref[c, k : k + 1, :] = jnp.sum(sums[k], axis=0, keepdims=True)


def tap_grad(edge, glu, dconv_parts, taps):
    groups, rows, _ = glu.shape
    steps = groups // SUB
    per = steps // len(dconv_parts)
    padded = -(-taps // 8) * 8
    specs = [
        pl.BlockSpec((SUB, rows, LANES), lambda j, part=part: (jnp.clip(j - part * per, 0, per - 1), 0, 0))
        for part in range(len(dconv_parts))
    ]
    return pl.pallas_call(
        functools.partial(tap_grad_kernel, taps),
        grid=(steps,),
        in_specs=[
            pl.BlockSpec((SUB, 2 * WIDE, LANES), lambda j: (j, 0, 0)),
            pl.BlockSpec((SUB, rows, LANES), lambda j: (j, 0, 0)),
            *specs,
        ],
        out_specs=pl.BlockSpec((SUB, padded, LANES), lambda j: (j, 0, 0)),
        out_shape=jax.ShapeDtypeStruct((groups, padded, LANES), F32),
        scratch_shapes=[
            pltpu.VMEM((SUB, rows + 2 * WIDE, LANES), F32),
            pltpu.VMEM((SUB, rows, LANES), F32),
        ],
        compiler_params=pltpu.CompilerParams(vmem_limit_bytes=VMEM_LIMIT),
        cost_estimate=pl.CostEstimate(
            flops=62 * rows * groups * LANES, bytes_accessed=4 * rows * groups * LANES, transcendentals=0
        ),
        name="tap_grad",
    )(edge, glu, *dconv_parts)


def frames_grad_kernel(*refs):
    *dpre_refs, w_ref, out_ref = refs
    width = dpre_refs[0].shape[2]
    channels = width * len(dpre_refs)
    total = 0.0
    for i, dpre_ref in enumerate(dpre_refs):
        for half in range(2):
            at = half * channels + i * width
            total = total + dot_nt(dpre_ref[half], w_ref[:, at : at + width])
    out_ref[...] = total.astype(BF16)


def frames_grad(dpre_parts, w_in):
    _, rows, width = dpre_parts[0].shape
    depth, outputs = w_in.shape
    whole = pl.BlockSpec((2, rows, width), lambda j: (0, 0, 0))
    return pl.pallas_call(
        frames_grad_kernel,
        grid=(depth // BLOCK,),
        in_specs=[whole] * len(dpre_parts) + [pl.BlockSpec((BLOCK, outputs), lambda j: (j, 0))],
        out_specs=pl.BlockSpec((rows, BLOCK), lambda j: (0, j)),
        out_shape=jax.ShapeDtypeStruct((rows, depth), BF16),
        compiler_params=pltpu.CompilerParams(vmem_limit_bytes=VMEM_LIMIT),
        cost_estimate=pl.CostEstimate(
            flops=2 * rows * depth * outputs, bytes_accessed=10 * rows * depth, transcendentals=0
        ),
        name="frames_grad",
    )(*dpre_parts, w_in)


def flip_kernel(owner_rows, orders, core_ref, left_ref, mine_ref, other_ref):
    flat = left_ref[...].astype(F32).T
    is_odd = core_ref[0] == 1

    def rows_of(order):
        return jnp.concatenate([flat[p * owner_rows : (p + 1) * owner_rows] for p in order], axis=0).astype(BF16)

    even, odd = rows_of(orders[0]), rows_of(orders[1])
    mine_ref[...] = jnp.where(is_odd, odd, even)
    other_ref[...] = jnp.where(is_odd, even, odd)


def flipped(core, left, plan):
    rows, depth = left.shape
    owner_rows = depth // (2 * len(plan.blocks[0]))
    shape = jax.ShapeDtypeStruct((depth // 2, rows), BF16)
    return pl.pallas_call(
        functools.partial(flip_kernel, owner_rows, plan.blocks),
        in_specs=[pl.BlockSpec(memory_space=pltpu.SMEM), pl.BlockSpec(memory_space=pltpu.VMEM)],
        out_specs=[pl.BlockSpec(memory_space=pltpu.VMEM)] * 2,
        out_shape=[shape, shape],
        compiler_params=pltpu.CompilerParams(vmem_limit_bytes=VMEM_LIMIT),
        cost_estimate=pl.CostEstimate(flops=4 * rows * depth, bytes_accessed=4 * rows * depth, transcendentals=0),
        name="flipped",
    )(core, left)


def pair_kernel(half_ref, left_own, left_got, own_ref, got_ref, send_ref, keep_ref):
    rows = send_ref.shape[0]
    term = dot_nn(left_own[...], own_ref[0]) + dot_nn(left_got[...], got_ref[0])
    low, high = term[:rows], term[rows:]
    upper = half_ref[0] == 1
    send_ref[...] = jnp.where(upper, low, high).astype(BF16)
    keep_ref[...] = jnp.where(upper, high, low).astype(BF16)


def pair_term(half, left_own, left_got, right_own, right_got):
    halves, rows, width = right_own.shape
    depth = left_own.shape[0]
    left = pl.BlockSpec((depth, rows), lambda j: (0, 0))
    right = pl.BlockSpec((1, rows, width), lambda j: (j, 0, 0))
    out = pl.BlockSpec((depth // 2, width), lambda j: (0, j))
    shape = jax.ShapeDtypeStruct((depth // 2, halves * width), BF16)
    return pl.pallas_call(
        pair_kernel,
        grid=(halves,),
        in_specs=[pl.BlockSpec(memory_space=pltpu.SMEM), left, left, right, right],
        out_specs=[out, out],
        out_shape=[shape, shape],
        compiler_params=pltpu.CompilerParams(vmem_limit_bytes=VMEM_LIMIT),
        cost_estimate=pl.CostEstimate(
            flops=4 * halves * rows * depth * width, bytes_accessed=8 * halves * rows * width, transcendentals=0
        ),
        name="pair_term",
    )(half.reshape(1), left_own, left_got, right_own, right_got)


def weight_kernel(owner_rows, orders, core_ref, left_ref, right_ref, send_ref, keep_ref):
    term = dot_tn(left_ref[...], right_ref[0])
    is_odd = core_ref[0] == 1
    send, keep = [], []
    for p, (even, odd) in enumerate(zip(*orders)):
        even = term[even * owner_rows : (even + 1) * owner_rows]
        odd = term[odd * owner_rows : (odd + 1) * owner_rows]
        send.append(jnp.where(is_odd, even, odd))
        keep.append(jnp.where(is_odd, odd, even))
    send_ref[...] = jnp.concatenate(send, axis=0).astype(BF16)
    keep_ref[...] = jnp.concatenate(keep, axis=0).astype(BF16)


def weight_term(core, left, right, plan):
    halves, rows, width = right.shape
    depth = left.shape[1]
    step = 512
    per = width // step
    out = pl.BlockSpec((depth // 2, step), lambda j: (0, j))
    shape = jax.ShapeDtypeStruct((depth // 2, halves * width), BF16)
    owner_rows = depth // (2 * len(plan.blocks[0]))
    return pl.pallas_call(
        functools.partial(weight_kernel, owner_rows, plan.blocks),
        grid=(halves * per,),
        in_specs=[
            pl.BlockSpec(memory_space=pltpu.SMEM),
            pl.BlockSpec((rows, depth), lambda j: (0, 0)),
            pl.BlockSpec((1, rows, step), lambda j: (j // per, 0, j % per)),
        ],
        out_specs=[out, out],
        out_shape=[shape, shape],
        compiler_params=pltpu.CompilerParams(vmem_limit_bytes=VMEM_LIMIT),
        cost_estimate=pl.CostEstimate(
            flops=2 * halves * rows * depth * width, bytes_accessed=6 * halves * rows * width, transcendentals=0
        ),
        name="weight_term",
    )(core, left, right)


class Halving:
    def __init__(self, dp_count, tm_count):
        near = [1 << i for i in range(1, (tm_count - 1).bit_length())]
        far = [tm_count << i for i in range((dp_count - 1).bit_length())]
        self.count = dp_count * tm_count
        self.masks = (near + far, far[: len(near)] + near + far[len(near) :])
        self.blocks = tuple(
            [self.block(core, masks, p) for p in range(self.count // 2)] for core, masks in enumerate(self.masks)
        )

    def block(self, core, masks, p):
        return core + sum(mask for i, mask in enumerate(masks) if p >> (len(masks) - 1 - i) & 1)

    def perm(self, step):
        if step < 0:
            return [(i, i ^ 1) for i in range(self.count)]
        return [(i, i ^ self.masks[i & 1][step]) for i in range(self.count)]

    def own_half(self, step, place):
        mask = jnp.where(place & 1 == 1, self.masks[1][step], self.masks[0][step])
        return ((place & mask) != 0).astype(jnp.int32)


def combine_kernel(half_ref, keep_other, got_other, keep_mine, got_mine, send_ref, keep_ref):
    send_ref[...] = (keep_other[...].astype(F32) + got_other[...].astype(F32)).astype(BF16)
    keep_ref[...] = (keep_mine[...].astype(F32) + got_mine[...].astype(F32)).astype(BF16)


def combine(half, keep, got):
    rows, width = keep.shape
    step = 512
    other = pl.BlockSpec((rows // 2, step), lambda j, half: (1 - half[0], j))
    mine = pl.BlockSpec((rows // 2, step), lambda j, half: (half[0], j))
    out = pl.BlockSpec((rows // 2, step), lambda j, half: (0, j))
    shape = jax.ShapeDtypeStruct((rows // 2, width), BF16)
    return pl.pallas_call(
        combine_kernel,
        grid_spec=pltpu.PrefetchScalarGridSpec(
            num_scalar_prefetch=1,
            grid=(width // step,),
            in_specs=[other, other, mine, mine],
            out_specs=[out, out],
        ),
        out_shape=[shape, shape],
        compiler_params=pltpu.CompilerParams(vmem_limit_bytes=VMEM_LIMIT),
        cost_estimate=pl.CostEstimate(flops=rows * width, bytes_accessed=6 * rows * width, transcendentals=0),
        name="combine",
    )(half.reshape(1), keep, got, keep, got)


class Scatter:
    def __init__(self, plan, place, parts):
        self.plan, self.place, self.step = plan, place, 0
        self.keep = [keep for _, keep in parts]
        self.got = [self.swap(send) for send, _ in parts]

    def swap(self, send):
        return lax.ppermute(send, ("dp", "tm"), self.plan.perm(self.step))

    def sums(self):
        parts = [keep.astype(F32) + got.astype(F32) for keep, got in zip(self.keep, self.got)]
        return parts[0] if len(parts) == 1 else jnp.concatenate(parts, axis=1)

    def ready(self):
        self.step += 1
        half = self.plan.own_half(self.step, self.place)
        both = self.sums()
        rows = both.shape[0] // 2
        low, high = both[:rows].astype(BF16), both[rows:].astype(BF16)
        self.keep = [jnp.where(half == 1, high, low)]
        return jnp.where(half == 1, low, high)

    def go(self, send):
        self.got = [self.swap(send)]

    def done(self):
        while self.step + 1 < len(self.plan.masks[0]):
            self.go(self.ready())
        return self.sums()


def from_all(copies):
    return lax.all_to_all(copies, ("dp", "tm"), 0, 0, tiled=True)


def shared(owned):
    count = lax.axis_size("dp") * lax.axis_size("tm")
    return from_all(jnp.broadcast_to(owned[None], (count,) + owned.shape))


def local(frames, lengths, w_in, w_dw, bn_gain, bn_bias, w_out, cotangent):
    feats, cot = frames[0], cotangent[0]
    rows, depth = feats.shape
    taps = w_dw.shape[0]
    tm_count = lax.axis_size("tm")
    device_count = lax.axis_size("dp") * tm_count
    plan = Halving(lax.axis_size("dp"), tm_count)
    place = lax.axis_index(("dp", "tm"))
    offset = lax.axis_index("tm") * rows
    span = jnp.stack([-offset, lengths[0] - offset]).astype(jnp.int32)
    core = (place & 1).astype(jnp.int32).reshape(1)
    gain, bias = bn_gain[None], bn_bias[None]

    everyone = ("dp", "tm")
    tail = jnp.concatenate([feats[rows - WIDE :], cot[rows - NEAR :]], axis=0)
    head = jnp.concatenate([feats[:WIDE], cot[:NEAR]], axis=0)
    before = lax.ppermute(tail, "tm", [(i, i + 1) for i in range(tm_count - 1)])
    after = lax.ppermute(head, "tm", [(i + 1, i) for i in range(tm_count - 1)])

    glu, first, second = gated(span, feats, w_in)
    conv, edge, sums = convolved(span, before, after, w_in, w_dw, glu, device_count)
    sums = from_all(sums)
    back = back_projected(before, cot, after, w_out)
    left_own, left_other = flipped(core, feats, plan)
    sums, left_other = lax.optimization_barrier((sums, left_other))
    left_got = lax.ppermute(left_other, everyone, plan.perm(-1))

    first_half = plan.own_half(0, place)
    swished, dshift, terms = swish(span, sums, gain, bias, conv, back)
    terms = from_all(terms)
    out_send, out_keep = weight_term(core, swished, cotangent, plan)
    out_got = lax.ppermute(out_send, everyone, plan.perm(-1))
    out_rows = dot_nn(swished, w_out).astype(BF16)
    out_send, out_keep = combine(first_half, out_keep, out_got)
    terms, out_rows, out_send, left_got = lax.optimization_barrier((terms, out_rows, out_send, left_got))
    out_scatter = Scatter(plan, place, [(out_send, out_keep)])

    parts = 2
    dpre_own, dpre_got, dconv = [], [], []
    for part in range(parts):
        own, grads = norm_grad(span, sums, terms, gain, w_dw, conv, dshift, first, second, part, parts)
        dpre_own.append(own)
        dconv.append(grads)
        dpre_got.append(lax.ppermute(own, everyone, plan.perm(-1)))
        if part == 0:
            send = out_scatter.ready()
            dshift, send = lax.optimization_barrier((dshift, send))
            out_scatter.go(send)
    in_parts = [pair_term(first_half, left_own, left_got, own, got) for own, got in zip(dpre_own, dpre_got)]
    in_scatter = Scatter(plan, place, in_parts)
    send = out_scatter.ready()
    glu, send, _ = lax.optimization_barrier((glu, send, [send for send, _ in in_parts]))
    out_scatter.go(send)
    tap_sums = tap_grad(edge, glu, dconv, taps)
    tap_sums, in_scatter.got, out_scatter.got = lax.optimization_barrier(
        (tap_sums, in_scatter.got, out_scatter.got)
    )
    out_send, in_send = out_scatter.ready(), in_scatter.ready()
    in_send, tap_sums = lax.optimization_barrier((in_send, tap_sums))
    in_scatter.go(in_send)
    out_scatter.go(out_send)
    owned = from_all(tap_sums.reshape(device_count, -1, LANES))
    in_send, *dpre_own = lax.optimization_barrier((in_scatter.ready(), *dpre_own))
    in_scatter.go(in_send)
    grad_rows = frames_grad(dpre_own, w_in)
    in_scatter.got, out_scatter.got, grad_rows, owned = lax.optimization_barrier(
        (in_scatter.got, out_scatter.got, grad_rows, owned)
    )
    owned = jnp.sum(owned, axis=0)
    in_send, owned = lax.optimization_barrier((in_scatter.ready(), owned))
    in_scatter.go(in_send)
    kernel_sum = shared(owned).reshape(tap_sums.shape).transpose(1, 0, 2).reshape(-1, depth)[:taps]
    grad_w_out = out_scatter.done()
    grad_w_in = in_scatter.done()
    grad_w_in = grad_w_in.reshape(-1, parts, 2, depth // parts).swapaxes(1, 2).reshape(-1, 2 * depth)
    by_gain, by_bias = jnp.sum(terms, axis=0)
    scale = 1.0 / math.sqrt(device_count * rows)
    return (
        out_rows[None],
        grad_rows[None],
        grad_w_in * scale,
        grad_w_out * scale,
        kernel_sum * scale,
        by_gain * scale,
        by_bias * scale,
    )


def solution(mesh):
    placed = (P("dp", "tm", None), P("dp"), P(), P(), P(), P(), P(), P("dp", "tm", None))
    return jax.shard_map(
        local,
        mesh=mesh,
        in_specs=placed,
        out_specs=(
            P("dp", "tm", None),
            P("dp", "tm", None),
            P(("dp", "tm"), None),
            P(("dp", "tm"), None),
            P(),
            P(),
            P(),
        ),
        check_vma=False,
    )
```

```python
import functools
import math

import jax
import jax.numpy as jnp
from jax import lax
from jax.experimental import pallas as pl
from jax.experimental.pallas import tpu as pltpu
from jax.sharding import PartitionSpec as P

F32 = jnp.float32
BF16 = jnp.bfloat16
LANES = 128
BLOCK = 256
SUB = BLOCK // LANES
WIDE = 32
NEAR = 16
VMEM_LIMIT = 30 << 20


def in_hbm(*arrays):
    return [pltpu.with_memory_space_constraint(x, pltpu.HBM) for x in arrays]


def in_vmem(*arrays):
    return [pltpu.with_memory_space_constraint(x, pltpu.VMEM) for x in arrays]


def dot_nn(a, b):
    return lax.dot_general(a, b, (((1,), (0,)), ((), ())), preferred_element_type=F32)


def dot_nt(a, b):
    return lax.dot_general(a, b, (((1,), (1,)), ((), ())), preferred_element_type=F32)


def dot_tn(a, b):
    return lax.dot_general(a, b, (((0,), (0,)), ((), ())), preferred_element_type=F32)


def logistic(x):
    return 1.0 / (1.0 + jnp.exp(-x))


def row_mask(start, count, low, high):
    rows = start + lax.broadcasted_iota(jnp.int32, (count, LANES), 0)
    return (rows >= low) & (rows < high)


def taps_chunk(src, c, begin, count, weight_row, taps):
    tiles = count // 8
    sums = [None] * tiles
    for residue in range(8):
        own = list(range(residue, taps, 8))
        weights = [jnp.broadcast_to(weight_row(k), (8, LANES)) for k in own]
        for q in range(tiles + len(own) - 1):
            tile = src[c, pl.ds(begin + residue + 8 * q, 8), :]
            for i, weight in enumerate(weights):
                u = q - i
                if 0 <= u < tiles:
                    term = weight * tile
                    sums[u] = term if sums[u] is None else sums[u] + term
    return sums


def lanes_of(c):
    return slice(c * LANES, (c + 1) * LANES)


def spread(copies_ref, c, lines):
    lines = jnp.concatenate(lines, axis=0)
    copies_ref[:, :, lanes_of(c)] = jnp.broadcast_to(lines[None], (copies_ref.shape[0],) + lines.shape)


def gate_kernel(span_ref, feats_ref, lin_w_ref, gate_w_ref, glu_ref, first_ref, second_ref):
    rows = feats_ref.shape[0]
    step = 128 if rows % 128 == 0 else rows
    for r in range(0, rows, step):
        lin = dot_nn(feats_ref[r : r + step, :], lin_w_ref[...])
        sig = logistic(dot_nn(feats_ref[r : r + step, :], gate_w_ref[...]))
        for c in range(SUB):
            lin_c, sig_c = lin[:, lanes_of(c)], sig[:, lanes_of(c)]
            live = row_mask(r, step, span_ref[0], span_ref[1])
            sig_c = jnp.where(live, sig_c, 0.0)
            prod = lin_c * sig_c
            glu_ref[c, r : r + step, :] = prod.astype(BF16)
            first_ref[r : r + step, lanes_of(c)] = sig_c.astype(BF16)
            second_ref[r : r + step, lanes_of(c)] = (prod * (1.0 - sig_c)).astype(BF16)


def gated(span, feats, w_in):
    rows, depth = feats.shape
    channels = w_in.shape[1] // 2
    blocks = channels // BLOCK
    return pl.pallas_call(
        gate_kernel,
        grid=(blocks,),
        in_specs=[
            pl.BlockSpec(memory_space=pltpu.SMEM),
            pl.BlockSpec((rows, depth), lambda j: (0, 0)),
            pl.BlockSpec((depth, BLOCK), lambda j: (0, j)),
            pl.BlockSpec((depth, BLOCK), lambda j: (0, j + blocks)),
        ],
        out_specs=[
            pl.BlockSpec((SUB, rows, LANES), lambda j: (j, 0, 0)),
            pl.BlockSpec((rows, BLOCK), lambda j: (0, j)),
            pl.BlockSpec((rows, BLOCK), lambda j: (0, j)),
        ],
        out_shape=[
            pltpu.HBM((channels // LANES, rows, LANES), BF16),
            pltpu.HBM((rows, channels), BF16),
            pltpu.HBM((rows, channels), BF16),
        ],
        compiler_params=pltpu.CompilerParams(vmem_limit_bytes=VMEM_LIMIT),
        cost_estimate=pl.CostEstimate(
            flops=4 * rows * depth * channels, bytes_accessed=14 * rows * channels, transcendentals=rows * channels
        ),
        name="gated",
    )(span, *in_hbm(feats, w_in, w_in))


def conv_kernel(span_ref, before_ref, after_ref, lin_w_ref, gate_w_ref, taps_ref, glu_ref, conv_ref, edge_ref, sums_ref, ext):
    rows = glu_ref.shape[1]
    taps = taps_ref.shape[0]
    full = rows + 2 * NEAR
    halo = jnp.concatenate([before_ref[...], after_ref[...]], axis=0)
    lin = dot_nn(halo, lin_w_ref[...])
    sig = logistic(dot_nn(halo, gate_w_ref[...]))
    low, high = span_ref[0], span_ref[1]
    live = jnp.concatenate([row_mask(-WIDE, WIDE, low, high), row_mask(rows, WIDE, low, high)], axis=0)
    for c in range(SUB):
        edge = jnp.where(live, lin[:, lanes_of(c)] * sig[:, lanes_of(c)], 0.0).astype(BF16)
        edge_ref[c] = edge
        edge = edge.astype(F32)
        ext[c, 0:WIDE, :] = edge[:WIDE]
        ext[c, WIDE + rows :, :] = edge[WIDE:]
        ext[c, WIDE : WIDE + rows, :] = glu_ref[c].astype(F32)
    count = 160 if full % 160 == 0 else NEAR
    own_low = jnp.maximum(low, 0) + NEAR
    own_high = jnp.minimum(high, rows) + NEAR
    shift = WIDE - NEAR - (taps - 1) // 2
    for c in range(SUB):

        def chunk(i, carry):
            r = pl.multiple_of(i * count, count)
            tiles = taps_chunk(ext, c, r + shift, count, lambda k: taps_ref[k : k + 1, lanes_of(c)], taps)
            total, square = carry
            for u, tile in enumerate(tiles):
                conv_ref[c, pl.ds(r + 8 * u, 8), :] = tile
                kept = jnp.where(row_mask(r + 8 * u, 8, own_low, own_high), tile, 0.0)
                total = total + kept
                square = square + kept * kept
            return total, square

        zero = jnp.zeros((8, LANES), F32)
        total, square = lax.fori_loop(0, full // count, chunk, (zero, zero))
        total = jnp.sum(total, axis=0, keepdims=True)
        square = jnp.sum(square, axis=0, keepdims=True)
        live_rows = jnp.full((1, LANES), 1.0, F32) * jnp.maximum(own_high - own_low, 0).astype(F32)
        spread(sums_ref, c, (total, square, live_rows))


def convolved(span, before, after, w_in, w_dw, glu, devices):
    groups, rows, _ = glu.shape
    channels = groups * LANES
    depth = w_in.shape[0]
    taps = w_dw.shape[0]
    blocks = channels // BLOCK
    full = rows + 2 * NEAR
    return pl.pallas_call(
        conv_kernel,
        grid=(blocks,),
        in_specs=[
            pl.BlockSpec(memory_space=pltpu.SMEM),
            pl.BlockSpec((WIDE, depth), lambda j: (0, 0)),
            pl.BlockSpec((WIDE, depth), lambda j: (0, 0)),
            pl.BlockSpec((depth, BLOCK), lambda j: (0, j)),
            pl.BlockSpec((depth, BLOCK), lambda j: (0, j + blocks)),
            pl.BlockSpec((taps, BLOCK), lambda j: (0, j)),
            pl.BlockSpec((SUB, rows, LANES), lambda j: (j, 0, 0)),
        ],
        out_specs=[
            pl.BlockSpec((SUB, full, LANES), lambda j: (j, 0, 0)),
            pl.BlockSpec((SUB, 2 * WIDE, LANES), lambda j: (j, 0, 0)),
            pl.BlockSpec((devices, 3, BLOCK), lambda j: (0, 0, j)),
        ],
        out_shape=[
            pltpu.VMEM((groups, full, LANES), F32),
            pltpu.HBM((groups, 2 * WIDE, LANES), BF16),
            pltpu.HBM((devices, 3, channels), F32),
        ],
        scratch_shapes=[pltpu.VMEM((SUB, rows + 2 * WIDE, LANES), F32)],
        compiler_params=pltpu.CompilerParams(vmem_limit_bytes=VMEM_LIMIT),
        cost_estimate=pl.CostEstimate(
            flops=4 * rows * depth * channels, bytes_accessed=14 * rows * channels, transcendentals=rows * channels
        ),
        name="convolved",
    )(span, *in_hbm(before, after, w_in, w_in, w_dw, glu))


def back_kernel(before_ref, own_ref, after_ref, w_ref, out_ref, left):
    rows = own_ref.shape[0]

    @pl.when(pl.program_id(0) == 0)
    def _():
        left[0:NEAR, :] = before_ref[...]
        left[NEAR : NEAR + rows, :] = own_ref[...]
        left[NEAR + rows :, :] = after_ref[...]

    prod = dot_nt(left[...], w_ref[...])
    for c in range(SUB):
        out_ref[c] = prod[:, lanes_of(c)].astype(BF16)


def back_projected(before, cot, after, w_out):
    rows, features = cot.shape
    channels = w_out.shape[0]
    full = rows + 2 * NEAR
    return pl.pallas_call(
        back_kernel,
        grid=(channels // BLOCK,),
        in_specs=[
            pl.BlockSpec((NEAR, features), lambda j: (WIDE // NEAR, 0)),
            pl.BlockSpec((rows, features), lambda j: (0, 0)),
            pl.BlockSpec((NEAR, features), lambda j: (WIDE // NEAR, 0)),
            pl.BlockSpec((BLOCK, features), lambda j: (j, 0)),
        ],
        out_specs=pl.BlockSpec((SUB, full, LANES), lambda j: (j, 0, 0)),
        out_shape=pltpu.HBM((channels // LANES, full, LANES), BF16),
        scratch_shapes=[pltpu.VMEM((full, features), BF16)],
        compiler_params=pltpu.CompilerParams(vmem_limit_bytes=VMEM_LIMIT),
        cost_estimate=pl.CostEstimate(
            flops=2 * rows * features * channels, bytes_accessed=8 * rows * channels, transcendentals=0
        ),
        name="back_projected",
    )(*in_hbm(before, cot, after, w_out))


def moments(sums_ref, c):
    sums = jnp.sum(sums_ref[:, :, lanes_of(c)], axis=0)
    count = sums[2:3]
    mean = sums[0:1] / count
    variance = sums[1:2] / count - mean * mean
    return mean, lax.rsqrt(variance + 1e-05), count


def swish_kernel(span_ref, sums_ref, gain_ref, bias_ref, conv_ref, back_ref, swished_ref, dshift_ref, terms_ref):
    rows = swished_ref.shape[0]
    low, high = span_ref[0], span_ref[1]
    count = 384 if rows % 384 == 0 else NEAR
    for c in range(SUB):
        mean, inv_std, _ = moments(sums_ref, c)
        gain, bias = gain_ref[:, lanes_of(c)], bias_ref[:, lanes_of(c)]

        def piece(r, size):
            at = pl.ds(r, size)
            normed = (conv_ref[c, at, :] - mean) * inv_std
            shifted = gain * normed + bias
            sig = logistic(shifted)
            live = row_mask(r - NEAR, size, low, high)
            swished = jnp.where(live, shifted * sig, 0.0)
            slope = sig + swished * (1.0 - sig)
            dshift = jnp.where(live, back_ref[c, at, :].astype(F32) * slope, 0.0)
            dshift_ref[c, at, :] = dshift.astype(BF16)
            return normed, swished, dshift

        def chunk(i, carry):
            r = pl.multiple_of(i * count, count)
            normed, swished, dshift = piece(r + NEAR, count)
            swished_ref[pl.ds(r, count), lanes_of(c)] = swished.astype(BF16)
            by_gain, by_bias = carry
            by_gain = by_gain + jnp.sum((dshift * normed).reshape(count // 8, 8, LANES), axis=0)
            by_bias = by_bias + jnp.sum(dshift.reshape(count // 8, 8, LANES), axis=0)
            return by_gain, by_bias

        zero = jnp.zeros((8, LANES), F32)
        by_gain, by_bias = lax.fori_loop(0, rows // count, chunk, (zero, zero))
        piece(0, NEAR)
        piece(rows + NEAR, NEAR)
        by_gain = jnp.sum(by_gain, axis=0, keepdims=True)
        by_bias = jnp.sum(by_bias, axis=0, keepdims=True)
        spread(terms_ref, c, (by_gain, by_bias))


def swish(span, sums, gain, bias, conv, back):
    groups, full, _ = conv.shape
    devices = sums.shape[0]
    rows = full - 2 * NEAR
    channels = groups * LANES
    vector = pl.BlockSpec((1, BLOCK), lambda j: (0, j))
    tall = pl.BlockSpec((SUB, full, LANES), lambda j: (j, 0, 0))
    return pl.pallas_call(
        swish_kernel,
        grid=(channels // BLOCK,),
        in_specs=[
            pl.BlockSpec(memory_space=pltpu.SMEM),
            pl.BlockSpec((devices, 3, BLOCK), lambda j: (0, 0, j)),
            vector,
            vector,
            tall,
            tall,
        ],
        out_specs=[
            pl.BlockSpec((rows, BLOCK), lambda j: (0, j)),
            tall,
            pl.BlockSpec((devices, 2, BLOCK), lambda j: (0, 0, j)),
        ],
        out_shape=[
            pltpu.HBM((rows, channels), BF16),
            pltpu.HBM((groups, full, LANES), BF16),
            pltpu.HBM((devices, 2, channels), F32),
        ],
        compiler_params=pltpu.CompilerParams(vmem_limit_bytes=VMEM_LIMIT),
        cost_estimate=pl.CostEstimate(
            flops=30 * rows * channels, bytes_accessed=14 * rows * channels, transcendentals=rows * channels
        ),
        name="swish",
    )(span, *in_hbm(sums, gain, bias), *in_vmem(conv), *in_hbm(back))


def grad_kernel(
    span_ref, sums_ref, terms_ref, gain_ref, taps_ref, conv_ref, dshift_ref, first_ref, second_ref, dpre_ref, dconv_ref, ext
):
    rows = first_ref.shape[0]
    taps = taps_ref.shape[0]
    full = rows + 2 * NEAR
    low, high = span_ref[0], span_ref[1]
    span = 160 if full % 160 == 0 else NEAR
    count = 128 if rows % 128 == 0 else NEAR
    shift = NEAR - (taps - 1) // 2
    for c in range(SUB):
        mean, inv_std, total = moments(sums_ref, c)
        at = lanes_of(c)
        outer = gain_ref[:, at] * inv_std
        terms = jnp.sum(terms_ref[:, :, at], axis=0)
        by_gain = terms[0:1] / total
        by_bias = terms[1:2] / total

        @pl.loop(0, full // span)
        def _(i):
            r = pl.multiple_of(i * span, span)
            normed = (conv_ref[c, pl.ds(r, span), :] - mean) * inv_std
            value = outer * (dshift_ref[c, pl.ds(r, span), :].astype(F32) - by_bias - normed * by_gain)
            live = row_mask(r - NEAR, span, low, high)
            ext[c, pl.ds(r, span), :] = jnp.where(live, value, 0.0).astype(BF16).astype(F32)

        dconv_ref[c] = ext[c, NEAR : NEAR + rows, :].astype(BF16)

        @pl.loop(0, rows // count)
        def _(i):
            r = pl.multiple_of(i * count, count)
            tiles = taps_chunk(ext, c, r + shift, count, lambda k: taps_ref[taps - 1 - k : taps - k, at], taps)
            for u in range(0, count // 8, 2):
                dglu = jnp.concatenate(tiles[u : u + 2], axis=0)
                own = pl.ds(r + 8 * u, 16)
                dpre_ref[0, own, at] = (dglu * first_ref[own, at].astype(F32)).astype(BF16)
                dpre_ref[1, own, at] = (dglu * second_ref[own, at].astype(F32)).astype(BF16)


def norm_grad(span, sums, terms, gain, w_dw, conv, dshift, first, second, part, parts):
    groups, full, _ = conv.shape
    devices = sums.shape[0]
    rows = full - 2 * NEAR
    channels = groups * LANES // parts
    taps = w_dw.shape[0]
    blocks = channels // BLOCK
    at = part * blocks
    tall = pl.BlockSpec((SUB, full, LANES), lambda j: (j + at, 0, 0))
    flat = pl.BlockSpec((rows, BLOCK), lambda j: (0, j + at))
    return pl.pallas_call(
        grad_kernel,
        grid=(blocks,),
        in_specs=[
            pl.BlockSpec(memory_space=pltpu.SMEM),
            pl.BlockSpec((devices, 3, BLOCK), lambda j: (0, 0, j + at)),
            pl.BlockSpec((devices, 2, BLOCK), lambda j: (0, 0, j + at)),
            pl.BlockSpec((1, BLOCK), lambda j: (0, j + at)),
            pl.BlockSpec((taps, BLOCK), lambda j: (0, j + at)),
            tall,
            tall,
            flat,
            flat,
        ],
        out_specs=[
            pl.BlockSpec((2, rows, BLOCK), lambda j: (0, 0, j)),
            pl.BlockSpec((SUB, rows, LANES), lambda j: (j, 0, 0)),
        ],
        out_shape=[
            pltpu.HBM((2, rows, channels), BF16),
            pltpu.HBM((channels // LANES, rows, LANES), BF16),
        ],
        scratch_shapes=[pltpu.VMEM((SUB, full, LANES), F32)],
        compiler_params=pltpu.CompilerParams(vmem_limit_bytes=VMEM_LIMIT),
        cost_estimate=pl.CostEstimate(
            flops=70 * rows * channels, bytes_accessed=16 * rows * channels, transcendentals=0
        ),
        name="norm_grad",
    )(span, *in_hbm(sums, terms, gain, w_dw), *in_vmem(conv), *in_hbm(dshift, first, second))


def tap_grad_kernel(taps, edge_ref, glu_ref, *refs):
    *dconv_refs, out_ref, ext, own = refs
    rows = glu_ref.shape[1]
    shift = WIDE - (taps - 1) // 2
    tiles = 16 if rows % 128 == 0 else 2
    per = pl.num_programs(0) // len(dconv_refs)
    for part, dconv_ref in enumerate(dconv_refs):

        @pl.when(pl.program_id(0) // per == part)
        def _(dconv_ref=dconv_ref):
            for c in range(SUB):
                own[c] = dconv_ref[c].astype(F32)

    for c in range(SUB):
        ext[c, 0:WIDE, :] = edge_ref[c, 0:WIDE, :].astype(F32)
        ext[c, WIDE : WIDE + rows, :] = glu_ref[c].astype(F32)
        ext[c, WIDE + rows :, :] = edge_ref[c, WIDE:, :].astype(F32)
    for c in range(SUB):

        def chunk(i, carry):
            sums = list(carry)
            r = pl.multiple_of(i * 8 * tiles, 8 * tiles)
            grads = [own[c, pl.ds(r + 8 * m, 8), :] for m in range(tiles)]
            for offset in range(taps + 8 * (tiles - 1)):
                held = None
                for m in range(tiles):
                    k = offset - 8 * m
                    if 0 <= k < taps:
                        if held is None:
                            held = ext[c, pl.ds(r + shift + offset, 8), :]
                        sums[k] = sums[k] + held * grads[m]
            return tuple(sums)

        zero = jnp.zeros((8, LANES), F32)
        sums = lax.fori_loop(0, rows // (8 * tiles), chunk, (zero,) * taps)
        out_ref[c] = jnp.zeros(out_ref.shape[1:], F32)
        for k in range(taps):
            out_ref[c, k : k + 1, :] = jnp.sum(sums[k], axis=0, keepdims=True)


def tap_grad(edge, glu, dconv_parts, taps):
    groups, rows, _ = glu.shape
    steps = groups // SUB
    per = steps // len(dconv_parts)
    padded = -(-taps // 8) * 8
    specs = [
        pl.BlockSpec((SUB, rows, LANES), lambda j, part=part: (jnp.clip(j - part * per, 0, per - 1), 0, 0))
        for part in range(len(dconv_parts))
    ]
    return pl.pallas_call(
        functools.partial(tap_grad_kernel, taps),
        grid=(steps,),
        in_specs=[
            pl.BlockSpec((SUB, 2 * WIDE, LANES), lambda j: (j, 0, 0)),
            pl.BlockSpec((SUB, rows, LANES), lambda j: (j, 0, 0)),
            *specs,
        ],
        out_specs=pl.BlockSpec((SUB, padded, LANES), lambda j: (j, 0, 0)),
        out_shape=jax.ShapeDtypeStruct((groups, padded, LANES), F32),
        scratch_shapes=[
            pltpu.VMEM((SUB, rows + 2 * WIDE, LANES), F32),
            pltpu.VMEM((SUB, rows, LANES), F32),
        ],
        compiler_params=pltpu.CompilerParams(vmem_limit_bytes=VMEM_LIMIT),
        cost_estimate=pl.CostEstimate(
            flops=62 * rows * groups * LANES, bytes_accessed=4 * rows * groups * LANES, transcendentals=0
        ),
        name="tap_grad",
    )(*in_hbm(edge, glu), *in_hbm(*dconv_parts))


def frames_grad_kernel(*refs):
    *dpre_refs, w_ref, out_ref = refs
    width = dpre_refs[0].shape[2]
    channels = width * len(dpre_refs)
    total = 0.0
    for i, dpre_ref in enumerate(dpre_refs):
        for half in range(2):
            at = half * channels + i * width
            total = total + dot_nt(dpre_ref[half], w_ref[:, at : at + width])
    out_ref[...] = total.astype(BF16)


def frames_grad(dpre_parts, w_in):
    _, rows, width = dpre_parts[0].shape
    depth, outputs = w_in.shape
    whole = pl.BlockSpec((2, rows, width), lambda j: (0, 0, 0))
    return pl.pallas_call(
        frames_grad_kernel,
        grid=(depth // BLOCK,),
        in_specs=[whole] * len(dpre_parts) + [pl.BlockSpec((BLOCK, outputs), lambda j: (j, 0))],
        out_specs=pl.BlockSpec((rows, BLOCK), lambda j: (0, j)),
        out_shape=jax.ShapeDtypeStruct((rows, depth), BF16),
        compiler_params=pltpu.CompilerParams(vmem_limit_bytes=VMEM_LIMIT),
        cost_estimate=pl.CostEstimate(
            flops=2 * rows * depth * outputs, bytes_accessed=10 * rows * depth, transcendentals=0
        ),
        name="frames_grad",
    )(*in_hbm(*dpre_parts, w_in))


def flip_kernel(owner_rows, orders, core_ref, left_ref, mine_ref, other_ref):
    flat = left_ref[...].astype(F32).T
    is_odd = core_ref[0] == 1

    def rows_of(order):
        return jnp.concatenate([flat[p * owner_rows : (p + 1) * owner_rows] for p in order], axis=0).astype(BF16)

    even, odd = rows_of(orders[0]), rows_of(orders[1])
    mine_ref[...] = jnp.where(is_odd, odd, even)
    other_ref[...] = jnp.where(is_odd, even, odd)


def flipped(core, left, plan):
    rows, depth = left.shape
    owner_rows = depth // (2 * len(plan.blocks[0]))
    shape = pltpu.HBM((depth // 2, rows), BF16)
    return pl.pallas_call(
        functools.partial(flip_kernel, owner_rows, plan.blocks),
        in_specs=[pl.BlockSpec(memory_space=pltpu.SMEM), pl.BlockSpec(memory_space=pltpu.VMEM)],
        out_specs=[pl.BlockSpec(memory_space=pltpu.VMEM)] * 2,
        out_shape=[shape, shape],
        compiler_params=pltpu.CompilerParams(vmem_limit_bytes=VMEM_LIMIT),
        cost_estimate=pl.CostEstimate(flops=4 * rows * depth, bytes_accessed=4 * rows * depth, transcendentals=0),
        name="flipped",
    )(core, *in_hbm(left))


def pair_kernel(half_ref, left_own, left_got, own_ref, got_ref, send_ref, keep_ref):
    rows = send_ref.shape[0]
    term = dot_nn(left_own[...], own_ref[0]) + dot_nn(left_got[...], got_ref[0])
    low, high = term[:rows], term[rows:]
    upper = half_ref[0] == 1
    send_ref[...] = jnp.where(upper, low, high).astype(BF16)
    keep_ref[...] = jnp.where(upper, high, low).astype(BF16)


def pair_term(half, left_own, left_got, right_own, right_got):
    halves, rows, width = right_own.shape
    depth = left_own.shape[0]
    left = pl.BlockSpec((depth, rows), lambda j: (0, 0))
    right = pl.BlockSpec((1, rows, width), lambda j: (j, 0, 0))
    out = pl.BlockSpec((depth // 2, width), lambda j: (0, j))
    shape = jax.ShapeDtypeStruct((depth // 2, halves * width), BF16)
    return pl.pallas_call(
        pair_kernel,
        grid=(halves,),
        in_specs=[pl.BlockSpec(memory_space=pltpu.SMEM), left, left, right, right],
        out_specs=[out, out],
        out_shape=[shape, shape],
        compiler_params=pltpu.CompilerParams(vmem_limit_bytes=VMEM_LIMIT),
        cost_estimate=pl.CostEstimate(
            flops=4 * halves * rows * depth * width, bytes_accessed=8 * halves * rows * width, transcendentals=0
        ),
        name="pair_term",
    )(half.reshape(1), *in_hbm(left_own, left_got, right_own, right_got))


def weight_kernel(owner_rows, orders, core_ref, left_ref, right_ref, send_ref, keep_ref):
    term = dot_tn(left_ref[...], right_ref[0])
    is_odd = core_ref[0] == 1
    send, keep = [], []
    for p, (even, odd) in enumerate(zip(*orders)):
        even = term[even * owner_rows : (even + 1) * owner_rows]
        odd = term[odd * owner_rows : (odd + 1) * owner_rows]
        send.append(jnp.where(is_odd, even, odd))
        keep.append(jnp.where(is_odd, odd, even))
    send_ref[...] = jnp.concatenate(send, axis=0).astype(BF16)
    keep_ref[...] = jnp.concatenate(keep, axis=0).astype(BF16)


def weight_term(core, left, right, plan):
    halves, rows, width = right.shape
    depth = left.shape[1]
    step = 512
    per = width // step
    out = pl.BlockSpec((depth // 2, step), lambda j: (0, j))
    shape = jax.ShapeDtypeStruct((depth // 2, halves * width), BF16)
    owner_rows = depth // (2 * len(plan.blocks[0]))
    return pl.pallas_call(
        functools.partial(weight_kernel, owner_rows, plan.blocks),
        grid=(halves * per,),
        in_specs=[
            pl.BlockSpec(memory_space=pltpu.SMEM),
            pl.BlockSpec((rows, depth), lambda j: (0, 0)),
            pl.BlockSpec((1, rows, step), lambda j: (j // per, 0, j % per)),
        ],
        out_specs=[out, out],
        out_shape=[shape, shape],
        compiler_params=pltpu.CompilerParams(vmem_limit_bytes=VMEM_LIMIT),
        name="weight_term",
    )(core, *in_hbm(left, right))


class Halving:
    def __init__(self, dp_count, tm_count):
        near = [1 << i for i in range(1, (tm_count - 1).bit_length())]
        far = [tm_count << i for i in range((dp_count - 1).bit_length())]
        self.count = dp_count * tm_count
        self.masks = (near + far, far[: len(near)] + near + far[len(near) :])
        self.blocks = tuple(
            [self.block(core, masks, p) for p in range(self.count // 2)] for core, masks in enumerate(self.masks)
        )

    def block(self, core, masks, p):
        return core + sum(mask for i, mask in enumerate(masks) if p >> (len(masks) - 1 - i) & 1)

    def perm(self, step):
        if step < 0:
            return [(i, i ^ 1) for i in range(self.count)]
        return [(i, i ^ self.masks[i & 1][step]) for i in range(self.count)]

    def own_half(self, step, place):
        mask = jnp.where(place & 1 == 1, self.masks[1][step], self.masks[0][step])
        return ((place & mask) != 0).astype(jnp.int32)


def combine_kernel(half_ref, keep_other, got_other, keep_mine, got_mine, send_ref, keep_ref):
    send_ref[...] = (keep_other[...].astype(F32) + got_other[...].astype(F32)).astype(BF16)
    keep_ref[...] = (keep_mine[...].astype(F32) + got_mine[...].astype(F32)).astype(BF16)


def combine(half, keep, got):
    rows, width = keep.shape
    step = 512
    other = pl.BlockSpec((rows // 2, step), lambda j, half: (1 - half[0], j))
    mine = pl.BlockSpec((rows // 2, step), lambda j, half: (half[0], j))
    out = pl.BlockSpec((rows // 2, step), lambda j, half: (0, j))
    shape = jax.ShapeDtypeStruct((rows // 2, width), BF16)
    return pl.pallas_call(
        combine_kernel,
        grid_spec=pltpu.PrefetchScalarGridSpec(
            num_scalar_prefetch=1,
            grid=(width // step,),
            in_specs=[other, other, mine, mine],
            out_specs=[out, out],
        ),
        out_shape=[shape, shape],
        compiler_params=pltpu.CompilerParams(vmem_limit_bytes=VMEM_LIMIT),
        name="combine",
    )(half.reshape(1), *in_hbm(keep, got, keep, got))


class Scatter:
    def __init__(self, plan, place, parts):
        self.plan, self.place, self.step = plan, place, 0
        self.keep = [keep for _, keep in parts]
        self.got = [self.swap(send) for send, _ in parts]

    def swap(self, send):
        return lax.ppermute(send, ("dp", "tm"), self.plan.perm(self.step))

    def sums(self):
        parts = [keep.astype(F32) + got.astype(F32) for keep, got in zip(self.keep, self.got)]
        return parts[0] if len(parts) == 1 else jnp.concatenate(parts, axis=1)

    def ready(self):
        self.step += 1
        half = self.plan.own_half(self.step, self.place)
        both = self.sums()
        rows = both.shape[0] // 2
        low, high = both[:rows].astype(BF16), both[rows:].astype(BF16)
        self.keep = [jnp.where(half == 1, high, low)]
        return jnp.where(half == 1, low, high)

    def go(self, send):
        self.got = [self.swap(send)]

    def done(self):
        while self.step + 1 < len(self.plan.masks[0]):
            self.go(self.ready())
        return self.sums()


def from_all(copies):
    return lax.all_to_all(copies, ("dp", "tm"), 0, 0, tiled=True)


def shared(owned):
    count = lax.axis_size("dp") * lax.axis_size("tm")
    return from_all(jnp.broadcast_to(owned[None], (count,) + owned.shape))


def local(frames, lengths, w_in, w_dw, bn_gain, bn_bias, w_out, cotangent):
    feats, cot = frames[0], cotangent[0]
    rows, depth = feats.shape
    taps = w_dw.shape[0]
    tm_count = lax.axis_size("tm")
    device_count = lax.axis_size("dp") * tm_count
    plan = Halving(lax.axis_size("dp"), tm_count)
    place = lax.axis_index(("dp", "tm"))
    offset = lax.axis_index("tm") * rows
    span = jnp.stack([-offset, lengths[0] - offset]).astype(jnp.int32)
    core = (place & 1).astype(jnp.int32).reshape(1)
    gain, bias = bn_gain[None], bn_bias[None]

    everyone = ("dp", "tm")
    tail = jnp.concatenate([feats[rows - WIDE :], cot[rows - NEAR :]], axis=0)
    head = jnp.concatenate([feats[:WIDE], cot[:NEAR]], axis=0)
    before = lax.ppermute(tail, "tm", [(i, i + 1) for i in range(tm_count - 1)])
    after = lax.ppermute(head, "tm", [(i + 1, i) for i in range(tm_count - 1)])

    glu, first, second = gated(span, feats, w_in)
    conv, edge, sums = convolved(span, before, after, w_in, w_dw, glu, device_count)
    sums = from_all(sums)
    back = back_projected(before, cot, after, w_out)
    left_own, left_other = flipped(core, feats, plan)
    sums, left_other = lax.optimization_barrier((sums, left_other))
    left_got = lax.ppermute(left_other, everyone, plan.perm(-1))

    first_half = plan.own_half(0, place)
    swished, dshift, terms = swish(span, sums, gain, bias, conv, back)
    terms = from_all(terms)
    out_send, out_keep = weight_term(core, swished, cotangent, plan)
    out_got = lax.ppermute(out_send, everyone, plan.perm(-1))
    out_rows = dot_nn(swished, w_out).astype(BF16)
    out_send, out_keep = combine(first_half, out_keep, out_got)
    terms, out_rows, out_send, left_got = lax.optimization_barrier((terms, out_rows, out_send, left_got))
    out_scatter = Scatter(plan, place, [(out_send, out_keep)])

    parts = 2
    dpre_own, dpre_got, dconv = [], [], []
    for part in range(parts):
        own, grads = norm_grad(span, sums, terms, gain, w_dw, conv, dshift, first, second, part, parts)
        dpre_own.append(own)
        dconv.append(grads)
        dpre_got.append(lax.ppermute(own, everyone, plan.perm(-1)))
        if part == 0:
            send = out_scatter.ready()
            dshift, send = lax.optimization_barrier((dshift, send))
            out_scatter.go(send)
    in_parts = [pair_term(first_half, left_own, left_got, own, got) for own, got in zip(dpre_own, dpre_got)]
    in_scatter = Scatter(plan, place, in_parts)
    send = out_scatter.ready()
    glu, send, _ = lax.optimization_barrier((glu, send, [send for send, _ in in_parts]))
    out_scatter.go(send)
    tap_sums = tap_grad(edge, glu, dconv, taps)
    tap_sums, in_scatter.got, out_scatter.got = lax.optimization_barrier(
        (tap_sums, in_scatter.got, out_scatter.got)
    )
    out_send, in_send = out_scatter.ready(), in_scatter.ready()
    in_send, tap_sums = lax.optimization_barrier((in_send, tap_sums))
    in_scatter.go(in_send)
    out_scatter.go(out_send)
    owned = from_all(tap_sums.reshape(device_count, -1, LANES))
    in_scatter.go(in_scatter.ready())
    in_scatter.got, out_scatter.got, owned = lax.optimization_barrier((in_scatter.got, out_scatter.got, owned))
    kernel_sum = shared(jnp.sum(owned, axis=0)).reshape(tap_sums.shape).transpose(1, 0, 2).reshape(-1, depth)[:taps]
    in_send, *dpre_own = lax.optimization_barrier((in_scatter.ready(), *dpre_own))
    in_scatter.go(in_send)
    grad_rows = frames_grad(dpre_own, w_in)
    grad_w_out = out_scatter.done()
    grad_w_in = in_scatter.done()
    grad_w_in = grad_w_in.reshape(-1, parts, 2, depth // parts).swapaxes(1, 2).reshape(-1, 2 * depth)
    by_gain, by_bias = jnp.sum(terms, axis=0)
    scale = 1.0 / math.sqrt(device_count * rows)
    return (
        out_rows[None],
        grad_rows[None],
        grad_w_in * scale,
        grad_w_out * scale,
        kernel_sum * scale,
        by_gain * scale,
        by_bias * scale,
    )


def solution(mesh):
    placed = (P("dp", "tm", None), P("dp"), P(), P(), P(), P(), P(), P("dp", "tm", None))
    return jax.shard_map(
        local,
        mesh=mesh,
        in_specs=placed,
        out_specs=(
            P("dp", "tm", None),
            P("dp", "tm", None),
            P(("dp", "tm"), None),
            P(("dp", "tm"), None),
            P(),
            P(),
            P(),
        ),
        check_vma=False,
    )
```

```python
import functools
import math

import jax
import jax.numpy as jnp
from jax import lax
from jax.experimental import pallas as pl
from jax.experimental.pallas import tpu as pltpu
from jax.sharding import PartitionSpec as P

F32 = jnp.float32
BF16 = jnp.bfloat16
LANES = 128
BLOCK = 256
SUB = BLOCK // LANES
WIDE = 32
NEAR = 16
VMEM_LIMIT = 30 << 20


def in_hbm(*arrays):
    return [pltpu.with_memory_space_constraint(x, pltpu.HBM) for x in arrays]


def in_vmem(*arrays):
    return [pltpu.with_memory_space_constraint(x, pltpu.VMEM) for x in arrays]


def dot_nn(a, b):
    return lax.dot_general(a, b, (((1,), (0,)), ((), ())), preferred_element_type=F32)


def dot_nt(a, b):
    return lax.dot_general(a, b, (((1,), (1,)), ((), ())), preferred_element_type=F32)


def dot_tn(a, b):
    return lax.dot_general(a, b, (((0,), (0,)), ((), ())), preferred_element_type=F32)


def logistic(x):
    return 1.0 / (1.0 + jnp.exp(-x))


def row_mask(start, count, low, high):
    rows = start + lax.broadcasted_iota(jnp.int32, (count, LANES), 0)
    return (rows >= low) & (rows < high)


def taps_chunk(src, c, begin, count, weight_row, taps):
    tiles = count // 8
    sums = [None] * tiles
    for residue in range(8):
        own = list(range(residue, taps, 8))
        weights = [jnp.broadcast_to(weight_row(k), (8, LANES)) for k in own]
        for q in range(tiles + len(own) - 1):
            tile = src[c, pl.ds(begin + residue + 8 * q, 8), :]
            for i, weight in enumerate(weights):
                u = q - i
                if 0 <= u < tiles:
                    term = weight * tile
                    sums[u] = term if sums[u] is None else sums[u] + term
    return sums


def lanes_of(c):
    return slice(c * LANES, (c + 1) * LANES)


def spread(copies_ref, c, lines):
    lines = jnp.concatenate(lines, axis=0)
    copies_ref[:, :, lanes_of(c)] = jnp.broadcast_to(lines[None], (copies_ref.shape[0],) + lines.shape)


def edges_kernel(last_ref, last_cot_ref, first_ref, first_cot_ref, tail_ref, head_ref):
    tail_ref[:WIDE] = last_ref[...]
    tail_ref[WIDE:] = last_cot_ref[...]
    head_ref[:WIDE] = first_ref[...]
    head_ref[WIDE:] = first_cot_ref[...]


def edges(feats, cot):
    rows, depth = feats.shape
    shape = jax.ShapeDtypeStruct((WIDE + NEAR, depth), BF16)
    return pl.pallas_call(
        edges_kernel,
        grid=(1,),
        in_specs=[
            pl.BlockSpec((WIDE, depth), lambda j: (rows // WIDE - 1, 0)),
            pl.BlockSpec((NEAR, depth), lambda j: (rows // NEAR - 1, 0)),
            pl.BlockSpec((WIDE, depth), lambda j: (0, 0)),
            pl.BlockSpec((NEAR, depth), lambda j: (0, 0)),
        ],
        out_specs=[pl.BlockSpec((WIDE + NEAR, depth), lambda j: (0, 0))] * 2,
        out_shape=[shape, shape],
        compiler_params=pltpu.CompilerParams(vmem_limit_bytes=VMEM_LIMIT),
        cost_estimate=pl.CostEstimate(flops=0, bytes_accessed=8 * WIDE * depth, transcendentals=0),
        name="edges",
    )(*in_hbm(feats, cot, feats, cot))


def gate_kernel(span_ref, feats_ref, lin_w_ref, gate_w_ref, glu_ref, first_ref, second_ref):
    rows = feats_ref.shape[0]
    step = 128 if rows % 128 == 0 else rows
    for r in range(0, rows, step):
        lin = dot_nn(feats_ref[r : r + step, :], lin_w_ref[...])
        sig = logistic(dot_nn(feats_ref[r : r + step, :], gate_w_ref[...]))
        for c in range(SUB):
            lin_c, sig_c = lin[:, lanes_of(c)], sig[:, lanes_of(c)]
            live = row_mask(r, step, span_ref[0], span_ref[1])
            sig_c = jnp.where(live, sig_c, 0.0)
            prod = lin_c * sig_c
            glu_ref[c, r : r + step, :] = prod.astype(BF16)
            first_ref[r : r + step, lanes_of(c)] = sig_c.astype(BF16)
            second_ref[r : r + step, lanes_of(c)] = (prod * (1.0 - sig_c)).astype(BF16)


def gated(span, feats, w_in):
    rows, depth = feats.shape
    channels = w_in.shape[1] // 2
    blocks = channels // BLOCK
    return pl.pallas_call(
        gate_kernel,
        grid=(blocks,),
        in_specs=[
            pl.BlockSpec(memory_space=pltpu.SMEM),
            pl.BlockSpec((rows, depth), lambda j: (0, 0)),
            pl.BlockSpec((depth, BLOCK), lambda j: (0, j)),
            pl.BlockSpec((depth, BLOCK), lambda j: (0, j + blocks)),
        ],
        out_specs=[
            pl.BlockSpec((SUB, rows, LANES), lambda j: (j, 0, 0)),
            pl.BlockSpec((rows, BLOCK), lambda j: (0, j)),
            pl.BlockSpec((rows, BLOCK), lambda j: (0, j)),
        ],
        out_shape=[
            pltpu.HBM((channels // LANES, rows, LANES), BF16),
            pltpu.HBM((rows, channels), BF16),
            pltpu.HBM((rows, channels), BF16),
        ],
        compiler_params=pltpu.CompilerParams(vmem_limit_bytes=VMEM_LIMIT),
        cost_estimate=pl.CostEstimate(
            flops=4 * rows * depth * channels, bytes_accessed=14 * rows * channels, transcendentals=rows * channels
        ),
        name="gated",
    )(span, *in_hbm(feats, w_in, w_in))


def conv_kernel(span_ref, before_ref, after_ref, lin_w_ref, gate_w_ref, taps_ref, glu_ref, conv_ref, edge_ref, sums_ref, ext):
    rows = glu_ref.shape[1]
    taps = taps_ref.shape[0]
    full = rows + 2 * NEAR
    halo = jnp.concatenate([before_ref[...], after_ref[...]], axis=0)
    pre = dot_nn(halo, jnp.concatenate([lin_w_ref[...], gate_w_ref[...]], axis=1))
    lin, sig = pre[:, :BLOCK], logistic(pre[:, BLOCK:])
    low, high = span_ref[0], span_ref[1]
    live = jnp.concatenate([row_mask(-WIDE, WIDE, low, high), row_mask(rows, WIDE, low, high)], axis=0)
    for c in range(SUB):
        edge = jnp.where(live, lin[:, lanes_of(c)] * sig[:, lanes_of(c)], 0.0).astype(BF16)
        edge_ref[c] = edge
        edge = edge.astype(F32)
        ext[c, 0:WIDE, :] = edge[:WIDE]
        ext[c, WIDE + rows :, :] = edge[WIDE:]
        ext[c, WIDE : WIDE + rows, :] = glu_ref[c].astype(F32)
    count = 160 if full % 160 == 0 else NEAR
    own_low = jnp.maximum(low, 0) + NEAR
    own_high = jnp.minimum(high, rows) + NEAR
    shift = WIDE - NEAR - (taps - 1) // 2
    for c in range(SUB):

        def chunk(i, carry):
            r = pl.multiple_of(i * count, count)
            tiles = taps_chunk(ext, c, r + shift, count, lambda k: taps_ref[k : k + 1, lanes_of(c)], taps)
            total, square = carry
            for u, tile in enumerate(tiles):
                conv_ref[c, pl.ds(r + 8 * u, 8), :] = tile
                kept = jnp.where(row_mask(r + 8 * u, 8, own_low, own_high), tile, 0.0)
                total = total + kept
                square = square + kept * kept
            return total, square

        zero = jnp.zeros((8, LANES), F32)
        total, square = lax.fori_loop(0, full // count, chunk, (zero, zero))
        total = jnp.sum(total, axis=0, keepdims=True)
        square = jnp.sum(square, axis=0, keepdims=True)
        live_rows = jnp.full((1, LANES), 1.0, F32) * jnp.maximum(own_high - own_low, 0).astype(F32)
        spread(sums_ref, c, (total, square, live_rows))


def convolved(span, before, after, w_in, w_dw, glu, devices):
    groups, rows, _ = glu.shape
    channels = groups * LANES
    depth = w_in.shape[0]
    taps = w_dw.shape[0]
    blocks = channels // BLOCK
    full = rows + 2 * NEAR
    return pl.pallas_call(
        conv_kernel,
        grid=(blocks,),
        in_specs=[
            pl.BlockSpec(memory_space=pltpu.SMEM),
            pl.BlockSpec((WIDE, depth), lambda j: (0, 0)),
            pl.BlockSpec((WIDE, depth), lambda j: (0, 0)),
            pl.BlockSpec((depth, BLOCK), lambda j: (0, j)),
            pl.BlockSpec((depth, BLOCK), lambda j: (0, j + blocks)),
            pl.BlockSpec((taps, BLOCK), lambda j: (0, j)),
            pl.BlockSpec((SUB, rows, LANES), lambda j: (j, 0, 0)),
        ],
        out_specs=[
            pl.BlockSpec((SUB, full, LANES), lambda j: (j, 0, 0)),
            pl.BlockSpec((SUB, 2 * WIDE, LANES), lambda j: (j, 0, 0)),
            pl.BlockSpec((devices, 3, BLOCK), lambda j: (0, 0, j)),
        ],
        out_shape=[
            pltpu.VMEM((groups, full, LANES), F32),
            pltpu.HBM((groups, 2 * WIDE, LANES), BF16),
            pltpu.HBM((devices, 3, channels), F32),
        ],
        scratch_shapes=[pltpu.VMEM((SUB, rows + 2 * WIDE, LANES), F32)],
        compiler_params=pltpu.CompilerParams(vmem_limit_bytes=VMEM_LIMIT),
        cost_estimate=pl.CostEstimate(
            flops=4 * rows * depth * channels, bytes_accessed=14 * rows * channels, transcendentals=rows * channels
        ),
        name="convolved",
    )(span, *in_hbm(before, after, w_in, w_in, w_dw, glu))


def back_kernel(before_ref, own_ref, after_ref, w_ref, out_ref, left):
    rows = own_ref.shape[0]

    @pl.when(pl.program_id(0) == 0)
    def _():
        left[0:NEAR, :] = before_ref[...]
        left[NEAR : NEAR + rows, :] = own_ref[...]
        left[NEAR + rows :, :] = after_ref[...]

    prod = dot_nt(left[...], w_ref[...])
    for c in range(SUB):
        out_ref[c] = prod[:, lanes_of(c)].astype(BF16)


def back_projected(before, cot, after, w_out):
    rows, features = cot.shape
    channels = w_out.shape[0]
    full = rows + 2 * NEAR
    return pl.pallas_call(
        back_kernel,
        grid=(channels // BLOCK,),
        in_specs=[
            pl.BlockSpec((NEAR, features), lambda j: (WIDE // NEAR, 0)),
            pl.BlockSpec((rows, features), lambda j: (0, 0)),
            pl.BlockSpec((NEAR, features), lambda j: (WIDE // NEAR, 0)),
            pl.BlockSpec((BLOCK, features), lambda j: (j, 0)),
        ],
        out_specs=pl.BlockSpec((SUB, full, LANES), lambda j: (j, 0, 0)),
        out_shape=pltpu.HBM((channels // LANES, full, LANES), BF16),
        scratch_shapes=[pltpu.VMEM((full, features), BF16)],
        compiler_params=pltpu.CompilerParams(vmem_limit_bytes=VMEM_LIMIT),
        cost_estimate=pl.CostEstimate(
            flops=2 * rows * features * channels, bytes_accessed=8 * rows * channels, transcendentals=0
        ),
        name="back_projected",
    )(*in_hbm(before, cot, after, w_out))


def moments(sums_ref, c):
    sums = jnp.sum(sums_ref[:, :, lanes_of(c)], axis=0)
    count = sums[2:3]
    mean = sums[0:1] / count
    variance = sums[1:2] / count - mean * mean
    return mean, lax.rsqrt(variance + 1e-05), count


def swish_kernel(span_ref, sums_ref, gain_ref, bias_ref, conv_ref, back_ref, swished_ref, dshift_ref, terms_ref):
    rows = swished_ref.shape[0]
    low, high = span_ref[0], span_ref[1]
    count = 384 if rows % 384 == 0 else NEAR
    for c in range(SUB):
        mean, inv_std, _ = moments(sums_ref, c)
        gain, bias = gain_ref[:, lanes_of(c)], bias_ref[:, lanes_of(c)]

        def piece(r, size):
            at = pl.ds(r, size)
            normed = (conv_ref[c, at, :] - mean) * inv_std
            shifted = gain * normed + bias
            sig = logistic(shifted)
            live = row_mask(r - NEAR, size, low, high)
            swished = jnp.where(live, shifted * sig, 0.0)
            slope = sig + swished * (1.0 - sig)
            dshift = jnp.where(live, back_ref[c, at, :].astype(F32) * slope, 0.0)
            dshift_ref[c, at, :] = dshift.astype(BF16)
            return normed, swished, dshift

        def chunk(i, carry):
            r = pl.multiple_of(i * count, count)
            normed, swished, dshift = piece(r + NEAR, count)
            swished_ref[pl.ds(r, count), lanes_of(c)] = swished.astype(BF16)
            by_gain, by_bias = carry
            by_gain = by_gain + jnp.sum((dshift * normed).reshape(count // 8, 8, LANES), axis=0)
            by_bias = by_bias + jnp.sum(dshift.reshape(count // 8, 8, LANES), axis=0)
            return by_gain, by_bias

        zero = jnp.zeros((8, LANES), F32)
        by_gain, by_bias = lax.fori_loop(0, rows // count, chunk, (zero, zero))
        piece(0, NEAR)
        piece(rows + NEAR, NEAR)
        by_gain = jnp.sum(by_gain, axis=0, keepdims=True)
        by_bias = jnp.sum(by_bias, axis=0, keepdims=True)
        spread(terms_ref, c, (by_gain, by_bias))


def swish(span, sums, gain, bias, conv, back):
    groups, full, _ = conv.shape
    devices = sums.shape[0]
    rows = full - 2 * NEAR
    channels = groups * LANES
    vector = pl.BlockSpec((1, BLOCK), lambda j: (0, j))
    tall = pl.BlockSpec((SUB, full, LANES), lambda j: (j, 0, 0))
    return pl.pallas_call(
        swish_kernel,
        grid=(channels // BLOCK,),
        in_specs=[
            pl.BlockSpec(memory_space=pltpu.SMEM),
            pl.BlockSpec((devices, 3, BLOCK), lambda j: (0, 0, j)),
            vector,
            vector,
            tall,
            tall,
        ],
        out_specs=[
            pl.BlockSpec((rows, BLOCK), lambda j: (0, j)),
            tall,
            pl.BlockSpec((devices, 2, BLOCK), lambda j: (0, 0, j)),
        ],
        out_shape=[
            pltpu.HBM((rows, channels), BF16),
            pltpu.HBM((groups, full, LANES), BF16),
            pltpu.HBM((devices, 2, channels), F32),
        ],
        compiler_params=pltpu.CompilerParams(vmem_limit_bytes=VMEM_LIMIT),
        cost_estimate=pl.CostEstimate(
            flops=30 * rows * channels, bytes_accessed=14 * rows * channels, transcendentals=rows * channels
        ),
        name="swish",
    )(span, *in_hbm(sums, gain, bias), *in_vmem(conv), *in_hbm(back))


def grad_kernel(
    span_ref, sums_ref, terms_ref, gain_ref, taps_ref, conv_ref, dshift_ref, first_ref, second_ref, dpre_ref, dconv_ref, ext
):
    rows = first_ref.shape[0]
    taps = taps_ref.shape[0]
    full = rows + 2 * NEAR
    low, high = span_ref[0], span_ref[1]
    span = 160 if full % 160 == 0 else NEAR
    count = 128 if rows % 128 == 0 else NEAR
    shift = NEAR - (taps - 1) // 2
    for c in range(SUB):
        mean, inv_std, total = moments(sums_ref, c)
        at = lanes_of(c)
        outer = gain_ref[:, at] * inv_std
        terms = jnp.sum(terms_ref[:, :, at], axis=0)
        by_gain = terms[0:1] / total
        by_bias = terms[1:2] / total

        @pl.loop(0, full // span)
        def _(i):
            r = pl.multiple_of(i * span, span)
            normed = (conv_ref[c, pl.ds(r, span), :] - mean) * inv_std
            value = outer * (dshift_ref[c, pl.ds(r, span), :].astype(F32) - by_bias - normed * by_gain)
            live = row_mask(r - NEAR, span, low, high)
            ext[c, pl.ds(r, span), :] = jnp.where(live, value, 0.0).astype(BF16).astype(F32)

        dconv_ref[c] = ext[c, NEAR : NEAR + rows, :].astype(BF16)

        @pl.loop(0, rows // count)
        def _(i):
            r = pl.multiple_of(i * count, count)
            tiles = taps_chunk(ext, c, r + shift, count, lambda k: taps_ref[taps - 1 - k : taps - k, at], taps)
            for u in range(0, count // 8, 2):
                dglu = jnp.concatenate(tiles[u : u + 2], axis=0)
                own = pl.ds(r + 8 * u, 16)
                dpre_ref[0, own, at] = (dglu * first_ref[own, at].astype(F32)).astype(BF16)
                dpre_ref[1, own, at] = (dglu * second_ref[own, at].astype(F32)).astype(BF16)


def norm_grad(span, sums, terms, gain, w_dw, conv, dshift, first, second, part, parts):
    groups, full, _ = conv.shape
    devices = sums.shape[0]
    rows = full - 2 * NEAR
    channels = groups * LANES // parts
    taps = w_dw.shape[0]
    blocks = channels // BLOCK
    at = part * blocks
    tall = pl.BlockSpec((SUB, full, LANES), lambda j: (j + at, 0, 0))
    flat = pl.BlockSpec((rows, BLOCK), lambda j: (0, j + at))
    return pl.pallas_call(
        grad_kernel,
        grid=(blocks,),
        in_specs=[
            pl.BlockSpec(memory_space=pltpu.SMEM),
            pl.BlockSpec((devices, 3, BLOCK), lambda j: (0, 0, j + at)),
            pl.BlockSpec((devices, 2, BLOCK), lambda j: (0, 0, j + at)),
            pl.BlockSpec((1, BLOCK), lambda j: (0, j + at)),
            pl.BlockSpec((taps, BLOCK), lambda j: (0, j + at)),
            tall,
            tall,
            flat,
            flat,
        ],
        out_specs=[
            pl.BlockSpec((2, rows, BLOCK), lambda j: (0, 0, j)),
            pl.BlockSpec((SUB, rows, LANES), lambda j: (j, 0, 0)),
        ],
        out_shape=[
            pltpu.HBM((2, rows, channels), BF16),
            pltpu.HBM((channels // LANES, rows, LANES), BF16),
        ],
        scratch_shapes=[pltpu.VMEM((SUB, full, LANES), F32)],
        compiler_params=pltpu.CompilerParams(vmem_limit_bytes=VMEM_LIMIT),
        cost_estimate=pl.CostEstimate(
            flops=70 * rows * channels, bytes_accessed=16 * rows * channels, transcendentals=0
        ),
        name="norm_grad",
    )(span, *in_hbm(sums, terms, gain, w_dw), *in_vmem(conv), *in_hbm(dshift, first, second))


def tap_grad_kernel(taps, edge_ref, glu_ref, *refs):
    *dconv_refs, out_ref, ext, own = refs
    rows = glu_ref.shape[1]
    shift = WIDE - (taps - 1) // 2
    tiles = 16 if rows % 128 == 0 else 2
    per = pl.num_programs(0) // len(dconv_refs)
    for part, dconv_ref in enumerate(dconv_refs):

        @pl.when(pl.program_id(0) // per == part)
        def _(dconv_ref=dconv_ref):
            for c in range(SUB):
                own[c] = dconv_ref[c].astype(F32)

    for c in range(SUB):
        ext[c, 0:WIDE, :] = edge_ref[c, 0:WIDE, :].astype(F32)
        ext[c, WIDE : WIDE + rows, :] = glu_ref[c].astype(F32)
        ext[c, WIDE + rows :, :] = edge_ref[c, WIDE:, :].astype(F32)
    for c in range(SUB):

        def chunk(i, carry):
            sums = list(carry)
            r = pl.multiple_of(i * 8 * tiles, 8 * tiles)
            grads = [own[c, pl.ds(r + 8 * m, 8), :] for m in range(tiles)]
            for offset in range(taps + 8 * (tiles - 1)):
                held = None
                for m in range(tiles):
                    k = offset - 8 * m
                    if 0 <= k < taps:
                        if held is None:
                            held = ext[c, pl.ds(r + shift + offset, 8), :]
                        sums[k] = sums[k] + held * grads[m]
            return tuple(sums)

        zero = jnp.zeros((8, LANES), F32)
        sums = lax.fori_loop(0, rows // (8 * tiles), chunk, (zero,) * taps)
        out_ref[c] = jnp.zeros(out_ref.shape[1:], F32)
        for k in range(taps):
            out_ref[c, k : k + 1, :] = jnp.sum(sums[k], axis=0, keepdims=True)


def tap_grad(edge, glu, dconv_parts, taps):
    groups, rows, _ = glu.shape
    steps = groups // SUB
    per = steps // len(dconv_parts)
    padded = -(-taps // 8) * 8
    specs = [
        pl.BlockSpec((SUB, rows, LANES), lambda j, part=part: (jnp.clip(j - part * per, 0, per - 1), 0, 0))
        for part in range(len(dconv_parts))
    ]
    return pl.pallas_call(
        functools.partial(tap_grad_kernel, taps),
        grid=(steps,),
        in_specs=[
            pl.BlockSpec((SUB, 2 * WIDE, LANES), lambda j: (j, 0, 0)),
            pl.BlockSpec((SUB, rows, LANES), lambda j: (j, 0, 0)),
            *specs,
        ],
        out_specs=pl.BlockSpec((SUB, padded, LANES), lambda j: (j, 0, 0)),
        out_shape=jax.ShapeDtypeStruct((groups, padded, LANES), F32),
        scratch_shapes=[
            pltpu.VMEM((SUB, rows + 2 * WIDE, LANES), F32),
            pltpu.VMEM((SUB, rows, LANES), F32),
        ],
        compiler_params=pltpu.CompilerParams(vmem_limit_bytes=VMEM_LIMIT),
        cost_estimate=pl.CostEstimate(
            flops=62 * rows * groups * LANES, bytes_accessed=4 * rows * groups * LANES, transcendentals=0
        ),
        name="tap_grad",
    )(*in_hbm(edge, glu), *in_hbm(*dconv_parts))


def frames_grad_kernel(*refs):
    *dpre_refs, w_ref, out_ref = refs
    width = dpre_refs[0].shape[2]
    channels = width * len(dpre_refs)
    total = 0.0
    for i, dpre_ref in enumerate(dpre_refs):
        for half in range(2):
            at = half * channels + i * width
            total = total + dot_nt(dpre_ref[half], w_ref[:, at : at + width])
    out_ref[...] = total.astype(BF16)


def frames_grad(dpre_parts, w_in):
    _, rows, width = dpre_parts[0].shape
    depth, outputs = w_in.shape
    whole = pl.BlockSpec((2, rows, width), lambda j: (0, 0, 0))
    return pl.pallas_call(
        frames_grad_kernel,
        grid=(depth // BLOCK,),
        in_specs=[whole] * len(dpre_parts) + [pl.BlockSpec((BLOCK, outputs), lambda j: (j, 0))],
        out_specs=pl.BlockSpec((rows, BLOCK), lambda j: (0, j)),
        out_shape=jax.ShapeDtypeStruct((rows, depth), BF16),
        compiler_params=pltpu.CompilerParams(vmem_limit_bytes=VMEM_LIMIT),
        cost_estimate=pl.CostEstimate(
            flops=2 * rows * depth * outputs, bytes_accessed=10 * rows * depth, transcendentals=0
        ),
        name="frames_grad",
    )(*in_hbm(*dpre_parts, w_in))


def flip_kernel(owner_rows, orders, core_ref, left_ref, mine_ref, other_ref):
    flat = left_ref[...].astype(F32).T
    is_odd = core_ref[0] == 1

    def rows_of(order):
        return jnp.concatenate([flat[p * owner_rows : (p + 1) * owner_rows] for p in order], axis=0).astype(BF16)

    even, odd = rows_of(orders[0]), rows_of(orders[1])
    mine_ref[...] = jnp.where(is_odd, odd, even)
    other_ref[...] = jnp.where(is_odd, even, odd)


def flipped(core, left, plan):
    rows, depth = left.shape
    owner_rows = depth // (2 * len(plan.blocks[0]))
    shape = pltpu.HBM((depth // 2, rows), BF16)
    return pl.pallas_call(
        functools.partial(flip_kernel, owner_rows, plan.blocks),
        in_specs=[pl.BlockSpec(memory_space=pltpu.SMEM), pl.BlockSpec(memory_space=pltpu.VMEM)],
        out_specs=[pl.BlockSpec(memory_space=pltpu.VMEM)] * 2,
        out_shape=[shape, shape],
        compiler_params=pltpu.CompilerParams(vmem_limit_bytes=VMEM_LIMIT),
        cost_estimate=pl.CostEstimate(flops=4 * rows * depth, bytes_accessed=4 * rows * depth, transcendentals=0),
        name="flipped",
    )(core, *in_hbm(left))


def pair_kernel(half_ref, left_own, left_got, own_ref, got_ref, send_ref, keep_ref):
    rows = send_ref.shape[0]
    term = dot_nn(left_own[...], own_ref[0]) + dot_nn(left_got[...], got_ref[0])
    low, high = term[:rows], term[rows:]
    upper = half_ref[0] == 1
    send_ref[...] = jnp.where(upper, low, high).astype(BF16)
    keep_ref[...] = jnp.where(upper, high, low).astype(BF16)


def pair_term(half, left_own, left_got, right_own, right_got):
    halves, rows, width = right_own.shape
    depth = left_own.shape[0]
    left = pl.BlockSpec((depth, rows), lambda j: (0, 0))
    right = pl.BlockSpec((1, rows, width), lambda j: (j, 0, 0))
    out = pl.BlockSpec((depth // 2, width), lambda j: (0, j))
    shape = jax.ShapeDtypeStruct((depth // 2, halves * width), BF16)
    return pl.pallas_call(
        pair_kernel,
        grid=(halves,),
        in_specs=[pl.BlockSpec(memory_space=pltpu.SMEM), left, left, right, right],
        out_specs=[out, out],
        out_shape=[shape, shape],
        compiler_params=pltpu.CompilerParams(vmem_limit_bytes=VMEM_LIMIT),
        cost_estimate=pl.CostEstimate(
            flops=4 * halves * rows * depth * width, bytes_accessed=8 * halves * rows * width, transcendentals=0
        ),
        name="pair_term",
    )(half.reshape(1), *in_hbm(left_own, left_got, right_own, right_got))


def weight_kernel(owner_rows, orders, core_ref, left_ref, right_ref, send_ref, keep_ref):
    term = dot_tn(left_ref[...], right_ref[0])
    is_odd = core_ref[0] == 1
    send, keep = [], []
    for p, (even, odd) in enumerate(zip(*orders)):
        even = term[even * owner_rows : (even + 1) * owner_rows]
        odd = term[odd * owner_rows : (odd + 1) * owner_rows]
        send.append(jnp.where(is_odd, even, odd))
        keep.append(jnp.where(is_odd, odd, even))
    send_ref[...] = jnp.concatenate(send, axis=0).astype(BF16)
    keep_ref[...] = jnp.concatenate(keep, axis=0).astype(BF16)


def weight_term(core, left, right, plan):
    halves, rows, width = right.shape
    depth = left.shape[1]
    step = 512
    per = width // step
    out = pl.BlockSpec((depth // 2, step), lambda j: (0, j))
    shape = jax.ShapeDtypeStruct((depth // 2, halves * width), BF16)
    owner_rows = depth // (2 * len(plan.blocks[0]))
    return pl.pallas_call(
        functools.partial(weight_kernel, owner_rows, plan.blocks),
        grid=(halves * per,),
        in_specs=[
            pl.BlockSpec(memory_space=pltpu.SMEM),
            pl.BlockSpec((rows, depth), lambda j: (0, 0)),
            pl.BlockSpec((1, rows, step), lambda j: (j // per, 0, j % per)),
        ],
        out_specs=[out, out],
        out_shape=[shape, shape],
        compiler_params=pltpu.CompilerParams(vmem_limit_bytes=VMEM_LIMIT),
        name="weight_term",
    )(core, *in_hbm(left, right))


class Halving:
    def __init__(self, dp_count, tm_count):
        near = [1 << i for i in range(1, (tm_count - 1).bit_length())]
        far = [tm_count << i for i in range((dp_count - 1).bit_length())]
        self.count = dp_count * tm_count
        self.masks = (near + far, far[: len(near)] + near + far[len(near) :])
        self.blocks = tuple(
            [self.block(core, masks, p) for p in range(self.count // 2)] for core, masks in enumerate(self.masks)
        )

    def block(self, core, masks, p):
        return core + sum(mask for i, mask in enumerate(masks) if p >> (len(masks) - 1 - i) & 1)

    def perm(self, step):
        if step < 0:
            return [(i, i ^ 1) for i in range(self.count)]
        return [(i, i ^ self.masks[i & 1][step]) for i in range(self.count)]

    def own_half(self, step, place):
        mask = jnp.where(place & 1 == 1, self.masks[1][step], self.masks[0][step])
        return ((place & mask) != 0).astype(jnp.int32)


def combine_kernel(half_ref, keep_other, got_other, keep_mine, got_mine, send_ref, keep_ref):
    send_ref[...] = (keep_other[...].astype(F32) + got_other[...].astype(F32)).astype(BF16)
    keep_ref[...] = (keep_mine[...].astype(F32) + got_mine[...].astype(F32)).astype(BF16)


def combine(half, keep, got):
    rows, width = keep.shape
    step = 512
    other = pl.BlockSpec((rows // 2, step), lambda j, half: (1 - half[0], j))
    mine = pl.BlockSpec((rows // 2, step), lambda j, half: (half[0], j))
    out = pl.BlockSpec((rows // 2, step), lambda j, half: (0, j))
    shape = jax.ShapeDtypeStruct((rows // 2, width), BF16)
    return pl.pallas_call(
        combine_kernel,
        grid_spec=pltpu.PrefetchScalarGridSpec(
            num_scalar_prefetch=1,
            grid=(width // step,),
            in_specs=[other, other, mine, mine],
            out_specs=[out, out],
        ),
        out_shape=[shape, shape],
        compiler_params=pltpu.CompilerParams(vmem_limit_bytes=VMEM_LIMIT),
        name="combine",
    )(half.reshape(1), *in_hbm(keep, got, keep, got))


class Scatter:
    def __init__(self, plan, place, parts):
        self.plan, self.place, self.step = plan, place, 0
        self.keep = [keep for _, keep in parts]
        self.got = [self.swap(send) for send, _ in parts]

    def swap(self, send):
        return lax.ppermute(send, ("dp", "tm"), self.plan.perm(self.step))

    def sums(self):
        parts = [keep.astype(F32) + got.astype(F32) for keep, got in zip(self.keep, self.got)]
        return parts[0] if len(parts) == 1 else jnp.concatenate(parts, axis=1)

    def ready(self):
        self.step += 1
        half = self.plan.own_half(self.step, self.place)
        both = self.sums()
        rows = both.shape[0] // 2
        low, high = both[:rows].astype(BF16), both[rows:].astype(BF16)
        self.keep = [jnp.where(half == 1, high, low)]
        return jnp.where(half == 1, low, high)

    def go(self, send):
        self.got = [self.swap(send)]

    def done(self):
        while self.step + 1 < len(self.plan.masks[0]):
            self.go(self.ready())
        return self.sums()


def from_all(copies):
    return lax.all_to_all(copies, ("dp", "tm"), 0, 0, tiled=True)


def shared(owned):
    count = lax.axis_size("dp") * lax.axis_size("tm")
    return from_all(jnp.broadcast_to(owned[None], (count,) + owned.shape))


def local(frames, lengths, w_in, w_dw, bn_gain, bn_bias, w_out, cotangent):
    feats, cot = frames[0], cotangent[0]
    rows, depth = feats.shape
    taps = w_dw.shape[0]
    tm_count = lax.axis_size("tm")
    device_count = lax.axis_size("dp") * tm_count
    plan = Halving(lax.axis_size("dp"), tm_count)
    place = lax.axis_index(("dp", "tm"))
    offset = lax.axis_index("tm") * rows
    span = jnp.stack([-offset, lengths[0] - offset]).astype(jnp.int32)
    core = (place & 1).astype(jnp.int32).reshape(1)
    gain, bias = bn_gain[None], bn_bias[None]

    everyone = ("dp", "tm")
    tail, head = edges(feats, cot)
    before = lax.ppermute(tail, "tm", [(i, i + 1) for i in range(tm_count - 1)])
    after = lax.ppermute(head, "tm", [(i + 1, i) for i in range(tm_count - 1)])

    glu, first, second = gated(span, feats, w_in)
    conv, edge, sums = convolved(span, before, after, w_in, w_dw, glu, device_count)
    sums = from_all(sums)
    back = back_projected(before, cot, after, w_out)
    left_own, left_other = flipped(core, feats, plan)
    sums, left_other = lax.optimization_barrier((sums, left_other))
    left_got = lax.ppermute(left_other, everyone, plan.perm(-1))

    first_half = plan.own_half(0, place)
    swished, dshift, terms = swish(span, sums, gain, bias, conv, back)
    terms = from_all(terms)
    out_send, out_keep = weight_term(core, swished, cotangent, plan)
    out_got = lax.ppermute(out_send, everyone, plan.perm(-1))
    out_rows = dot_nn(swished, w_out).astype(BF16)
    out_send, out_keep = combine(first_half, out_keep, out_got)
    terms, out_rows, out_send, left_got = lax.optimization_barrier((terms, out_rows, out_send, left_got))
    out_scatter = Scatter(plan, place, [(out_send, out_keep)])

    parts = 2
    dpre_own, dpre_got, dconv = [], [], []
    for part in range(parts):
        own, grads = norm_grad(span, sums, terms, gain, w_dw, conv, dshift, first, second, part, parts)
        dpre_own.append(own)
        dconv.append(grads)
        dpre_got.append(lax.ppermute(own, everyone, plan.perm(-1)))
        if part == 0:
            send = out_scatter.ready()
            dshift, send = lax.optimization_barrier((dshift, send))
            out_scatter.go(send)
    in_parts = [pair_term(first_half, left_own, left_got, own, got) for own, got in zip(dpre_own, dpre_got)]
    in_scatter = Scatter(plan, place, in_parts)
    send = out_scatter.ready()
    glu, send, _ = lax.optimization_barrier((glu, send, [send for send, _ in in_parts]))
    out_scatter.go(send)
    tap_sums = tap_grad(edge, glu, dconv, taps)
    tap_sums, in_scatter.got, out_scatter.got = lax.optimization_barrier(
        (tap_sums, in_scatter.got, out_scatter.got)
    )
    out_send, in_send = out_scatter.ready(), in_scatter.ready()
    in_send, tap_sums = lax.optimization_barrier((in_send, tap_sums))
    in_scatter.go(in_send)
    out_scatter.go(out_send)
    owned = from_all(tap_sums.reshape(device_count, -1, LANES))
    in_scatter.go(in_scatter.ready())
    in_scatter.got, out_scatter.got, owned = lax.optimization_barrier((in_scatter.got, out_scatter.got, owned))
    kernel_sum = shared(jnp.sum(owned, axis=0)).reshape(tap_sums.shape).transpose(1, 0, 2).reshape(-1, depth)[:taps]
    in_send, *dpre_own = lax.optimization_barrier((in_scatter.ready(), *dpre_own))
    in_scatter.go(in_send)
    grad_rows = frames_grad(dpre_own, w_in)
    grad_w_out = out_scatter.done()
    grad_w_in = in_scatter.done()
    grad_w_in = grad_w_in.reshape(-1, parts, 2, depth // parts).swapaxes(1, 2).reshape(-1, 2 * depth)
    by_gain, by_bias = jnp.sum(terms, axis=0)
    scale = 1.0 / math.sqrt(device_count * rows)
    return (
        out_rows[None],
        grad_rows[None],
        grad_w_in * scale,
        grad_w_out * scale,
        kernel_sum * scale,
        by_gain * scale,
        by_bias * scale,
    )


def solution(mesh):
    placed = (P("dp", "tm", None), P("dp"), P(), P(), P(), P(), P(), P("dp", "tm", None))
    return jax.shard_map(
        local,
        mesh=mesh,
        in_specs=placed,
        out_specs=(
            P("dp", "tm", None),
            P("dp", "tm", None),
            P(("dp", "tm"), None),
            P(("dp", "tm"), None),
            P(),
            P(),
            P(),
        ),
        check_vma=False,
    )
```

```python
import functools
import math

import jax
import jax.numpy as jnp
from jax import lax
from jax.experimental import pallas as pl
from jax.experimental.pallas import tpu as pltpu
from jax.sharding import PartitionSpec as P

F32 = jnp.float32
BF16 = jnp.bfloat16
LANES = 128
BLOCK = 256
SUB = BLOCK // LANES
WIDE = 32
NEAR = 16
VMEM_LIMIT = 30 << 20


def in_hbm(*arrays):
    return [pltpu.with_memory_space_constraint(x, pltpu.HBM) for x in arrays]


def in_vmem(*arrays):
    return [pltpu.with_memory_space_constraint(x, pltpu.VMEM) for x in arrays]


def dot_nn(a, b):
    return lax.dot_general(a, b, (((1,), (0,)), ((), ())), preferred_element_type=F32)


def dot_nt(a, b):
    return lax.dot_general(a, b, (((1,), (1,)), ((), ())), preferred_element_type=F32)


def dot_tn(a, b):
    return lax.dot_general(a, b, (((0,), (0,)), ((), ())), preferred_element_type=F32)


def logistic(x):
    return 1.0 / (1.0 + jnp.exp(-x))


def row_mask(start, count, low, high):
    rows = start + lax.broadcasted_iota(jnp.int32, (count, LANES), 0)
    return (rows >= low) & (rows < high)


def taps_chunk(src, c, begin, count, weight_row, taps):
    tiles = count // 8
    sums = [None] * tiles
    for residue in range(8):
        own = list(range(residue, taps, 8))
        weights = [jnp.broadcast_to(weight_row(k), (8, LANES)) for k in own]
        for q in range(tiles + len(own) - 1):
            tile = src[c, pl.ds(begin + residue + 8 * q, 8), :]
            for i, weight in enumerate(weights):
                u = q - i
                if 0 <= u < tiles:
                    term = weight * tile
                    sums[u] = term if sums[u] is None else sums[u] + term
    return sums


def lanes_of(c):
    return slice(c * LANES, (c + 1) * LANES)


def spread(copies_ref, c, lines):
    lines = jnp.concatenate(lines, axis=0)
    copies_ref[:, :, lanes_of(c)] = jnp.broadcast_to(lines[None], (copies_ref.shape[0],) + lines.shape)


def edges_kernel(last_ref, last_cot_ref, first_ref, first_cot_ref, tail_ref, head_ref):
    tail_ref[:WIDE] = last_ref[...]
    tail_ref[WIDE:] = last_cot_ref[...]
    head_ref[:WIDE] = first_ref[...]
    head_ref[WIDE:] = first_cot_ref[...]


def edges(feats, cot):
    rows, depth = feats.shape
    shape = jax.ShapeDtypeStruct((WIDE + NEAR, depth), BF16)
    return pl.pallas_call(
        edges_kernel,
        grid=(1,),
        in_specs=[
            pl.BlockSpec((WIDE, depth), lambda j: (rows // WIDE - 1, 0)),
            pl.BlockSpec((NEAR, depth), lambda j: (rows // NEAR - 1, 0)),
            pl.BlockSpec((WIDE, depth), lambda j: (0, 0)),
            pl.BlockSpec((NEAR, depth), lambda j: (0, 0)),
        ],
        out_specs=[pl.BlockSpec((WIDE + NEAR, depth), lambda j: (0, 0))] * 2,
        out_shape=[shape, shape],
        compiler_params=pltpu.CompilerParams(vmem_limit_bytes=VMEM_LIMIT),
        cost_estimate=pl.CostEstimate(flops=0, bytes_accessed=8 * WIDE * depth, transcendentals=0),
        name="edges",
    )(*in_hbm(feats, cot, feats, cot))


def gate_kernel(span_ref, feats_ref, lin_w_ref, gate_w_ref, glu_ref, first_ref, second_ref):
    rows = feats_ref.shape[0]
    step = 128 if rows % 128 == 0 else rows
    for r in range(0, rows, step):
        lin = dot_nn(feats_ref[r : r + step, :], lin_w_ref[...])
        sig = logistic(dot_nn(feats_ref[r : r + step, :], gate_w_ref[...]))
        for c in range(SUB):
            lin_c, sig_c = lin[:, lanes_of(c)], sig[:, lanes_of(c)]
            live = row_mask(r, step, span_ref[0], span_ref[1])
            sig_c = jnp.where(live, sig_c, 0.0)
            prod = lin_c * sig_c
            glu_ref[c, r : r + step, :] = prod.astype(BF16)
            first_ref[r : r + step, lanes_of(c)] = sig_c.astype(BF16)
            second_ref[r : r + step, lanes_of(c)] = (prod * (1.0 - sig_c)).astype(BF16)


def gated(span, feats, w_in):
    rows, depth = feats.shape
    channels = w_in.shape[1] // 2
    blocks = channels // BLOCK
    return pl.pallas_call(
        gate_kernel,
        grid=(blocks,),
        in_specs=[
            pl.BlockSpec(memory_space=pltpu.SMEM),
            pl.BlockSpec((rows, depth), lambda j: (0, 0)),
            pl.BlockSpec((depth, BLOCK), lambda j: (0, j)),
            pl.BlockSpec((depth, BLOCK), lambda j: (0, j + blocks)),
        ],
        out_specs=[
            pl.BlockSpec((SUB, rows, LANES), lambda j: (j, 0, 0)),
            pl.BlockSpec((rows, BLOCK), lambda j: (0, j)),
            pl.BlockSpec((rows, BLOCK), lambda j: (0, j)),
        ],
        out_shape=[
            pltpu.HBM((channels // LANES, rows, LANES), BF16),
            pltpu.HBM((rows, channels), BF16),
            pltpu.HBM((rows, channels), BF16),
        ],
        compiler_params=pltpu.CompilerParams(vmem_limit_bytes=VMEM_LIMIT),
        cost_estimate=pl.CostEstimate(
            flops=4 * rows * depth * channels, bytes_accessed=14 * rows * channels, transcendentals=rows * channels
        ),
        name="gated",
    )(span, *in_hbm(feats, w_in, w_in))


def conv_kernel(span_ref, before_ref, after_ref, lin_w_ref, gate_w_ref, taps_ref, glu_ref, conv_ref, edge_ref, sums_ref, ext):
    rows = glu_ref.shape[1]
    taps = taps_ref.shape[0]
    full = rows + 2 * NEAR
    halo = jnp.concatenate([before_ref[...], after_ref[...]], axis=0)
    pre = dot_nn(halo, jnp.concatenate([lin_w_ref[...], gate_w_ref[...]], axis=1))
    lin, sig = pre[:, :BLOCK], logistic(pre[:, BLOCK:])
    low, high = span_ref[0], span_ref[1]
    live = jnp.concatenate([row_mask(-WIDE, WIDE, low, high), row_mask(rows, WIDE, low, high)], axis=0)
    for c in range(SUB):
        edge = jnp.where(live, lin[:, lanes_of(c)] * sig[:, lanes_of(c)], 0.0).astype(BF16)
        edge_ref[c] = edge
        edge = edge.astype(F32)
        ext[c, 0:WIDE, :] = edge[:WIDE]
        ext[c, WIDE + rows :, :] = edge[WIDE:]
        ext[c, WIDE : WIDE + rows, :] = glu_ref[c].astype(F32)
    count = 160 if full % 160 == 0 else NEAR
    own_low = jnp.maximum(low, 0) + NEAR
    own_high = jnp.minimum(high, rows) + NEAR
    shift = WIDE - NEAR - (taps - 1) // 2
    for c in range(SUB):

        def chunk(i, carry):
            r = pl.multiple_of(i * count, count)
            tiles = taps_chunk(ext, c, r + shift, count, lambda k: taps_ref[k : k + 1, lanes_of(c)], taps)
            total, square = carry
            for u, tile in enumerate(tiles):
                conv_ref[c, pl.ds(r + 8 * u, 8), :] = tile
                kept = jnp.where(row_mask(r + 8 * u, 8, own_low, own_high), tile, 0.0)
                total = total + kept
                square = square + kept * kept
            return total, square

        zero = jnp.zeros((8, LANES), F32)
        total, square = lax.fori_loop(0, full // count, chunk, (zero, zero))
        total = jnp.sum(total, axis=0, keepdims=True)
        square = jnp.sum(square, axis=0, keepdims=True)
        live_rows = jnp.full((1, LANES), 1.0, F32) * jnp.maximum(own_high - own_low, 0).astype(F32)
        spread(sums_ref, c, (total, square, live_rows))


def convolved(span, before, after, w_in, w_dw, glu, devices):
    groups, rows, _ = glu.shape
    channels = groups * LANES
    depth = w_in.shape[0]
    taps = w_dw.shape[0]
    blocks = channels // BLOCK
    full = rows + 2 * NEAR
    return pl.pallas_call(
        conv_kernel,
        grid=(blocks,),
        in_specs=[
            pl.BlockSpec(memory_space=pltpu.SMEM),
            pl.BlockSpec((WIDE, depth), lambda j: (0, 0)),
            pl.BlockSpec((WIDE, depth), lambda j: (0, 0)),
            pl.BlockSpec((depth, BLOCK), lambda j: (0, j)),
            pl.BlockSpec((depth, BLOCK), lambda j: (0, j + blocks)),
            pl.BlockSpec((taps, BLOCK), lambda j: (0, j)),
            pl.BlockSpec((SUB, rows, LANES), lambda j: (j, 0, 0)),
        ],
        out_specs=[
            pl.BlockSpec((SUB, full, LANES), lambda j: (j, 0, 0)),
            pl.BlockSpec((SUB, 2 * WIDE, LANES), lambda j: (j, 0, 0)),
            pl.BlockSpec((devices, 3, BLOCK), lambda j: (0, 0, j)),
        ],
        out_shape=[
            pltpu.VMEM((groups, full, LANES), F32),
            pltpu.HBM((groups, 2 * WIDE, LANES), BF16),
            pltpu.HBM((devices, 3, channels), F32),
        ],
        scratch_shapes=[pltpu.VMEM((SUB, rows + 2 * WIDE, LANES), F32)],
        compiler_params=pltpu.CompilerParams(vmem_limit_bytes=VMEM_LIMIT),
        cost_estimate=pl.CostEstimate(
            flops=4 * rows * depth * channels, bytes_accessed=14 * rows * channels, transcendentals=rows * channels
        ),
        name="convolved",
    )(span, *in_hbm(before, after, w_in, w_in, w_dw, glu))


def back_kernel(before_ref, own_ref, after_ref, w_ref, out_ref, left):
    rows = own_ref.shape[0]

    @pl.when(pl.program_id(0) == 0)
    def _():
        left[0:NEAR, :] = before_ref[...]
        left[NEAR : NEAR + rows, :] = own_ref[...]
        left[NEAR + rows :, :] = after_ref[...]

    prod = dot_nt(left[...], w_ref[...])
    for c in range(SUB):
        out_ref[c] = prod[:, lanes_of(c)].astype(BF16)


def back_projected(before, cot, after, w_out):
    rows, features = cot.shape
    channels = w_out.shape[0]
    full = rows + 2 * NEAR
    return pl.pallas_call(
        back_kernel,
        grid=(channels // BLOCK,),
        in_specs=[
            pl.BlockSpec((NEAR, features), lambda j: (WIDE // NEAR, 0)),
            pl.BlockSpec((rows, features), lambda j: (0, 0)),
            pl.BlockSpec((NEAR, features), lambda j: (WIDE // NEAR, 0)),
            pl.BlockSpec((BLOCK, features), lambda j: (j, 0)),
        ],
        out_specs=pl.BlockSpec((SUB, full, LANES), lambda j: (j, 0, 0)),
        out_shape=pltpu.HBM((channels // LANES, full, LANES), BF16),
        scratch_shapes=[pltpu.VMEM((full, features), BF16)],
        compiler_params=pltpu.CompilerParams(vmem_limit_bytes=VMEM_LIMIT),
        cost_estimate=pl.CostEstimate(
            flops=2 * rows * features * channels, bytes_accessed=8 * rows * channels, transcendentals=0
        ),
        name="back_projected",
    )(*in_hbm(before, cot, after, w_out))


def moments(sums_ref, c):
    sums = jnp.sum(sums_ref[:, :, lanes_of(c)], axis=0)
    count = sums[2:3]
    mean = sums[0:1] / count
    variance = sums[1:2] / count - mean * mean
    return mean, lax.rsqrt(variance + 1e-05), count


def swish_kernel(span_ref, sums_ref, gain_ref, bias_ref, conv_ref, back_ref, swished_ref, dshift_ref, terms_ref):
    rows = swished_ref.shape[0]
    low, high = span_ref[0], span_ref[1]
    count = 768 if rows % 768 == 0 else NEAR
    for c in range(SUB):
        mean, inv_std, _ = moments(sums_ref, c)
        gain, bias = gain_ref[:, lanes_of(c)], bias_ref[:, lanes_of(c)]

        def piece(r, size):
            at = pl.ds(r, size)
            normed = (conv_ref[c, at, :] - mean) * inv_std
            shifted = gain * normed + bias
            sig = logistic(shifted)
            live = row_mask(r - NEAR, size, low, high)
            swished = jnp.where(live, shifted * sig, 0.0)
            slope = sig + swished * (1.0 - sig)
            dshift = jnp.where(live, back_ref[c, at, :].astype(F32) * slope, 0.0)
            dshift_ref[c, at, :] = dshift.astype(BF16)
            return normed, swished, dshift

        def chunk(i, carry):
            r = pl.multiple_of(i * count, count)
            normed, swished, dshift = piece(r + NEAR, count)
            swished_ref[pl.ds(r, count), lanes_of(c)] = swished.astype(BF16)
            by_gain, by_bias = carry
            by_gain = by_gain + jnp.sum((dshift * normed).reshape(count // 8, 8, LANES), axis=0)
            by_bias = by_bias + jnp.sum(dshift.reshape(count // 8, 8, LANES), axis=0)
            return by_gain, by_bias

        zero = jnp.zeros((8, LANES), F32)
        by_gain, by_bias = lax.fori_loop(0, rows // count, chunk, (zero, zero))
        piece(0, NEAR)
        piece(rows + NEAR, NEAR)
        by_gain = jnp.sum(by_gain, axis=0, keepdims=True)
        by_bias = jnp.sum(by_bias, axis=0, keepdims=True)
        spread(terms_ref, c, (by_gain, by_bias))


def swish(span, sums, gain, bias, conv, back):
    groups, full, _ = conv.shape
    devices = sums.shape[0]
    rows = full - 2 * NEAR
    channels = groups * LANES
    vector = pl.BlockSpec((1, BLOCK), lambda j: (0, j))
    tall = pl.BlockSpec((SUB, full, LANES), lambda j: (j, 0, 0))
    return pl.pallas_call(
        swish_kernel,
        grid=(channels // BLOCK,),
        in_specs=[
            pl.BlockSpec(memory_space=pltpu.SMEM),
            pl.BlockSpec((devices, 3, BLOCK), lambda j: (0, 0, j)),
            vector,
            vector,
            tall,
            tall,
        ],
        out_specs=[
            pl.BlockSpec((rows, BLOCK), lambda j: (0, j)),
            tall,
            pl.BlockSpec((devices, 2, BLOCK), lambda j: (0, 0, j)),
        ],
        out_shape=[
            pltpu.HBM((rows, channels), BF16),
            pltpu.HBM((groups, full, LANES), BF16),
            pltpu.HBM((devices, 2, channels), F32),
        ],
        compiler_params=pltpu.CompilerParams(vmem_limit_bytes=VMEM_LIMIT),
        cost_estimate=pl.CostEstimate(
            flops=30 * rows * channels, bytes_accessed=14 * rows * channels, transcendentals=rows * channels
        ),
        name="swish",
    )(span, *in_hbm(sums, gain, bias), *in_vmem(conv), *in_hbm(back))


def grad_kernel(
    span_ref, sums_ref, terms_ref, gain_ref, taps_ref, conv_ref, dshift_ref, first_ref, second_ref, dpre_ref, dconv_ref, ext
):
    rows = first_ref.shape[0]
    taps = taps_ref.shape[0]
    full = rows + 2 * NEAR
    low, high = span_ref[0], span_ref[1]
    span = 400 if full % 400 == 0 else NEAR
    count = 128 if rows % 128 == 0 else NEAR
    shift = NEAR - (taps - 1) // 2
    for c in range(SUB):
        mean, inv_std, total = moments(sums_ref, c)
        at = lanes_of(c)
        outer = gain_ref[:, at] * inv_std
        terms = jnp.sum(terms_ref[:, :, at], axis=0)
        by_gain = terms[0:1] / total
        by_bias = terms[1:2] / total

        @pl.loop(0, full // span)
        def _(i):
            r = pl.multiple_of(i * span, span)
            normed = (conv_ref[c, pl.ds(r, span), :] - mean) * inv_std
            value = outer * (dshift_ref[c, pl.ds(r, span), :].astype(F32) - by_bias - normed * by_gain)
            live = row_mask(r - NEAR, span, low, high)
            ext[c, pl.ds(r, span), :] = jnp.where(live, value, 0.0).astype(BF16).astype(F32)

        dconv_ref[c] = ext[c, NEAR : NEAR + rows, :].astype(BF16)

        @pl.loop(0, rows // count)
        def _(i):
            r = pl.multiple_of(i * count, count)
            tiles = taps_chunk(ext, c, r + shift, count, lambda k: taps_ref[taps - 1 - k : taps - k, at], taps)
            for u in range(0, count // 8, 2):
                dglu = jnp.concatenate(tiles[u : u + 2], axis=0)
                own = pl.ds(r + 8 * u, 16)
                dpre_ref[0, own, at] = (dglu * first_ref[own, at].astype(F32)).astype(BF16)
                dpre_ref[1, own, at] = (dglu * second_ref[own, at].astype(F32)).astype(BF16)


def norm_grad(span, sums, terms, gain, w_dw, conv, dshift, first, second, part, parts):
    groups, full, _ = conv.shape
    devices = sums.shape[0]
    rows = full - 2 * NEAR
    channels = groups * LANES // parts
    taps = w_dw.shape[0]
    blocks = channels // BLOCK
    at = part * blocks
    tall = pl.BlockSpec((SUB, full, LANES), lambda j: (j + at, 0, 0))
    flat = pl.BlockSpec((rows, BLOCK), lambda j: (0, j + at))
    return pl.pallas_call(
        grad_kernel,
        grid=(blocks,),
        in_specs=[
            pl.BlockSpec(memory_space=pltpu.SMEM),
            pl.BlockSpec((devices, 3, BLOCK), lambda j: (0, 0, j + at)),
            pl.BlockSpec((devices, 2, BLOCK), lambda j: (0, 0, j + at)),
            pl.BlockSpec((1, BLOCK), lambda j: (0, j + at)),
            pl.BlockSpec((taps, BLOCK), lambda j: (0, j + at)),
            tall,
            tall,
            flat,
            flat,
        ],
        out_specs=[
            pl.BlockSpec((2, rows, BLOCK), lambda j: (0, 0, j)),
            pl.BlockSpec((SUB, rows, LANES), lambda j: (j, 0, 0)),
        ],
        out_shape=[
            pltpu.HBM((2, rows, channels), BF16),
            pltpu.HBM((channels // LANES, rows, LANES), BF16),
        ],
        scratch_shapes=[pltpu.VMEM((SUB, full, LANES), F32)],
        compiler_params=pltpu.CompilerParams(vmem_limit_bytes=VMEM_LIMIT),
        cost_estimate=pl.CostEstimate(
            flops=70 * rows * channels, bytes_accessed=16 * rows * channels, transcendentals=0
        ),
        name="norm_grad",
    )(span, *in_hbm(sums, terms, gain, w_dw), *in_vmem(conv), *in_hbm(dshift, first, second))


def tap_grad_kernel(taps, edge_ref, glu_ref, *refs):
    *dconv_refs, out_ref, ext, own = refs
    rows = glu_ref.shape[1]
    shift = WIDE - (taps - 1) // 2
    tiles = 16 if rows % 128 == 0 else 2
    per = pl.num_programs(0) // len(dconv_refs)
    for part, dconv_ref in enumerate(dconv_refs):

        @pl.when(pl.program_id(0) // per == part)
        def _(dconv_ref=dconv_ref):
            for c in range(SUB):
                own[c] = dconv_ref[c].astype(F32)

    for c in range(SUB):
        ext[c, 0:WIDE, :] = edge_ref[c, 0:WIDE, :].astype(F32)
        ext[c, WIDE : WIDE + rows, :] = glu_ref[c].astype(F32)
        ext[c, WIDE + rows :, :] = edge_ref[c, WIDE:, :].astype(F32)
    for c in range(SUB):

        def chunk(i, carry):
            sums = list(carry)
            r = pl.multiple_of(i * 8 * tiles, 8 * tiles)
            grads = [own[c, pl.ds(r + 8 * m, 8), :] for m in range(tiles)]
            for offset in range(taps + 8 * (tiles - 1)):
                held = None
                for m in range(tiles):
                    k = offset - 8 * m
                    if 0 <= k < taps:
                        if held is None:
                            held = ext[c, pl.ds(r + shift + offset, 8), :]
                        sums[k] = sums[k] + held * grads[m]
            return tuple(sums)

        zero = jnp.zeros((8, LANES), F32)
        sums = lax.fori_loop(0, rows // (8 * tiles), chunk, (zero,) * taps)
        out_ref[c] = jnp.zeros(out_ref.shape[1:], F32)
        for k in range(taps):
            out_ref[c, k : k + 1, :] = jnp.sum(sums[k], axis=0, keepdims=True)


def tap_grad(edge, glu, dconv_parts, taps):
    groups, rows, _ = glu.shape
    steps = groups // SUB
    per = steps // len(dconv_parts)
    padded = -(-taps // 8) * 8
    specs = [
        pl.BlockSpec((SUB, rows, LANES), lambda j, part=part: (jnp.clip(j - part * per, 0, per - 1), 0, 0))
        for part in range(len(dconv_parts))
    ]
    return pl.pallas_call(
        functools.partial(tap_grad_kernel, taps),
        grid=(steps,),
        in_specs=[
            pl.BlockSpec((SUB, 2 * WIDE, LANES), lambda j: (j, 0, 0)),
            pl.BlockSpec((SUB, rows, LANES), lambda j: (j, 0, 0)),
            *specs,
        ],
        out_specs=pl.BlockSpec((SUB, padded, LANES), lambda j: (j, 0, 0)),
        out_shape=jax.ShapeDtypeStruct((groups, padded, LANES), F32),
        scratch_shapes=[
            pltpu.VMEM((SUB, rows + 2 * WIDE, LANES), F32),
            pltpu.VMEM((SUB, rows, LANES), F32),
        ],
        compiler_params=pltpu.CompilerParams(vmem_limit_bytes=VMEM_LIMIT),
        cost_estimate=pl.CostEstimate(
            flops=62 * rows * groups * LANES, bytes_accessed=4 * rows * groups * LANES, transcendentals=0
        ),
        name="tap_grad",
    )(*in_hbm(edge, glu), *in_hbm(*dconv_parts))


def frames_grad_kernel(*refs):
    *dpre_refs, w_ref, out_ref = refs
    width = dpre_refs[0].shape[2]
    channels = width * len(dpre_refs)
    total = 0.0
    for i, dpre_ref in enumerate(dpre_refs):
        for half in range(2):
            at = half * channels + i * width
            total = total + dot_nt(dpre_ref[half], w_ref[:, at : at + width])
    out_ref[...] = total.astype(BF16)


def frames_grad(dpre_parts, w_in):
    _, rows, width = dpre_parts[0].shape
    depth, outputs = w_in.shape
    whole = pl.BlockSpec((2, rows, width), lambda j: (0, 0, 0))
    return pl.pallas_call(
        frames_grad_kernel,
        grid=(depth // BLOCK,),
        in_specs=[whole] * len(dpre_parts) + [pl.BlockSpec((BLOCK, outputs), lambda j: (j, 0))],
        out_specs=pl.BlockSpec((rows, BLOCK), lambda j: (0, j)),
        out_shape=jax.ShapeDtypeStruct((rows, depth), BF16),
        compiler_params=pltpu.CompilerParams(vmem_limit_bytes=VMEM_LIMIT),
        cost_estimate=pl.CostEstimate(
            flops=2 * rows * depth * outputs, bytes_accessed=10 * rows * depth, transcendentals=0
        ),
        name="frames_grad",
    )(*in_hbm(*dpre_parts, w_in))


def flip_kernel(owner_rows, orders, core_ref, left_ref, mine_ref, other_ref):
    flat = left_ref[...].astype(F32).T
    is_odd = core_ref[0] == 1

    def rows_of(order):
        return jnp.concatenate([flat[p * owner_rows : (p + 1) * owner_rows] for p in order], axis=0).astype(BF16)

    even, odd = rows_of(orders[0]), rows_of(orders[1])
    mine_ref[...] = jnp.where(is_odd, odd, even)
    other_ref[...] = jnp.where(is_odd, even, odd)


def flipped(core, left, plan):
    rows, depth = left.shape
    owner_rows = depth // (2 * len(plan.blocks[0]))
    shape = pltpu.HBM((depth // 2, rows), BF16)
    return pl.pallas_call(
        functools.partial(flip_kernel, owner_rows, plan.blocks),
        in_specs=[pl.BlockSpec(memory_space=pltpu.SMEM), pl.BlockSpec(memory_space=pltpu.VMEM)],
        out_specs=[pl.BlockSpec(memory_space=pltpu.VMEM)] * 2,
        out_shape=[shape, shape],
        compiler_params=pltpu.CompilerParams(vmem_limit_bytes=VMEM_LIMIT),
        cost_estimate=pl.CostEstimate(flops=4 * rows * depth, bytes_accessed=4 * rows * depth, transcendentals=0),
        name="flipped",
    )(core, *in_hbm(left))


def pair_kernel(half_ref, left_own, left_got, own_ref, got_ref, send_ref, keep_ref):
    rows = send_ref.shape[0]
    term = dot_nn(left_own[...], own_ref[0]) + dot_nn(left_got[...], got_ref[0])
    low, high = term[:rows], term[rows:]
    upper = half_ref[0] == 1
    send_ref[...] = jnp.where(upper, low, high).astype(BF16)
    keep_ref[...] = jnp.where(upper, high, low).astype(BF16)


def pair_term(half, left_own, left_got, right_own, right_got):
    halves, rows, width = right_own.shape
    depth = left_own.shape[0]
    left = pl.BlockSpec((depth, rows), lambda j: (0, 0))
    right = pl.BlockSpec((1, rows, width), lambda j: (j, 0, 0))
    out = pl.BlockSpec((depth // 2, width), lambda j: (0, j))
    shape = jax.ShapeDtypeStruct((depth // 2, halves * width), BF16)
    return pl.pallas_call(
        pair_kernel,
        grid=(halves,),
        in_specs=[pl.BlockSpec(memory_space=pltpu.SMEM), left, left, right, right],
        out_specs=[out, out],
        out_shape=[shape, shape],
        compiler_params=pltpu.CompilerParams(vmem_limit_bytes=VMEM_LIMIT),
        cost_estimate=pl.CostEstimate(
            flops=4 * halves * rows * depth * width, bytes_accessed=8 * halves * rows * width, transcendentals=0
        ),
        name="pair_term",
    )(half.reshape(1), *in_hbm(left_own, left_got, right_own, right_got))


def weight_kernel(owner_rows, orders, core_ref, left_ref, right_ref, send_ref, keep_ref):
    term = dot_tn(left_ref[...], right_ref[0])
    is_odd = core_ref[0] == 1
    send, keep = [], []
    for p, (even, odd) in enumerate(zip(*orders)):
        even = term[even * owner_rows : (even + 1) * owner_rows]
        odd = term[odd * owner_rows : (odd + 1) * owner_rows]
        send.append(jnp.where(is_odd, even, odd))
        keep.append(jnp.where(is_odd, odd, even))
    send_ref[...] = jnp.concatenate(send, axis=0).astype(BF16)
    keep_ref[...] = jnp.concatenate(keep, axis=0).astype(BF16)


def weight_term(core, left, right, plan):
    halves, rows, width = right.shape
    depth = left.shape[1]
    step = 512
    per = width // step
    out = pl.BlockSpec((depth // 2, step), lambda j: (0, j))
    shape = jax.ShapeDtypeStruct((depth // 2, halves * width), BF16)
    owner_rows = depth // (2 * len(plan.blocks[0]))
    return pl.pallas_call(
        functools.partial(weight_kernel, owner_rows, plan.blocks),
        grid=(halves * per,),
        in_specs=[
            pl.BlockSpec(memory_space=pltpu.SMEM),
            pl.BlockSpec((rows, depth), lambda j: (0, 0)),
            pl.BlockSpec((1, rows, step), lambda j: (j // per, 0, j % per)),
        ],
        out_specs=[out, out],
        out_shape=[shape, shape],
        compiler_params=pltpu.CompilerParams(vmem_limit_bytes=VMEM_LIMIT),
        name="weight_term",
    )(core, *in_hbm(left, right))


class Halving:
    def __init__(self, dp_count, tm_count):
        near = [1 << i for i in range(1, (tm_count - 1).bit_length())]
        far = [tm_count << i for i in range((dp_count - 1).bit_length())]
        self.count = dp_count * tm_count
        self.masks = (near + far, far[: len(near)] + near + far[len(near) :])
        self.blocks = tuple(
            [self.block(core, masks, p) for p in range(self.count // 2)] for core, masks in enumerate(self.masks)
        )

    def block(self, core, masks, p):
        return core + sum(mask for i, mask in enumerate(masks) if p >> (len(masks) - 1 - i) & 1)

    def perm(self, step):
        if step < 0:
            return [(i, i ^ 1) for i in range(self.count)]
        return [(i, i ^ self.masks[i & 1][step]) for i in range(self.count)]

    def own_half(self, step, place):
        mask = jnp.where(place & 1 == 1, self.masks[1][step], self.masks[0][step])
        return ((place & mask) != 0).astype(jnp.int32)


def combine_kernel(half_ref, keep_other, got_other, keep_mine, got_mine, send_ref, keep_ref):
    send_ref[...] = (keep_other[...].astype(F32) + got_other[...].astype(F32)).astype(BF16)
    keep_ref[...] = (keep_mine[...].astype(F32) + got_mine[...].astype(F32)).astype(BF16)


def combine(half, keep, got):
    rows, width = keep.shape
    step = 512
    other = pl.BlockSpec((rows // 2, step), lambda j, half: (1 - half[0], j))
    mine = pl.BlockSpec((rows // 2, step), lambda j, half: (half[0], j))
    out = pl.BlockSpec((rows // 2, step), lambda j, half: (0, j))
    shape = jax.ShapeDtypeStruct((rows // 2, width), BF16)
    return pl.pallas_call(
        combine_kernel,
        grid_spec=pltpu.PrefetchScalarGridSpec(
            num_scalar_prefetch=1,
            grid=(width // step,),
            in_specs=[other, other, mine, mine],
            out_specs=[out, out],
        ),
        out_shape=[shape, shape],
        compiler_params=pltpu.CompilerParams(vmem_limit_bytes=VMEM_LIMIT),
        name="combine",
    )(half.reshape(1), *in_hbm(keep, got, keep, got))


class Scatter:
    def __init__(self, plan, place, parts):
        self.plan, self.place, self.step = plan, place, 0
        self.keep = [keep for _, keep in parts]
        self.got = [self.swap(send) for send, _ in parts]

    def swap(self, send):
        return lax.ppermute(send, ("dp", "tm"), self.plan.perm(self.step))

    def sums(self):
        parts = [keep.astype(F32) + got.astype(F32) for keep, got in zip(self.keep, self.got)]
        return parts[0] if len(parts) == 1 else jnp.concatenate(parts, axis=1)

    def ready(self):
        self.step += 1
        half = self.plan.own_half(self.step, self.place)
        both = self.sums()
        rows = both.shape[0] // 2
        low, high = both[:rows].astype(BF16), both[rows:].astype(BF16)
        self.keep = [jnp.where(half == 1, high, low)]
        return jnp.where(half == 1, low, high)

    def go(self, send):
        self.got = [self.swap(send)]

    def done(self):
        while self.step + 1 < len(self.plan.masks[0]):
            self.go(self.ready())
        return self.sums()


def from_all(copies):
    return lax.all_to_all(copies, ("dp", "tm"), 0, 0, tiled=True)


def shared(owned):
    count = lax.axis_size("dp") * lax.axis_size("tm")
    return from_all(jnp.broadcast_to(owned[None], (count,) + owned.shape))


def local(frames, lengths, w_in, w_dw, bn_gain, bn_bias, w_out, cotangent):
    feats, cot = frames[0], cotangent[0]
    rows, depth = feats.shape
    taps = w_dw.shape[0]
    tm_count = lax.axis_size("tm")
    device_count = lax.axis_size("dp") * tm_count
    plan = Halving(lax.axis_size("dp"), tm_count)
    place = lax.axis_index(("dp", "tm"))
    offset = lax.axis_index("tm") * rows
    span = jnp.stack([-offset, lengths[0] - offset]).astype(jnp.int32)
    core = (place & 1).astype(jnp.int32).reshape(1)
    gain, bias = bn_gain[None], bn_bias[None]

    everyone = ("dp", "tm")
    tail, head = edges(feats, cot)
    before = lax.ppermute(tail, "tm", [(i, i + 1) for i in range(tm_count - 1)])
    after = lax.ppermute(head, "tm", [(i + 1, i) for i in range(tm_count - 1)])

    glu, first, second = gated(span, feats, w_in)
    conv, edge, sums = convolved(span, before, after, w_in, w_dw, glu, device_count)
    sums = from_all(sums)
    back = back_projected(before, cot, after, w_out)
    left_own, left_other = flipped(core, feats, plan)
    sums, left_other = lax.optimization_barrier((sums, left_other))
    left_got = lax.ppermute(left_other, everyone, plan.perm(-1))

    first_half = plan.own_half(0, place)
    swished, dshift, terms = swish(span, sums, gain, bias, conv, back)
    terms = from_all(terms)
    out_send, out_keep = weight_term(core, swished, cotangent, plan)
    out_got = lax.ppermute(out_send, everyone, plan.perm(-1))
    out_rows = dot_nn(swished, w_out).astype(BF16)
    out_send, out_keep = combine(first_half, out_keep, out_got)
    terms, out_rows, out_send, left_got = lax.optimization_barrier((terms, out_rows, out_send, left_got))
    out_scatter = Scatter(plan, place, [(out_send, out_keep)])

    parts = 2
    dpre_own, dpre_got, dconv = [], [], []
    for part in range(parts):
        own, grads = norm_grad(span, sums, terms, gain, w_dw, conv, dshift, first, second, part, parts)
        dpre_own.append(own)
        dconv.append(grads)
        dpre_got.append(lax.ppermute(own, everyone, plan.perm(-1)))
        if part == 0:
            send = out_scatter.ready()
            dshift, send = lax.optimization_barrier((dshift, send))
            out_scatter.go(send)
    in_parts = [pair_term(first_half, left_own, left_got, own, got) for own, got in zip(dpre_own, dpre_got)]
    in_scatter = Scatter(plan, place, in_parts)
    send = out_scatter.ready()
    glu, send, _ = lax.optimization_barrier((glu, send, [send for send, _ in in_parts]))
    out_scatter.go(send)
    tap_sums = tap_grad(edge, glu, dconv, taps)
    tap_sums, in_scatter.got, out_scatter.got = lax.optimization_barrier(
        (tap_sums, in_scatter.got, out_scatter.got)
    )
    out_send, in_send = out_scatter.ready(), in_scatter.ready()
    in_send, tap_sums = lax.optimization_barrier((in_send, tap_sums))
    in_scatter.go(in_send)
    out_scatter.go(out_send)
    owned = from_all(tap_sums.reshape(device_count, -1, LANES))
    in_scatter.go(in_scatter.ready())
    in_scatter.got, out_scatter.got, owned = lax.optimization_barrier((in_scatter.got, out_scatter.got, owned))
    kernel_sum = shared(jnp.sum(owned, axis=0)).reshape(tap_sums.shape).transpose(1, 0, 2).reshape(-1, depth)[:taps]
    in_send, *dpre_own = lax.optimization_barrier((in_scatter.ready(), *dpre_own))
    in_scatter.go(in_send)
    grad_rows = frames_grad(dpre_own, w_in)
    grad_w_out = out_scatter.done()
    grad_w_in = in_scatter.done()
    grad_w_in = grad_w_in.reshape(-1, parts, 2, depth // parts).swapaxes(1, 2).reshape(-1, 2 * depth)
    by_gain, by_bias = jnp.sum(terms, axis=0)
    scale = 1.0 / math.sqrt(device_count * rows)
    return (
        out_rows[None],
        grad_rows[None],
        grad_w_in * scale,
        grad_w_out * scale,
        kernel_sum * scale,
        by_gain * scale,
        by_bias * scale,
    )


def solution(mesh):
    placed = (P("dp", "tm", None), P("dp"), P(), P(), P(), P(), P(), P("dp", "tm", None))
    return jax.shard_map(
        local,
        mesh=mesh,
        in_specs=placed,
        out_specs=(
            P("dp", "tm", None),
            P("dp", "tm", None),
            P(("dp", "tm"), None),
            P(("dp", "tm"), None),
            P(),
            P(),
            P(),
        ),
        check_vma=False,
    )
```
